32 devices in a mesh: seq: 4 (over z), head: 8 (over y, x, core).
Axes of the slice: x: 2, y: 2, z: 4, core: 2. Of those that a mesh axis runs over, the one named last changes fastest.
Arguments:
- x_in: bfloat16 [4096, 16384], P('seq', 'head'), may hold values from -40 to 40
- z_gate: bfloat16 [4096, 16384], P('seq', 'head'), may hold values from -6 to 6
- b_input: bfloat16 [4096, 8, 128], P('seq'), may hold values from -2 to 2
- c_input: bfloat16 [4096, 8, 128], P('seq'), may hold values from -2 to 2
- dt_raw: float32 [128, 4096], P('head', 'seq'), may hold values from -5 to 1366
- a_log: float32 [128], P('head'), may hold values from -20 to 0
- d_skip: float32 [128], P('head'), may hold values from 0.5 to 2
- norm_gain: float32 [16384], P('head'), may hold values from 0.25 to 1.75
- doc_lengths: int32 [6], replicated, may hold values from 1 to 1365, 4096 in all
- doc_lang: int32 [6], replicated, may hold values from 0 to 3
- adapt_down: bfloat16 [4, 16384, 128], P(None, 'head'), may hold values from -0.046875 to 0.046875
- adapt_up: bfloat16 [4, 128, 16384], P(None, None, 'head'), may hold values from -0.5 to 0.5
Outputs:
- adapted: bfloat16 [4096, 16384], P('seq', 'head')
The draws below stay inside these ranges and needn't reach their ends.
Inputs may be any that keep to these rules, and one draw needn't show every extreme that they name: `doc_lengths`: the lengths sum to 4096; the longest document has exactly 1365 tokens.
All inputs are finite; a program needn't handle non-finite values.
Results may differ from the reference program's by a relative error of at most 0.0075.
Values may be sent and summed in bfloat16 or wider, within the bound.
No kernel may reach another device: no remote copies, remote signals or barrier semaphores. Data moves between devices by JAX's collectives and lax.ppermute only.
A program may use at most 128 MiB of HBM per device.

```python
import math
import jax
import jax.numpy as jnp
import numpy as np
from jax import lax

SPACE_HEADS = 128
HEAD_DIM = 128
STATE = 128
GROUPS = 8
RANK = 128
NLANG = 4
NDOC = 6
STREAM_TOKENS = 4096
D_INNER = 16384
MOST_LEN = 1365


def decay_layout(key):
    base_key = jax.random.fold_in(key, 7)
    key_kind, key_fast, key_slow, random_key_locations, random_key_penalty, random_key_jitter = jax.random.split(base_key, 6)
    slow_share = 0.5
    slow_heads = jax.random.uniform(key_kind, (SPACE_HEADS,)) < slow_share
    fast_span = jnp.exp(jax.random.uniform(key_fast, (SPACE_HEADS,), minval=jnp.log(30.0), maxval=jnp.log(50.0)))
    fast_rate = 1.0 / (0.2 * fast_span)
    slow_rate = jnp.exp(jax.random.uniform(key_slow, (SPACE_HEADS,), minval=jnp.log(0.3), maxval=jnp.log(0.8))) / (0.2 * STREAM_TOKENS)
    spike_amplitude = jnp.where(slow_heads, slow_rate, fast_rate)
    spike_locations = jax.random.randint(random_key_locations, (2,), 0, STREAM_TOKENS)
    spike_penalty = jax.random.uniform(random_key_penalty, (SPACE_HEADS, 2), minval=0.22, maxval=0.5)
    return (spike_amplitude, spike_locations, spike_penalty, random_key_jitter)


def dt_table(key):
    spike_amplitude, spike_locations, spike_penalty, random_key_jitter = decay_layout(key)
    noise = jnp.clip(jax.random.normal(random_key_jitter, (SPACE_HEADS, STREAM_TOKENS), jnp.float32), -2.5, 2.5)
    starting_values = -2.0 + noise
    token_positions = jnp.arange(STREAM_TOKENS)
    match_count = token_positions[None, :, None] == spike_locations[None, None, :]
    expected_output = jnp.sum(jnp.where(match_count, (spike_penalty / spike_amplitude[:, None])[:, None, :], 0.0), axis=2)
    spike_flags = jnp.any(match_count, axis=2)
    return jnp.where(spike_flags, expected_output, starting_values)


def draw_dt_raw(key, part):
    return dt_table(key).astype(jnp.float32)


def draw_a_log(key, part):
    spike_amplitude, spike_locations, spike_penalty, random_key_jitter = decay_layout(key)
    return jnp.log(spike_amplitude).astype(jnp.float32)


def draw_x_in(key, part):
    step_dt = jax.nn.softplus(dt_table(key))
    key_values = jax.random.fold_in(key, 19)
    values = jnp.clip(jax.random.normal(key_values, (STREAM_TOKENS, SPACE_HEADS, HEAD_DIM), jnp.float32), -4.0, 4.0)
    rising = 3.0 ** (jnp.arange(SPACE_HEADS, dtype=jnp.float32) / max(SPACE_HEADS - 1, 1))
    scaling = rising[None, :] * jnp.minimum(1.0, 1.0 / step_dt).T
    return (values * scaling[:, :, None]).reshape(STREAM_TOKENS, D_INNER).astype(jnp.bfloat16)


def plant(array, own_key, low, largest):
    extent = array.shape
    spot = [jax.random.randint(jax.random.fold_in(own_key, axis), (), 0, extent[axis]) for axis in range(len(extent))]
    array = array.at[tuple(spot)].set(low)
    longest = extent.index(max(extent))
    spot[longest] = (spot[longest] + 1) % extent[longest]
    return array.at[tuple(spot)].set(largest)


def block_scale(stream_key, dims, shards, low, high):
    def one(position, parts):
        heights = jax.random.uniform(jax.random.fold_in(jax.random.fold_in(stream_key, 6), position), (parts,), jnp.float32, low / len(shards), high / len(shards))
        return jnp.repeat(jnp.exp(heights), dims[position] // parts).reshape((-1,) + (1,) * (len(dims) - position - 1))

    loudness = one(*shards[0])
    for cut in shards[1:]:
        loudness = loudness * one(*cut)
    return loudness


def length_profile(amount, total, most, lean):
    portions = [(1 << 20) // math.isqrt(standing ** lean) + 1 for standing in range(2, amount + 1)]
    surplus, given = total - most - (amount - 1), [1] * (amount - 1)
    while surplus > 0:
        candidates = [i for i in range(amount - 1) if given[i] < most]
        whole, remaining = sum([portions[i] for i in candidates]), surplus
        for i in candidates:
            more = min(most - given[i], max(1, remaining * portions[i] // whole), surplus)
            given[i] = given[i] + more
            surplus = surplus - more
    return np.array([most] + given)


def uneven(own_key, amount, total, limit, slope):
    if amount == 2:
        one = jax.random.randint(own_key, (), max(1, total - limit), min(limit, total - 1) + 1)
        return jnp.stack([one, total - one])
    lengths = jnp.asarray(length_profile(amount, total, limit, slope), jnp.int32)
    twos = (amount - 1) // 2
    source_of, sink = lengths[1:1 + 2 * twos:2], lengths[2:2 + 2 * twos:2]
    slack = jnp.minimum(source_of - 1, limit - sink)
    passed = jax.random.randint(jax.random.fold_in(own_key, 1), (twos,), 0, 1 << 20) % (slack + 1)
    lengths = lengths.at[1:1 + 2 * twos:2].set(source_of - passed).at[2:2 + 2 * twos:2].set(sink + passed)
    return lengths[jax.random.permutation(jax.random.fold_in(own_key, 2), amount)]


def centred(rng, dims, width, reach, cuts=(), kind=jnp.bfloat16):
    drawn = jax.random.normal(rng, dims, jnp.float32) * width
    if len(cuts) > 0:
        drawn = block_scale(rng, dims, cuts, -0.22, 0.18) * drawn
    return jnp.clip(drawn, min=-reach, max=reach).astype(kind)


def setup_inputs(seed: int = 0) -> dict:
    arg_keys = jax.random.split(jax.random.key(seed), 13)
    x_in = draw_x_in(jax.random.fold_in(arg_keys[12], 71), 0)
    z_gate = centred(arg_keys[1], (STREAM_TOKENS, D_INNER), 1.0, 6.0, ((0, 4), (1, 8)))
    b_input = centred(arg_keys[2], (STREAM_TOKENS, GROUPS, STATE), 0.3, 2.0, ((0, 4),))
    c_input = centred(arg_keys[3], (STREAM_TOKENS, GROUPS, STATE), 0.3, 2.0, ((0, 4),))
    dt_raw = draw_dt_raw(jax.random.fold_in(arg_keys[12], 71), 0)
    a_log = draw_a_log(jax.random.fold_in(arg_keys[12], 71), 0)
    d_skip = jnp.clip(0.5 + 1.5 * jax.random.uniform(arg_keys[6], (SPACE_HEADS,), jnp.float32) ** block_scale(arg_keys[6], (SPACE_HEADS,), ((0, 8),), -0.2, 0.2), 0.5, 2.0)
    norm_gain = jnp.clip(1.0 + 0.15 * jax.random.normal(arg_keys[7], (D_INNER,), jnp.float32), 0.25, 1.75)
    doc_lengths = uneven(arg_keys[8], NDOC, STREAM_TOKENS, MOST_LEN, 2).astype(jnp.int32)
    doc_lang = plant(jax.random.randint(arg_keys[9], (NDOC,), 0, NLANG), jax.random.fold_in(arg_keys[9], 1), 0, NLANG - 1).astype(jnp.int32)
    adapt_down = centred(arg_keys[10], (NLANG, D_INNER, RANK), D_INNER ** -0.5, 0.046875, ((1, 8),))
    adapt_up = centred(arg_keys[11], (NLANG, RANK, D_INNER), RANK ** -0.5, 0.5, ((2, 8),))
    return dict(x_in=x_in, z_gate=z_gate, b_input=b_input, c_input=c_input, dt_raw=dt_raw, a_log=a_log, d_skip=d_skip, norm_gain=norm_gain, doc_lengths=doc_lengths, doc_lang=doc_lang, adapt_down=adapt_down, adapt_up=adapt_up)


highest = lax.Precision.HIGHEST

def doc_tables(doc_lengths, doc_lang, token_positions, lang_count):
    doc_ends = jnp.cumsum(doc_lengths).astype(jnp.int32)
    doc_start = (doc_ends - doc_lengths).astype(jnp.int32)
    doc_index = lax.optimization_barrier(jnp.sum((token_positions[:, None] >= doc_start[None, :]).astype(jnp.int32), axis=1)).astype(jnp.int32) - 1
    is_first = lax.optimization_barrier(jnp.sum((token_positions[:, None] == doc_start[None, :]).astype(jnp.int32), axis=1)).astype(jnp.int32)
    doc_hot = (doc_index[:, None] == jnp.arange(doc_lengths.shape[0], dtype=jnp.int32)[None, :]).astype(jnp.int32)
    lang_index = lax.optimization_barrier(jnp.sum(doc_hot * doc_lang[None, :], axis=1)).astype(jnp.int32)
    lang_hot = lang_index[:, None] == jnp.arange(lang_count, dtype=jnp.int32)[None, :]
    return (doc_index, is_first, lang_hot)

def block_scan(x_vals, step_dt, log_decay, b_vals, c_vals, doc_index, is_first):
    head_count, length, head_width = x_vals.shape
    states = b_vals.shape[1]
    block_len = min(128, length)
    block_count = length // block_len
    x_blocks = x_vals.reshape(head_count, block_count, block_len, head_width).transpose(1, 0, 2, 3)
    dt_blocks = step_dt.reshape(head_count, block_count, block_len).transpose(1, 0, 2)
    dec_blocks = log_decay.reshape(head_count, block_count, block_len).transpose(1, 0, 2)
    b_blocks = b_vals.reshape(block_count, block_len, states)
    c_blocks = c_vals.reshape(block_count, block_len, states)
    doc_blocks = doc_index.reshape(block_count, block_len)
    first_blocks = is_first.reshape(block_count, block_len)
    lower_mask = jnp.arange(block_len)[:, None] >= jnp.arange(block_len)[None, :]

    def advance(carry_state, pieces):
        x_block, dt_block, dec_block, b_block, c_block, doc_block, first_block = pieces
        cumulative = jnp.cumsum(dec_block, axis=1)
        keep_mask = lower_mask & (doc_block[:, None] == doc_block[None, :])
        decay_gaps = jnp.where(keep_mask[None], cumulative[:, :, None] - cumulative[:, None, :], 0.0)
        scores = jnp.dot(c_block, b_block.T, preferred_element_type=jnp.float32)
        weights = jnp.where(keep_mask[None], jnp.exp(decay_gaps), 0.0) * scores[None] * dt_block[:, None, :]
        x_float = x_block.astype(jnp.float32)
        inner_part = jnp.einsum('hij,hjp->hip', weights, x_float, precision=highest)
        reach_mask = (jnp.cumsum(first_block) == 0).astype(jnp.float32)
        carried = jnp.einsum('in,hnp->hip', c_block.astype(jnp.float32), carry_state, precision=highest)
        carried = carried * (jnp.exp(cumulative) * reach_mask[None])[:, :, None]
        tail_keep = doc_block == doc_block[-1]
        tail_gaps = jnp.where(tail_keep[None], cumulative[:, -1:] - cumulative, 0.0)
        fresh_weight = jnp.where(tail_keep[None], jnp.exp(tail_gaps), 0.0) * dt_block
        written = jnp.einsum('jn,hjp->hnp', b_block.astype(jnp.float32), x_float * fresh_weight[:, :, None], precision=highest)
        kept_share = jnp.exp(cumulative[:, -1]) * reach_mask[-1]
        return (carry_state * kept_share[:, None, None] + written, inner_part + carried)
    initial = jnp.zeros((head_count, states, head_width), jnp.float32)
    final_state, outputs = lax.scan(advance, initial, (x_blocks, dt_blocks, dec_blocks, b_blocks, c_blocks, doc_blocks, first_blocks))
    outputs = outputs.transpose(1, 0, 2, 3).reshape(head_count, length, head_width)
    return (outputs, final_state)

def reference(x_in, z_gate, b_input, c_input, dt_raw, a_log, d_skip, norm_gain, doc_lengths, doc_lang, adapt_down, adapt_up):
    token_positions = jnp.arange(STREAM_TOKENS, dtype=jnp.int32)
    doc_index, is_first, lang_hot = doc_tables(doc_lengths, doc_lang, token_positions, NLANG)
    step_dt = jax.nn.softplus(dt_raw)
    log_decay = step_dt * (-jnp.exp(a_log))[:, None]
    per_group = SPACE_HEADS // GROUPS
    x_heads = x_in.reshape(STREAM_TOKENS, GROUPS, per_group, HEAD_DIM).transpose(1, 2, 0, 3)
    dt_groups = step_dt.reshape(GROUPS, per_group, STREAM_TOKENS)
    dec_groups = log_decay.reshape(GROUPS, per_group, STREAM_TOKENS)
    b_groups = b_input.transpose(1, 0, 2)
    c_groups = c_input.transpose(1, 0, 2)

    def one_group(pieces):
        x_group, dt_group, dec_group, b_group, c_group = pieces
        outputs, final_state = block_scan(x_group, dt_group, dec_group, b_group, c_group, doc_index, is_first)
        return outputs
    ssd_heads = lax.map(one_group, (x_heads, dt_groups, dec_groups, b_groups, c_groups))
    ssd_rows = ssd_heads.transpose(2, 0, 1, 3).reshape(STREAM_TOKENS, D_INNER)
    skip_rows = jnp.repeat(d_skip, HEAD_DIM)
    ssd_rows = ssd_rows + skip_rows[None, :] * x_in.astype(jnp.float32)
    gated = ssd_rows * jax.nn.silu(z_gate.astype(jnp.float32))
    mean_square = lax.optimization_barrier(jnp.sum(gated * gated, axis=1)) / D_INNER
    normed = (gated * lax.rsqrt(mean_square + 1e-05)[:, None] * norm_gain[None, :]).astype(jnp.bfloat16)
    low_sum = jnp.zeros((STREAM_TOKENS, RANK), jnp.float32)
    for language in range(NLANG):
        product = jnp.dot(normed, adapt_down[language], preferred_element_type=jnp.float32)
        low_sum = low_sum + jnp.where(lang_hot[:, language:language + 1], product, 0.0)
    low_rank = low_sum.astype(jnp.bfloat16)
    selected = jnp.where(lang_hot[:, :, None], low_rank[:, None, :], jnp.zeros((), jnp.bfloat16)).reshape(STREAM_TOKENS, NLANG * RANK)
    lifted = jnp.dot(selected, adapt_up.reshape(NLANG * RANK, D_INNER), preferred_element_type=jnp.float32)
    return (normed.astype(jnp.float32) + lifted).astype(jnp.bfloat16)
```

```python
import functools

import jax
import jax.numpy as jnp
from jax import lax
from jax.experimental import pallas as pl
from jax.experimental.pallas import tpu as pltpu
from jax.sharding import PartitionSpec as P

F32 = jnp.float32
BF16 = jnp.bfloat16
I32 = jnp.int32
LOG2E = 1.4426950408889634
EPS = 1e-05
LANES = 128
SUM_ROWS = 16
LONGEST_SHARE = 3
VMEM_LIMIT = 48 * 1024 * 1024


def params():
    return pltpu.CompilerParams(vmem_limit_bytes=VMEM_LIMIT)


def starts_of(len_ref):
    starts, at = [], jnp.int32(0)
    for d in range(len_ref.shape[0]):
        starts.append(at)
        at = at + len_ref[d]
    return starts


def doc_at(pos, starts):
    found = jnp.where(pos >= starts[0], 0, -1)
    for s in starts[1:]:
        found = found + jnp.where(pos >= s, 1, 0)
    return found


def lang_at(pos, starts, lang_ref):
    found = jnp.where(pos >= 0, lang_ref[0], 0)
    for d in range(1, len(starts)):
        found = jnp.where(pos >= starts[d], lang_ref[d], found)
    return found


def rates(alog_ref, rows):
    which = lax.broadcasted_iota(I32, (rows, LANES), 0)
    column = jnp.zeros((rows, LANES), F32)
    for h in range(rows):
        column = jnp.where(which == h, alog_ref[h], column)
    return -LOG2E * jnp.exp(column)


def softplus(v):
    return jnp.maximum(v, 0.0) + jnp.log(1.0 + jnp.exp(-jnp.abs(v)))


def running(v, back):
    width = v.shape[1]
    lane = lax.broadcasted_iota(I32, v.shape, 1)
    step = 1
    while step < width:
        if back:
            v = v + jnp.where(lane + step < width, pltpu.roll(v, width - step, 1), 0.0)
        else:
            v = v + jnp.where(lane >= step, pltpu.roll(v, step, 1), 0.0)
        step *= 2
    return v


def pick_matrix(group, groups):
    shape = (LANES, LANES * groups)
    row = lax.broadcasted_iota(I32, shape, 0)
    col = lax.broadcasted_iota(I32, shape, 1)
    return jnp.where(col == row * groups + group, 1.0, 0.0).astype(BF16)


def dot(a, b):
    return jnp.dot(a, b, preferred_element_type=F32)


def state_kernel(heads_per, meta, len_ref, alog_ref, dt_ref, b_ref, x_ref, state_ref, thr_ref, bsel_ref, bt_ref, w_ref, all_ref):
    step = pl.program_id(0)
    heads, tokens = dt_ref.shape
    groups = b_ref.shape[0] // tokens

    @pl.when(step == 0)
    def _():
        pick = pick_matrix(meta[1], groups)
        for c in range(tokens // LANES):
            here = slice(c * LANES, (c + 1) * LANES)
            chosen = dot(pick, b_ref[c * LANES * groups:(c + 1) * LANES * groups, :])
            bsel_ref[here, :] = chosen.astype(BF16)
            bt_ref[:, here] = chosen.T
        starts = starts_of(len_ref)
        base = meta[0]
        rate = rates(alog_ref, heads)
        parts, totals = [], []
        for c in range(tokens // LANES):
            step_dt = softplus(dt_ref[:, c * LANES:(c + 1) * LANES])
            decay = step_dt * rate
            after = running(decay, True)
            parts.append((step_dt, after - decay))
            totals.append(after[:, 0:1])
        last_doc = doc_at(base + tokens - 1, starts)
        first_doc = doc_at(base - 1, starts)
        later = jnp.zeros((heads, 1), F32)
        for c in reversed(range(tokens // LANES)):
            step_dt, inside = parts[c]
            pos = base + c * LANES + lax.broadcasted_iota(I32, (heads, LANES), 1)
            alive = doc_at(pos, starts) == last_doc
            w_ref[:, c * LANES:(c + 1) * LANES] = jnp.where(alive, jnp.exp2(inside + later) * step_dt, 0.0)
            later = later + totals[c]
        kept = jnp.where(last_doc == first_doc, 1.0, 0.0)
        all_ref[...] = jnp.broadcast_to(jnp.exp2(later) * kept, all_ref.shape)

    for i in range(heads_per):
        h = step * heads_per + i
        here = slice(i * LANES, (i + 1) * LANES)
        weighted = (bt_ref[...] * w_ref[pl.ds(h, 1), :]).astype(BF16)
        state_ref[:, here] = dot(weighted, x_ref[:, here]).astype(BF16)
        thr_ref[:, here] = jnp.broadcast_to(all_ref[pl.ds(h, 1), :], (8, LANES))


def block_states(meta, doc_lengths, a_log, dt_raw, b_rows, x_in):
    heads, tokens = dt_raw.shape
    features = x_in.shape[1]
    width = features // heads
    per = min(4, heads)
    return pl.pallas_call(
        functools.partial(state_kernel, per),
        grid_spec=pltpu.PrefetchScalarGridSpec(
            num_scalar_prefetch=3,
            grid=(heads // per,),
            in_specs=[
                pl.BlockSpec((heads, tokens), lambda s, *_: (0, 0)),
                pl.BlockSpec(b_rows.shape, lambda s, *_: (0, 0)),
                pl.BlockSpec((tokens, per * width), lambda s, *_: (0, s)),
            ],
            out_specs=[
                pl.BlockSpec((LANES, per * width), lambda s, *_: (0, s)),
                pl.BlockSpec((8, per * width), lambda s, *_: (0, s)),
                pl.BlockSpec((tokens, LANES), lambda s, *_: (0, 0)),
            ],
            scratch_shapes=[
                pltpu.VMEM((LANES, tokens), F32),
                pltpu.VMEM((heads, tokens), F32),
                pltpu.VMEM((heads, LANES), F32),
            ],
        ),
        out_shape=[
            jax.ShapeDtypeStruct((LANES, features), BF16),
            jax.ShapeDtypeStruct((8, features), F32),
            jax.ShapeDtypeStruct((tokens, LANES), BF16),
        ],
        compiler_params=params(),
        name="block_states",
    )(meta, doc_lengths, a_log, dt_raw, b_rows, x_in)


def scan_kernel(meta, len_ref, alog_ref, skip_ref, dt_ref, b_ref, c_ref, x_ref, z_ref,
                part_ref, gate_ref, csel_ref, reach_ref, state_ref, past_ref, stack_ref):
    step = pl.program_id(0)
    heads = dt_ref.shape[0]
    groups = c_ref.shape[0] // LANES
    slot = max(8, heads)
    starts = starts_of(len_ref)
    block = meta[0]
    base = block + step * LANES

    @pl.when(step == 0)
    def _():
        state_ref[...] = jnp.zeros_like(state_ref)
        past_ref[...] = jnp.zeros_like(past_ref)
        stack_ref[...] = jnp.zeros_like(stack_ref)

    step_dt = softplus(dt_ref[...])
    decay = step_dt * rates(alog_ref, heads)
    total_to = running(decay, False)
    chunk_total = jnp.broadcast_to(total_to[:, LANES - 1:LANES], (heads, LANES))
    past = past_ref[...]
    before = total_to - jnp.log(step_dt) * LOG2E

    pos = base + lax.broadcasted_iota(I32, (heads, LANES), 1)
    doc = doc_at(pos, starts)
    doc_in = doc_at(base - 1, starts)
    doc_out = doc_at(base + LANES - 1, starts)
    doc_block = doc_at(block - 1, starts)
    into = jnp.where(doc == doc_in, jnp.exp2(total_to), 0.0)
    into_block = jnp.where(doc == doc_block, jnp.exp2(past + total_to), 0.0)
    fresh = jnp.where(doc == doc_out, jnp.exp2(chunk_total - total_to) * step_dt, 0.0)
    kept = jnp.exp2(chunk_total) * jnp.where(doc_in == doc_out, 1.0, 0.0)
    past_ref[...] = past + chunk_total

    stack_ref[0:heads, :] = total_to
    stack_ref[slot:slot + heads, :] = into
    stack_ref[2 * slot:2 * slot + heads, :] = into_block
    columns = stack_ref[...].T
    reach_ref[...] = columns

    row_pos = base + lax.broadcasted_iota(I32, (LANES, LANES), 0)
    col_pos = base + lax.broadcasted_iota(I32, (LANES, LANES), 1)
    keep = (row_pos >= col_pos) & (doc_at(row_pos, starts) == doc_at(col_pos, starts))
    chosen = dot(pick_matrix(meta[1], groups), c_ref[...])
    c_low = chosen.astype(BF16)
    csel_ref[...] = c_low
    b_low = b_ref[...]
    scores = lax.dot_general(c_low, b_low, (((1,), (1,)), ((), ())), preferred_element_type=F32)
    scores = jnp.where(keep, scores, 0.0)
    b_turned = b_low.astype(F32).T

    for h in range(heads):
        here = slice(h * LANES, (h + 1) * LANES)
        gaps = jnp.minimum(columns[:, h:h + 1] - before[h:h + 1, :], 80.0)
        weights = (jnp.exp2(gaps) * scores).astype(BF16)
        carried = (chosen * columns[:, slot + h:slot + h + 1]).astype(BF16)
        x_head = x_ref[:, here]
        state = state_ref[:, here]
        out = dot(jnp.concatenate([weights, carried], axis=1), jnp.concatenate([x_head, state.astype(BF16)], axis=0))
        out = out + skip_ref[h] * x_head.astype(F32)
        written = dot((b_turned * fresh[h:h + 1, :]).astype(BF16), x_head)
        state_ref[:, here] = state * kept[h:h + 1, :] + written
        z = z_ref[:, here].astype(F32)
        gate = z * (0.5 + 0.5 * jnp.tanh(0.5 * z))
        part_ref[:, here] = (out * gate).astype(BF16)
        gate_ref[:, here] = gate.astype(BF16)


def local_scan(meta, doc_lengths, a_log, d_skip, dt_raw, b_sel, c_rows, x_in, z_gate):
    heads, tokens = dt_raw.shape
    features = x_in.shape[1]
    chunks = tokens // LANES
    groups = c_rows.shape[0] // tokens
    wide = pl.BlockSpec((LANES, features), lambda s, *_: (s, 0))
    narrow = pl.BlockSpec((LANES, LANES), lambda s, *_: (s, 0))
    return pl.pallas_call(
        scan_kernel,
        grid_spec=pltpu.PrefetchScalarGridSpec(
            num_scalar_prefetch=4,
            grid=(chunks,),
            in_specs=[
                pl.BlockSpec((heads, LANES), lambda s, *_: (0, s)),
                narrow,
                pl.BlockSpec((LANES * groups, LANES), lambda s, *_: (s, 0)),
                wide,
                wide,
            ],
            out_specs=[wide, wide, narrow, narrow],
            scratch_shapes=[
                pltpu.VMEM((LANES, features), F32),
                pltpu.VMEM((heads, LANES), F32),
                pltpu.VMEM((LANES, LANES), F32),
            ],
        ),
        out_shape=[
            jax.ShapeDtypeStruct((tokens, features), BF16),
            jax.ShapeDtypeStruct((tokens, features), BF16),
            jax.ShapeDtypeStruct((tokens, LANES), BF16),
            jax.ShapeDtypeStruct((tokens, LANES), F32),
        ],
        compiler_params=params(),
        name="local_scan",
    )(meta, doc_lengths, a_log, d_skip, dt_raw, b_sel, c_rows, x_in, z_gate)


def tile_of(step, half, odd):
    return (step + (1 - odd) * half) % (2 * half)


def one_language(first, size, starts, lang_ref):
    lang = lang_at(first, starts, lang_ref)
    same = jnp.bool_(True)
    for d, s in enumerate(starts):
        inside = (s > first) & (s < first + size)
        same = same & jnp.logical_not(inside & (lang_ref[d] != lang))
    return lang, same


def has_language(which, first, size, starts, len_ref, lang_ref):
    found = jnp.bool_(False)
    for d, s in enumerate(starts):
        overlap = (s < first + size) & (s + len_ref[d] > first)
        found = found | (overlap & (lang_ref[d] == which))
    return found


def combine_kernel(n_states, slot, half, offset, meta, len_ref, lang_ref, c_ref, reach_ref, part_ref, gate_ref, gain_ref, down_ref, *rest):
    states, (gated_ref, other_ref, mine_ref, enter_ref, low_ref) = rest[:n_states], rest[n_states:]
    step = pl.program_id(0)
    tokens, features = part_ref.shape
    heads = features // LANES
    tile = tile_of(step, half, meta[2])
    first = meta[0] + (offset + tile) * tokens
    starts = starts_of(len_ref)

    if n_states > 1:
        @pl.when(step == 0)
        def _():
            total = states[0][...].astype(F32)
            for more in states[1:]:
                total = total + more[...].astype(F32)
            enter_ref[...] = total.astype(BF16)
        entering = enter_ref
    else:
        entering = states[0]

    squares = jnp.zeros((tokens, LANES), F32)
    c_low = c_ref[...]
    reach = reach_ref[...]
    pair = min(2, heads)
    for p in range(heads // pair):
        both = dot(c_low, entering[:, p * pair * LANES:(p + 1) * pair * LANES])
        for i in range(pair):
            h = p * pair + i
            here = slice(h * LANES, (h + 1) * LANES)
            entered = both[:, i * LANES:(i + 1) * LANES] * reach[:, 2 * slot + h:2 * slot + h + 1]
            gated = part_ref[:, here].astype(F32) + entered * gate_ref[:, here].astype(F32)
            squares = squares + gated * gated
            gated_ref[:, here] = (gated * gain_ref[:, here]).astype(BF16)

    lang, same = one_language(first, tokens, starts, lang_ref)

    @pl.when(same)
    def _():
        low_ref[...] = dot(gated_ref[...], down_ref[lang])

    @pl.when(jnp.logical_not(same))
    def _():
        low_ref[...] = jnp.zeros_like(low_ref)
        token_lang = lang_at(first + lax.broadcasted_iota(I32, (tokens, LANES), 0), starts, lang_ref)
        for k in range(down_ref.shape[0]):
            @pl.when(has_language(k, first, tokens, starts, len_ref, lang_ref))
            def _():
                low_ref[...] += jnp.where(token_lang == k, dot(gated_ref[...], down_ref[k]), 0.0)

    ones = jnp.ones((8, LANES), F32)
    sums = lax.dot_general(ones, squares, (((1,), (1,)), ((), ())), precision=lax.Precision.HIGHEST, preferred_element_type=F32)
    rows = jnp.concatenate([sums[:, :LANES], sums[:, LANES:]], axis=0)

    def message(ref):
        ref[0, 0:tokens, :] = low_ref[...].astype(BF16)
        ref[0, tokens:tokens + SUM_ROWS, :] = rows.astype(BF16)

    @pl.when(step < half)
    def _():
        message(other_ref)

    @pl.when(step >= half)
    def _():
        message(mine_ref)


TILE = 2 * LANES


def combine(meta, doc_lengths, doc_lang, c_sel, reach, part, gate, gain, down, states, offset, tiles, slot):
    features = part.shape[1]
    half = tiles // 2
    tile_map = lambda s, meta, *_: (offset + tile_of(s, half, meta[2]), 0)
    whole = lambda s, *_: (0, 0)
    return pl.pallas_call(
        functools.partial(combine_kernel, len(states), slot, half, offset),
        grid_spec=pltpu.PrefetchScalarGridSpec(
            num_scalar_prefetch=3,
            grid=(tiles,),
            in_specs=[
                pl.BlockSpec((TILE, LANES), tile_map),
                pl.BlockSpec((TILE, LANES), tile_map),
                pl.BlockSpec((TILE, features), tile_map),
                pl.BlockSpec((TILE, features), tile_map),
                pl.BlockSpec(gain.shape, whole),
                pl.BlockSpec(down.shape, lambda s, *_: (0, 0, 0)),
            ] + [pl.BlockSpec(v.shape, whole) for v in states],
            out_specs=[
                pl.BlockSpec((TILE, features), lambda s, meta, *_: (tile_of(s, half, meta[2]), 0)),
                pl.BlockSpec((1, TILE + SUM_ROWS, LANES), lambda s, *_: (jnp.minimum(s, half - 1), 0, 0)),
                pl.BlockSpec((1, TILE + SUM_ROWS, LANES), lambda s, *_: (jnp.maximum(s - half, 0), 0, 0)),
            ],
            scratch_shapes=[
                pltpu.VMEM(states[0].shape, BF16),
                pltpu.VMEM((TILE, LANES), F32),
            ],
        ),
        out_shape=[
            jax.ShapeDtypeStruct((tiles * TILE, features), BF16),
            jax.ShapeDtypeStruct((half, TILE + SUM_ROWS, LANES), BF16),
            jax.ShapeDtypeStruct((half, TILE + SUM_ROWS, LANES), BF16),
        ],
        compiler_params=params(),
        name="combine",
    )(meta, doc_lengths, doc_lang, c_sel, reach, part, gate, gain, down, *states)


def finish_kernel(half, offset, all_features, meta, len_ref, lang_ref, mine_ref, other_ref, gated_ref, up_ref, *rest):
    out_ref = rest[-1]
    step = pl.program_id(0)
    tokens, features = gated_ref.shape
    ranks = up_ref.shape[1]
    first = meta[0] + (offset + step) * tokens
    starts = starts_of(len_ref)
    is_mine = (step // half) == meta[2]
    message = jnp.where(is_mine, mine_ref[0].astype(F32), other_ref[0].astype(F32))
    scale = lax.rsqrt(message[tokens:tokens + SUM_ROWS, :] / all_features + EPS)
    turned = jnp.concatenate([scale] * (LANES // SUM_ROWS), axis=0).T
    scale = jnp.concatenate([turned[:, 0:1], turned[:, 8:9]], axis=0)
    low = (message[0:tokens, :] * scale).astype(BF16)
    lang, same = one_language(first, tokens, starts, lang_ref)
    piece = min(4 * LANES, features)

    @pl.when(same)
    def _():
        for at in range(0, features, piece):
            here = slice(at, at + piece)
            lifted = dot(low, up_ref[lang, :, here])
            out_ref[:, here] = (gated_ref[:, here].astype(F32) * scale + lifted).astype(BF16)

    @pl.when(jnp.logical_not(same))
    def _():
        token_lang = lang_at(first + lax.broadcasted_iota(I32, (tokens, LANES), 0), starts, lang_ref)
        zero = jnp.zeros((), BF16)
        spread = jnp.concatenate([jnp.where(token_lang == k, low, zero) for k in range(up_ref.shape[0])], axis=1)
        for at in range(0, features, piece):
            here = slice(at, at + piece)
            lifted = dot(spread, up_ref[:, :, here].reshape(up_ref.shape[0] * ranks, piece))
            out_ref[:, here] = (gated_ref[:, here].astype(F32) * scale + lifted).astype(BF16)


def finish(meta, doc_lengths, doc_lang, mine, other, gated, up, offset, all_tiles, all_features, into=None):
    features = gated.shape[1]
    tiles = gated.shape[0] // TILE
    half = tiles // 2
    part = pl.BlockSpec((1, TILE + SUM_ROWS, LANES), lambda s, *_: (s % half, 0, 0))
    more = [] if into is None else [into]
    return pl.pallas_call(
        functools.partial(finish_kernel, half, offset, all_features),
        grid_spec=pltpu.PrefetchScalarGridSpec(
            num_scalar_prefetch=3,
            grid=(tiles,),
            in_specs=[
                part,
                part,
                pl.BlockSpec((TILE, features), lambda s, *_: (s, 0)),
                pl.BlockSpec(up.shape, lambda s, *_: (0, 0, 0)),
            ] + [pl.BlockSpec(memory_space=pl.ANY) for _ in more],
            out_specs=pl.BlockSpec((TILE, features), lambda s, *_: (offset + s, 0)),
        ),
        out_shape=jax.ShapeDtypeStruct((all_tiles * TILE, features), BF16),
        input_output_aliases={7: 0} if more else {},
        compiler_params=params(),
        name="finish",
    )(meta, doc_lengths, doc_lang, mine, other, gated, up, *more)


def sum_over_head(other, mine, devices):
    def across(v, mask):
        return lax.ppermute(v, "head", [(i, i ^ mask) for i in range(devices)])

    if devices == 1:
        return mine, other
    total = (mine.astype(F32) + across(other, 1).astype(F32)).astype(BF16)
    bit = 2
    while bit < devices:
        masks = [bit] if 2 * bit >= devices else [bit, 2 * bit, 3 * bit]
        arrived = [across(total, m) for m in masks]
        added = total.astype(F32)
        for a in arrived:
            added = added + a.astype(F32)
        total = added.astype(BF16)
        bit *= 2 ** (1 if len(masks) == 1 else 2)
    return total, across(total, 1)


def per_device(seq_size, head_size, x_in, z_gate, b_input, c_input, dt_raw, a_log, d_skip, norm_gain,
               doc_lengths, doc_lang, adapt_down, adapt_up):
    tokens, features = x_in.shape
    heads = dt_raw.shape[0]
    groups = b_input.shape[1]
    head_rank = lax.axis_index("head")
    group = head_rank * heads // (heads * head_size // groups)
    meta = jnp.stack([lax.axis_index("seq") * tokens, group, head_rank % 2]).astype(I32)
    b_rows = b_input.reshape(tokens * groups, b_input.shape[2])
    c_rows = c_input.reshape(tokens * groups, c_input.shape[2])
    longest = tokens * seq_size // LONGEST_SHARE
    hops = min(-(-(longest - 1) // tokens), seq_size - 1)

    state, through, b_sel = block_states(meta, doc_lengths, a_log, dt_raw, b_rows, x_in)
    onward = [(i, i + 1) for i in range(seq_size - 1)]
    states = []
    for hop in range(hops):
        if hop > 0:
            state = (state.astype(F32) * through[0:1]).astype(BF16)
        state = lax.ppermute(state, "seq", onward)
        states.append(state)
    part, gate, c_sel, reach = local_scan(meta, doc_lengths, a_log, d_skip, dt_raw, b_sel, c_rows, x_in, z_gate)
    slot = max(8, heads)
    all_tiles = tokens // TILE
    gated, other, mine = combine(
        meta, doc_lengths, doc_lang, c_sel, reach, part, gate, norm_gain.reshape(1, features), adapt_down, states, 0, all_tiles, slot
    )
    mine, other = sum_over_head(other, mine, head_size)
    return finish(meta, doc_lengths, doc_lang, mine, other, gated, adapt_up, 0, all_tiles, features * head_size)


def solution(mesh):
    placed = (
        P("seq", "head"),
        P("seq", "head"),
        P("seq", None, None),
        P("seq", None, None),
        P("head", "seq"),
        P("head"),
        P("head"),
        P("head"),
        P(),
        P(),
        P(None, "head", None),
        P(None, None, "head"),
    )
    return jax.shard_map(
        functools.partial(per_device, mesh.shape["seq"], mesh.shape["head"]),
        mesh=mesh, in_specs=placed, out_specs=P("seq", "head"), check_vma=False,
    )
```

```python
import functools

import jax
import jax.numpy as jnp
from jax import lax
from jax.experimental import pallas as pl
from jax.experimental.pallas import tpu as pltpu
from jax.sharding import PartitionSpec as P

F32 = jnp.float32
BF16 = jnp.bfloat16
I32 = jnp.int32
LOG2E = 1.4426950408889634
EPS = 1e-05
LANES = 128
SUM_ROWS = 16
LONGEST_SHARE = 3
VMEM_LIMIT = 16 * 1024 * 1024


def params():
    return pltpu.CompilerParams(vmem_limit_bytes=VMEM_LIMIT)


def starts_of(docs):
    starts, at = [], jnp.int32(0)
    for d in range(docs.shape[0] // 2):
        starts.append(at)
        at = at + docs[d]
    return starts


def langs_of(docs):
    count = docs.shape[0] // 2
    return [docs[count + d] for d in range(count)]


def doc_at(pos, starts):
    found = jnp.where(pos >= starts[0], 0, -1)
    for s in starts[1:]:
        found = found + jnp.where(pos >= s, 1, 0)
    return found


def lang_at(pos, starts, lang_ref):
    found = jnp.where(pos >= 0, lang_ref[0], 0)
    for d in range(1, len(starts)):
        found = jnp.where(pos >= starts[d], lang_ref[d], found)
    return found


def rates(alog_ref, rows):
    which = lax.broadcasted_iota(I32, (rows, LANES), 0)
    column = jnp.zeros((rows, LANES), F32)
    for h in range(rows):
        column = jnp.where(which == h, alog_ref[h], column)
    return -LOG2E * jnp.exp(column)


def softplus(v):
    return jnp.maximum(v, 0.0) + jnp.log(1.0 + jnp.exp(-jnp.abs(v)))


def running(v, back):
    width = v.shape[1]
    lane = lax.broadcasted_iota(I32, v.shape, 1)
    step = 1
    while step < width:
        if back:
            v = v + jnp.where(lane + step < width, pltpu.roll(v, width - step, 1), 0.0)
        else:
            v = v + jnp.where(lane >= step, pltpu.roll(v, step, 1), 0.0)
        step *= 2
    return v


def pick_matrix(group, groups):
    shape = (LANES, LANES * groups)
    row = lax.broadcasted_iota(I32, shape, 0)
    col = lax.broadcasted_iota(I32, shape, 1)
    return jnp.where(col == row * groups + group, 1.0, 0.0).astype(BF16)


def dot(a, b):
    return jnp.dot(a, b, preferred_element_type=F32)


def state_kernel(x_parts, b_parts, meta, docs, alog_ref, dt_hbm, b_hbm, x_hbm, state_ref, thr_ref, bsel_ref, x_ref,
                 dt_ref, b_ref, bt_ref, w_ref, all_ref, sems):
    heads, tokens = dt_ref.shape
    groups = b_ref.shape[0] // tokens
    features = x_ref.shape[1]
    rows = b_ref.shape[0] // b_parts
    wide = features // x_parts
    dt_copy = pltpu.make_async_copy(dt_hbm, dt_ref, sems.at[0])
    b_copies = [
        pltpu.make_async_copy(b_hbm.at[pl.ds(i * rows, rows)], b_ref.at[pl.ds(i * rows, rows)], sems.at[1 + i])
        for i in range(b_parts)
    ]
    x_copies = [
        pltpu.make_async_copy(x_hbm.at[:, pl.ds(i * wide, wide)], x_ref.at[:, pl.ds(i * wide, wide)], sems.at[1 + b_parts + i])
        for i in range(x_parts)
    ]
    for copy in [dt_copy] + b_copies + x_copies:
        copy.start()

    dt_copy.wait()
    starts = starts_of(docs)
    base = meta[0]
    rate = rates(alog_ref, heads)
    parts, totals = [], []
    for c in range(tokens // LANES):
        step_dt = softplus(dt_ref[:, c * LANES:(c + 1) * LANES])
        decay = step_dt * rate
        after = running(decay, True)
        parts.append((step_dt, after - decay))
        totals.append(after[:, 0:1])
    last_doc = doc_at(base + tokens - 1, starts)
    first_doc = doc_at(base - 1, starts)
    later = jnp.zeros((heads, 1), F32)
    for c in reversed(range(tokens // LANES)):
        step_dt, inside = parts[c]
        pos = base + c * LANES + lax.broadcasted_iota(I32, (heads, LANES), 1)
        alive = doc_at(pos, starts) == last_doc
        w_ref[:, c * LANES:(c + 1) * LANES] = jnp.where(alive, jnp.exp2(inside + later) * step_dt, 0.0)
        later = later + totals[c]
    kept = jnp.where(last_doc == first_doc, 1.0, 0.0)
    all_ref[...] = jnp.broadcast_to(jnp.exp2(later) * kept, all_ref.shape)

    pick = pick_matrix(meta[1], groups)
    per = tokens // LANES // b_parts
    for i in range(b_parts):
        b_copies[i].wait()
        for c in range(i * per, (i + 1) * per):
            here = slice(c * LANES, (c + 1) * LANES)
            chosen = dot(pick, b_ref[c * LANES * groups:(c + 1) * LANES * groups, :])
            bsel_ref[here, :] = chosen.astype(BF16)
            bt_ref[:, here] = chosen.T

    for i in range(x_parts):
        x_copies[i].wait()
        for h in range(i * heads // x_parts, (i + 1) * heads // x_parts):
            here = slice(h * LANES, (h + 1) * LANES)
            weighted = (bt_ref[...] * w_ref[h:h + 1, :]).astype(BF16)
            state_ref[:, here] = dot(weighted, x_ref[:, here]).astype(BF16)
            thr_ref[:, here] = jnp.broadcast_to(all_ref[h:h + 1, :], (8, LANES))


def in_vmem():
    return pl.BlockSpec(memory_space=pltpu.VMEM)


def block_states(meta, docs, a_log, dt_raw, b_rows, x_in):
    heads, tokens = dt_raw.shape
    features = x_in.shape[1]
    x_parts, b_parts = min(4, heads), 4
    anywhere = pl.BlockSpec(memory_space=pl.ANY)
    return pl.pallas_call(
        functools.partial(state_kernel, x_parts, b_parts),
        grid_spec=pltpu.PrefetchScalarGridSpec(
            num_scalar_prefetch=3,
            grid=(1,),
            in_specs=[anywhere, anywhere, anywhere],
            out_specs=[in_vmem(), in_vmem(), in_vmem(), in_vmem()],
            scratch_shapes=[
                pltpu.VMEM((heads, tokens), F32),
                pltpu.VMEM(b_rows.shape, BF16),
                pltpu.VMEM((LANES, tokens), F32),
                pltpu.VMEM((heads, tokens), F32),
                pltpu.VMEM((heads, LANES), F32),
                pltpu.SemaphoreType.DMA((1 + b_parts + x_parts,)),
            ],
        ),
        out_shape=[
            pltpu.VMEM((LANES, features), BF16),
            pltpu.VMEM((8, features), F32),
            pltpu.VMEM((tokens, LANES), BF16),
            pltpu.VMEM((tokens, features), BF16),
        ],
        compiler_params=params(),
        cost_estimate=pl.CostEstimate(flops=2 * LANES * tokens * features, bytes_accessed=8 * tokens * features, transcendentals=0),
        name="block_states",
    )(meta, docs, a_log, *[pltpu.with_memory_space_constraint(v, pltpu.HBM) for v in (dt_raw, b_rows, x_in)])


def scan_kernel(meta, docs, alog_ref, skip_ref, dt_ref, b_ref, c_ref, x_ref, z_ref,
                part_ref, gate_ref, csel_ref, reach_ref, state_ref, past_ref, stack_ref):
    step = pl.program_id(0)
    heads, tokens = dt_ref.shape
    groups = c_ref.shape[0] // tokens
    slot = max(8, heads)
    starts = starts_of(docs)
    now = pl.ds(pl.multiple_of(step * LANES, LANES), LANES)
    block = meta[0]
    base = block + step * LANES

    @pl.when(step == 0)
    def _():
        state_ref[...] = jnp.zeros_like(state_ref)
        past_ref[...] = jnp.zeros_like(past_ref)
        stack_ref[...] = jnp.zeros_like(stack_ref)

    step_dt = softplus(dt_ref[:, now])
    decay = step_dt * rates(alog_ref, heads)
    total_to = running(decay, False)
    chunk_total = jnp.broadcast_to(total_to[:, LANES - 1:LANES], (heads, LANES))
    past = past_ref[...]
    before = total_to - jnp.log(step_dt) * LOG2E

    pos = base + lax.broadcasted_iota(I32, (heads, LANES), 1)
    doc = doc_at(pos, starts)
    doc_in = doc_at(base - 1, starts)
    doc_out = doc_at(base + LANES - 1, starts)
    doc_block = doc_at(block - 1, starts)
    into = jnp.where(doc == doc_in, jnp.exp2(total_to), 0.0)
    into_block = jnp.where(doc == doc_block, jnp.exp2(past + total_to), 0.0)
    fresh = jnp.where(doc == doc_out, jnp.exp2(chunk_total - total_to) * step_dt, 0.0)
    kept = jnp.exp2(chunk_total) * jnp.where(doc_in == doc_out, 1.0, 0.0)
    past_ref[...] = past + chunk_total

    stack_ref[0:heads, :] = total_to
    stack_ref[slot:slot + heads, :] = into
    stack_ref[2 * slot:2 * slot + heads, :] = into_block
    columns = stack_ref[...].T
    reach_ref[now, :] = columns

    row_pos = base + lax.broadcasted_iota(I32, (LANES, LANES), 0)
    col_pos = base + lax.broadcasted_iota(I32, (LANES, LANES), 1)
    keep = (row_pos >= col_pos) & (doc_at(row_pos, starts) == doc_at(col_pos, starts))
    chosen = dot(pick_matrix(meta[1], groups), c_ref[pl.ds(pl.multiple_of(step * LANES * groups, LANES), LANES * groups), :])
    c_low = chosen.astype(BF16)
    csel_ref[now, :] = c_low
    b_low = b_ref[now, :]
    scores = lax.dot_general(c_low, b_low, (((1,), (1,)), ((), ())), preferred_element_type=F32)
    scores = jnp.where(keep, scores, 0.0)
    b_turned = b_low.astype(F32).T

    for h in range(heads):
        here = slice(h * LANES, (h + 1) * LANES)
        gaps = jnp.minimum(columns[:, h:h + 1] - before[h:h + 1, :], 80.0)
        weights = (jnp.exp2(gaps) * scores).astype(BF16)
        carried = (chosen * columns[:, slot + h:slot + h + 1]).astype(BF16)
        x_head = x_ref[now, here]
        state = state_ref[:, here]
        out = dot(jnp.concatenate([weights, carried], axis=1), jnp.concatenate([x_head, state.astype(BF16)], axis=0))
        out = out + skip_ref[h] * x_head.astype(F32)
        written = dot((b_turned * fresh[h:h + 1, :]).astype(BF16), x_head)
        state_ref[:, here] = state * kept[h:h + 1, :] + written
        z = 0.5 * z_ref[now, here].astype(F32)
        gate = z + z * jnp.tanh(z)
        part_ref[now, here] = out * gate
        gate_ref[now, here] = gate.astype(BF16)


def local_scan(meta, docs, a_log, d_skip, dt_raw, b_sel, c_rows, x_in, z_gate):
    heads, tokens = dt_raw.shape
    features = x_in.shape[1]
    chunks = tokens // LANES
    held = [pltpu.with_memory_space_constraint(v, pltpu.VMEM) for v in (dt_raw, c_rows, z_gate)]
    return pl.pallas_call(
        scan_kernel,
        grid_spec=pltpu.PrefetchScalarGridSpec(
            num_scalar_prefetch=4,
            grid=(chunks,),
            in_specs=[in_vmem()] * 5,
            out_specs=[in_vmem()] * 4,
            scratch_shapes=[
                pltpu.VMEM((LANES, features), F32),
                pltpu.VMEM((heads, LANES), F32),
                pltpu.VMEM((LANES, LANES), F32),
            ],
        ),
        out_shape=[
            pltpu.VMEM((tokens, features), F32),
            pltpu.VMEM((tokens, features), BF16),
            pltpu.VMEM((tokens, LANES), BF16),
            pltpu.VMEM((tokens, LANES), F32),
        ],
        compiler_params=params(),
        cost_estimate=pl.CostEstimate(flops=16 * LANES * tokens * features, bytes_accessed=8 * tokens * features, transcendentals=0),
        name="local_scan",
    )(meta, docs, a_log, d_skip, held[0], b_sel, held[1], x_in, held[2])


def tile_of(step, half, odd):
    return (step + (1 - odd) * half) % (2 * half)


def one_language(first, size, starts, lang_ref):
    lang = lang_at(first, starts, lang_ref)
    same = jnp.bool_(True)
    for d, s in enumerate(starts):
        inside = (s > first) & (s < first + size)
        same = same & jnp.logical_not(inside & (lang_ref[d] != lang))
    return lang, same


def has_language(which, first, size, starts, lang_ref):
    found = lang_at(first, starts, lang_ref) == which
    for d, s in enumerate(starts):
        found = found | ((s > first) & (s < first + size) & (lang_ref[d] == which))
    return found


def combine_kernel(n_states, slot, half, offset, meta, docs, c_ref, reach_ref, part_ref, gate_ref, gain_ref, down_ref, *rest):
    states, (all_gated_ref, other_ref, mine_ref, enter_ref, low_ref) = rest[:n_states], rest[n_states:]
    step = pl.program_id(0)
    tokens, features = TILE, part_ref.shape[1]
    heads = features // LANES
    tile = tile_of(step, half, meta[2])
    now = pl.ds(pl.multiple_of((offset + tile) * tokens, tokens), tokens)
    gated_ref = all_gated_ref.at[pl.ds(pl.multiple_of(tile * tokens, tokens), tokens)]
    first = meta[0] + (offset + tile) * tokens
    starts = starts_of(docs)
    lang_ref = langs_of(docs)

    if n_states > 1:
        @pl.when(step == 0)
        def _():
            total = states[0][...].astype(F32)
            for more in states[1:]:
                total = total + more[...].astype(F32)
            enter_ref[...] = total.astype(BF16)
        entering = enter_ref
    else:
        entering = states[0]

    squares = jnp.zeros((tokens, LANES), F32)
    c_low = c_ref[now, :]
    reach = reach_ref[now, :]
    pair = min(2, heads)
    for p in range(heads // pair):
        both = dot(c_low, entering[:, p * pair * LANES:(p + 1) * pair * LANES])
        for i in range(pair):
            h = p * pair + i
            here = slice(h * LANES, (h + 1) * LANES)
            entered = both[:, i * LANES:(i + 1) * LANES] * reach[:, 2 * slot + h:2 * slot + h + 1]
            gated = part_ref[now, here] + entered * gate_ref[now, here].astype(F32)
            squares = squares + gated * gated
            gated_ref[:, here] = (gated * gain_ref[:, here]).astype(BF16)

    lang, same = one_language(first, tokens, starts, lang_ref)

    @pl.when(same)
    def _():
        low_ref[...] = dot(gated_ref[...], down_ref[lang])

    @pl.when(jnp.logical_not(same))
    def _():
        low_ref[...] = jnp.zeros_like(low_ref)
        token_lang = lang_at(first + lax.broadcasted_iota(I32, (tokens, LANES), 0), starts, lang_ref)
        for k in range(down_ref.shape[0]):
            @pl.when(has_language(k, first, tokens, starts, lang_ref))
            def _():
                low_ref[...] += jnp.where(token_lang == k, dot(gated_ref[...], down_ref[k]), 0.0)

    ones = jnp.ones((8, LANES), F32)
    sums = lax.dot_general(ones, squares, (((1,), (1,)), ((), ())), precision=lax.Precision.HIGHEST, preferred_element_type=F32)
    rows = jnp.concatenate([sums[:, :LANES], sums[:, LANES:]], axis=0)

    def message(ref, at):
        ref[at, 0:tokens, :] = low_ref[...].astype(BF16)
        ref[at, tokens:tokens + SUM_ROWS, :] = rows.astype(BF16)

    @pl.when(step < half)
    def _():
        message(other_ref, step)

    @pl.when(step >= half)
    def _():
        message(mine_ref, step - half)


TILE = 2 * LANES


def combine(meta, docs, c_sel, reach, part, gate, gain, down, states, offset, tiles, slot):
    features = part.shape[1]
    half = tiles // 2
    held = [pltpu.with_memory_space_constraint(v, pltpu.VMEM) for v in [gain, down] + states]
    return pl.pallas_call(
        functools.partial(combine_kernel, len(states), slot, half, offset),
        grid_spec=pltpu.PrefetchScalarGridSpec(
            num_scalar_prefetch=2,
            grid=(tiles,),
            in_specs=[in_vmem()] * (6 + len(states)),
            out_specs=[in_vmem()] * 3,
            scratch_shapes=[
                pltpu.VMEM(states[0].shape, BF16),
                pltpu.VMEM((TILE, LANES), F32),
            ],
        ),
        out_shape=[
            pltpu.VMEM((tiles * TILE, features), BF16),
            pltpu.VMEM((half, TILE + SUM_ROWS, LANES), BF16),
            pltpu.VMEM((half, TILE + SUM_ROWS, LANES), BF16),
        ],
        compiler_params=params(),
        cost_estimate=pl.CostEstimate(flops=16 * LANES * tiles * TILE * features, bytes_accessed=8 * tiles * TILE * features, transcendentals=0),
        name="combine",
    )(meta, docs, c_sel, reach, part, gate, *held)


def finish_kernel(half, offset, all_features, meta, docs, mine_ref, other_ref, all_gated_ref, up_ref, *rest):
    out_ref = rest[-1]
    step = pl.program_id(0)
    tokens, features = TILE, all_gated_ref.shape[1]
    gated_ref = all_gated_ref.at[pl.ds(pl.multiple_of(step * tokens, tokens), tokens)]
    ranks = up_ref.shape[1]
    first = meta[0] + (offset + step) * tokens
    starts = starts_of(docs)
    lang_ref = langs_of(docs)
    is_mine = (step // half) == meta[2]
    part = step % half
    message = jnp.where(is_mine, mine_ref[part].astype(F32), other_ref[part].astype(F32))
    scale = lax.rsqrt(message[tokens:tokens + SUM_ROWS, :] / all_features + EPS)
    turned = jnp.concatenate([scale] * (LANES // SUM_ROWS), axis=0).T
    scale = jnp.concatenate([turned[:, 0:1], turned[:, 8:9]], axis=0)
    low = (message[0:tokens, :] * scale).astype(BF16)
    lang, same = one_language(first, tokens, starts, lang_ref)
    piece = min(4 * LANES, features)

    @pl.when(same)
    def _():
        for at in range(0, features, piece):
            here = slice(at, at + piece)
            lifted = dot(low, up_ref[lang, :, here])
            out_ref[:, here] = (gated_ref[:, here].astype(F32) * scale + lifted).astype(BF16)

    @pl.when(jnp.logical_not(same))
    def _():
        token_lang = lang_at(first + lax.broadcasted_iota(I32, (tokens, LANES), 0), starts, lang_ref)
        zero = jnp.zeros((), BF16)
        spread = jnp.concatenate([jnp.where(token_lang == k, low, zero) for k in range(up_ref.shape[0])], axis=1)
        for at in range(0, features, piece):
            here = slice(at, at + piece)
            lifted = dot(spread, up_ref[:, :, here].reshape(up_ref.shape[0] * ranks, piece))
            out_ref[:, here] = (gated_ref[:, here].astype(F32) * scale + lifted).astype(BF16)


def finish(meta, docs, mine, other, gated, up, offset, all_tiles, all_features, into=None):
    features = gated.shape[1]
    tiles = gated.shape[0] // TILE
    half = tiles // 2
    held = [pltpu.with_memory_space_constraint(v, pltpu.VMEM) for v in (mine, other, gated, up)]
    more = [] if into is None else [into]
    return pl.pallas_call(
        functools.partial(finish_kernel, half, offset, all_features),
        grid_spec=pltpu.PrefetchScalarGridSpec(
            num_scalar_prefetch=2,
            grid=(tiles,),
            in_specs=[in_vmem()] * 4 + [pl.BlockSpec(memory_space=pl.ANY) for _ in more],
            out_specs=pl.BlockSpec((TILE, features), lambda s, *_: (offset + s, 0)),
        ),
        out_shape=jax.ShapeDtypeStruct((all_tiles * TILE, features), BF16),
        input_output_aliases={6: 0} if more else {},
        compiler_params=params(),
        cost_estimate=pl.CostEstimate(flops=2 * LANES * tiles * TILE * features, bytes_accessed=8 * tiles * TILE * features, transcendentals=0),
        name="finish",
    )(meta, docs, *held, *more)


def sum_over_head(other, mine, devices):
    def across(v, mask):
        return lax.ppermute(v, "head", [(i, i ^ mask) for i in range(devices)])

    if devices == 1:
        return mine, other
    total = (mine.astype(F32) + across(other, 1).astype(F32)).astype(BF16)
    bit = 2
    while bit < devices:
        masks = [bit] if 2 * bit >= devices else [bit, 2 * bit, 3 * bit]
        arrived = [across(total, m) for m in masks]
        added = total.astype(F32)
        for a in arrived:
            added = added + a.astype(F32)
        total = added.astype(BF16)
        bit *= 2 ** (1 if len(masks) == 1 else 2)
    return total, across(total, 1)


def per_device(seq_size, head_size, x_in, z_gate, b_input, c_input, dt_raw, a_log, d_skip, norm_gain,
               doc_lengths, doc_lang, adapt_down, adapt_up):
    tokens, features = x_in.shape
    heads = dt_raw.shape[0]
    groups = b_input.shape[1]
    head_rank = lax.axis_index("head")
    group = head_rank * heads // (heads * head_size // groups)
    meta = jnp.stack([lax.axis_index("seq") * tokens, group, head_rank % 2]).astype(I32)
    b_rows = b_input.reshape(tokens * groups, b_input.shape[2])
    c_rows = c_input.reshape(tokens * groups, c_input.shape[2])
    longest = tokens * seq_size // LONGEST_SHARE
    hops = min(-(-(longest - 1) // tokens), seq_size - 1)

    docs = jnp.concatenate([doc_lengths, doc_lang])
    gain = norm_gain.reshape(1, features)
    all_features = features * head_size
    slot = max(8, heads)
    all_tiles = tokens // TILE
    reached = longest - 1 - (hops - 1) * tokens
    head_tiles = -(-reached // (2 * TILE)) * 2

    state, through, b_sel, x_held = block_states(meta, docs, a_log, dt_raw, b_rows, x_in)
    onward = [(i, i + 1) for i in range(seq_size - 1)]

    arrived = lax.ppermute(state, "seq", onward)
    part, gate, c_sel, reach = local_scan(meta, docs, a_log, d_skip, dt_raw, b_sel, c_rows, x_held, z_gate)
    arrived, part = lax.optimization_barrier((arrived, part))
    states = [arrived]
    for hop in range(1, hops):
        arrived = lax.ppermute((arrived.astype(F32) * through[0:1]).astype(BF16), "seq", onward)
        states.append(arrived)

    def joined(states, offset, tiles):
        return combine(meta, docs, c_sel, reach, part, gate, gain, adapt_down, states, offset, tiles, slot)

    if hops < 2 or head_tiles >= all_tiles:
        gated, other, mine = joined(states, 0, all_tiles)
        mine, other = sum_over_head(other, mine, head_size)
        return finish(meta, docs, mine, other, gated, adapt_up, 0, all_tiles, all_features)
    late, other, mine = joined(states[:-1], head_tiles, all_tiles - head_tiles)
    late_sums = sum_over_head(other, mine, head_size)
    early, other, mine = joined(states, 0, head_tiles)
    early_sums = sum_over_head(other, mine, head_size)
    out = finish(meta, docs, *late_sums, late, adapt_up, head_tiles, all_tiles, all_features)
    return finish(meta, docs, *early_sums, early, adapt_up, 0, all_tiles, all_features, out)


def solution(mesh):
    placed = (
        P("seq", "head"),
        P("seq", "head"),
        P("seq", None, None),
        P("seq", None, None),
        P("head", "seq"),
        P("head"),
        P("head"),
        P("head"),
        P(),
        P(),
        P(None, "head", None),
        P(None, None, "head"),
    )
    return jax.shard_map(
        functools.partial(per_device, mesh.shape["seq"], mesh.shape["head"]),
        mesh=mesh, in_specs=placed, out_specs=P("seq", "head"), check_vma=False,
    )
```

```python
import functools

import jax
import jax.numpy as jnp
from jax import lax
from jax.experimental import pallas as pl
from jax.experimental.pallas import tpu as pltpu
from jax.sharding import PartitionSpec as P

F32 = jnp.float32
BF16 = jnp.bfloat16
I32 = jnp.int32
LOG2E = 1.4426950408889634
EPS = 1e-05
LANES = 128
LONGEST_SHARE = 3
VMEM_LIMIT = 16 * 1024 * 1024


def params():
    return pltpu.CompilerParams(vmem_limit_bytes=VMEM_LIMIT)


def starts_of(len_ref):
    starts, at = [], jnp.int32(0)
    for d in range(len_ref.shape[0]):
        starts.append(at)
        at = at + len_ref[d]
    return starts


def doc_at(pos, starts):
    found = jnp.where(pos >= starts[0], 0, -1)
    for s in starts[1:]:
        found = found + jnp.where(pos >= s, 1, 0)
    return found


def lang_at(pos, starts, lang_ref):
    found = jnp.where(pos >= 0, lang_ref[0], 0)
    for d in range(1, len(starts)):
        found = jnp.where(pos >= starts[d], lang_ref[d], found)
    return found


def rates(alog_ref, rows):
    which = lax.broadcasted_iota(I32, (rows, LANES), 0)
    column = jnp.zeros((rows, LANES), F32)
    for h in range(rows):
        column = jnp.where(which == h, alog_ref[h], column)
    return -LOG2E * jnp.exp(column)


def softplus(v):
    return jnp.maximum(v, 0.0) + jnp.log(1.0 + jnp.exp(-jnp.abs(v)))


def running(v, back):
    width = v.shape[1]
    lane = lax.broadcasted_iota(I32, v.shape, 1)
    step = 1
    while step < width:
        if back:
            v = v + jnp.where(lane + step < width, pltpu.roll(v, width - step, 1), 0.0)
        else:
            v = v + jnp.where(lane >= step, pltpu.roll(v, step, 1), 0.0)
        step *= 2
    return v


def pick_matrix(group, groups):
    shape = (LANES, LANES * groups)
    row = lax.broadcasted_iota(I32, shape, 0)
    col = lax.broadcasted_iota(I32, shape, 1)
    return jnp.where(col == row * groups + group, 1.0, 0.0).astype(BF16)


def dot(a, b):
    return jnp.dot(a, b, preferred_element_type=F32)


def group_of(head_rank, heads, head_size, groups):
    return head_rank * heads // (heads * head_size // groups)


def state_kernel(head_size, len_hbm, alog_hbm, dt_hbm, b_hbm, x_hbm, state_ref, thr_ref, bsel_ref, bt_ref, x_ref,
                 len_ref, alog_ref, dt_ref, b_ref, w_ref, all_ref, sems):
    heads, tokens = dt_ref.shape
    groups = b_ref.shape[0] // tokens
    copies = [
        pltpu.make_async_copy(source, target, sems.at[i])
        for i, (source, target) in enumerate([
            (dt_hbm, dt_ref), (len_hbm, len_ref), (alog_hbm, alog_ref), (b_hbm, b_ref), (x_hbm, x_ref),
        ])
    ]
    for copy in copies:
        copy.start()
    for copy in copies[:3]:
        copy.wait()

    starts = starts_of(len_ref)
    base = lax.axis_index("seq") * tokens
    rate = rates(alog_ref, heads)
    parts, totals = [], []
    for c in range(tokens // LANES):
        step_dt = softplus(dt_ref[:, c * LANES:(c + 1) * LANES])
        decay = step_dt * rate
        after = running(decay, True)
        parts.append((step_dt, after - decay))
        totals.append(after[:, 0:1])
    last_doc = doc_at(base + tokens - 1, starts)
    first_doc = doc_at(base - 1, starts)
    later = jnp.zeros((heads, 1), F32)
    for c in reversed(range(tokens // LANES)):
        step_dt, inside = parts[c]
        pos = base + c * LANES + lax.broadcasted_iota(I32, (heads, LANES), 1)
        alive = doc_at(pos, starts) == last_doc
        w_ref[:, c * LANES:(c + 1) * LANES] = jnp.where(alive, jnp.exp2(inside + later) * step_dt, 0.0)
        later = later + totals[c]
    kept = jnp.where(last_doc == first_doc, 1.0, 0.0)
    all_ref[...] = jnp.broadcast_to(jnp.exp2(later) * kept, all_ref.shape)
    for h in range(heads):
        thr_ref[:, h * LANES:(h + 1) * LANES] = jnp.broadcast_to(all_ref[h:h + 1, :], (8, LANES))

    pick = pick_matrix(group_of(lax.axis_index("head"), heads, head_size, groups), groups)
    copies[3].wait()
    for c in range(tokens // LANES):
        here = slice(c * LANES, (c + 1) * LANES)
        chosen = dot(pick, b_ref[c * LANES * groups:(c + 1) * LANES * groups, :])
        bsel_ref[here, :] = chosen.astype(BF16)
        bt_ref[:, here] = chosen.T.astype(BF16)

    copies[4].wait()
    for h in range(heads):
        here = slice(h * LANES, (h + 1) * LANES)
        weighted = bt_ref[...] * w_ref[h:h + 1, :].astype(BF16)
        state_ref[:, here] = dot(weighted, x_ref[:, here]).astype(BF16)


def in_vmem():
    return pl.BlockSpec(memory_space=pltpu.VMEM)


def block_states(head_size, doc_lengths, a_log, dt_raw, b_rows, x_in):
    heads, tokens = dt_raw.shape
    features = x_in.shape[1]
    return pl.pallas_call(
        functools.partial(state_kernel, head_size),
        grid_spec=pltpu.PrefetchScalarGridSpec(
            num_scalar_prefetch=0,
            grid=(1,),
            in_specs=[pl.BlockSpec(memory_space=pl.ANY)] * 5,
            out_specs=[in_vmem()] * 5,
            scratch_shapes=[
                pltpu.SMEM(doc_lengths.shape, I32),
                pltpu.SMEM(a_log.shape, F32),
                pltpu.VMEM((heads, tokens), F32),
                pltpu.VMEM(b_rows.shape, BF16),
                pltpu.VMEM((heads, tokens), F32),
                pltpu.VMEM((heads, LANES), F32),
                pltpu.SemaphoreType.DMA((5,)),
            ],
        ),
        out_shape=[
            pltpu.VMEM((LANES, features), BF16),
            pltpu.VMEM((8, features), F32),
            pltpu.VMEM((tokens, LANES), BF16),
            pltpu.VMEM((LANES, tokens), BF16),
            pltpu.VMEM((tokens, features), BF16),
        ],
        compiler_params=params(),
        cost_estimate=pl.CostEstimate(flops=2 * LANES * tokens * features, bytes_accessed=8 * tokens * features, transcendentals=0),
        name="block_states",
    )(*[pltpu.with_memory_space_constraint(v, pltpu.HBM) for v in (doc_lengths, a_log, dt_raw, b_rows, x_in)])


def scan_kernel(head_size, len_ref, alog_ref, skip_ref, dt_ref, b_ref, bt_ref, c_ref, x_ref, z_ref,
                part_ref, gate_ref, csel_ref, reach_ref, state_ref, before_ref, fresh_ref, kept_ref, scores_ref, stack_ref):
    step = pl.program_id(0)
    heads, tokens = dt_ref.shape
    groups = c_ref.shape[0] // tokens
    slot = max(8, heads)

    @pl.when(step == 0)
    def _():
        state_ref[...] = jnp.zeros_like(state_ref)
        stack_ref[...] = jnp.zeros_like(stack_ref)
        starts = starts_of(len_ref)
        block = lax.axis_index("seq") * tokens
        rate = rates(alog_ref, heads)
        pick = pick_matrix(group_of(lax.axis_index("head"), heads, head_size, groups), groups)
        past = jnp.zeros((heads, LANES), F32)
        doc_block = doc_at(block - 1, starts)
        for c in range(tokens // LANES):
            here = slice(c * LANES, (c + 1) * LANES)
            base = block + c * LANES
            step_dt = softplus(dt_ref[:, here])
            total_to = running(step_dt * rate, False)
            chunk_total = jnp.broadcast_to(total_to[:, LANES - 1:LANES], (heads, LANES))
            before_ref[:, here] = total_to - jnp.log(step_dt) * LOG2E
            doc = doc_at(base + lax.broadcasted_iota(I32, (heads, LANES), 1), starts)
            doc_in = doc_at(base - 1, starts)
            doc_out = doc_at(base + LANES - 1, starts)
            fresh_ref[:, here] = jnp.where(doc == doc_out, jnp.exp2(chunk_total - total_to) * step_dt, 0.0)
            kept_ref[c] = jnp.exp2(chunk_total) * jnp.where(doc_in == doc_out, 1.0, 0.0)
            stack_ref[c, 0:heads, :] = total_to
            stack_ref[c, slot:slot + heads, :] = jnp.where(doc == doc_in, jnp.exp2(total_to), 0.0)
            stack_ref[c, 2 * slot:2 * slot + heads, :] = jnp.where(doc == doc_block, jnp.exp2(past + total_to), 0.0)
            past = past + chunk_total
            reach_ref[here, :] = stack_ref[c].T
            row_pos = base + lax.broadcasted_iota(I32, (LANES, LANES), 0)
            col_pos = base + lax.broadcasted_iota(I32, (LANES, LANES), 1)
            keep = (row_pos >= col_pos) & (doc_at(row_pos, starts) == doc_at(col_pos, starts))
            c_low = dot(pick, c_ref[c * LANES * groups:(c + 1) * LANES * groups, :]).astype(BF16)
            csel_ref[here, :] = c_low
            scores = lax.dot_general(c_low, b_ref[here, :], (((1,), (1,)), ((), ())), preferred_element_type=F32)
            scores_ref[c] = jnp.where(keep, scores, 0.0)

    now = pl.ds(pl.multiple_of(step * LANES, LANES), LANES)
    columns = reach_ref[now, :]
    chosen = csel_ref[now, :]
    before = before_ref[:, now]
    fresh = fresh_ref[:, now].astype(BF16)
    kept = kept_ref[step]
    scores = scores_ref[step]
    b_turned = bt_ref[:, now]

    for h in range(heads):
        here = slice(h * LANES, (h + 1) * LANES)
        gaps = jnp.minimum(columns[:, h:h + 1] - before[h:h + 1, :], 80.0)
        weights = (jnp.exp2(gaps) * scores).astype(BF16)
        carried = chosen * columns[:, slot + h:slot + h + 1].astype(BF16)
        x_head = x_ref[now, here]
        state = state_ref[:, here]
        out = dot(jnp.concatenate([weights, carried], axis=1), jnp.concatenate([x_head, state.astype(BF16)], axis=0))
        out = out + skip_ref[h] * x_head.astype(F32)
        written = dot(b_turned * fresh[h:h + 1, :], x_head)
        state_ref[:, here] = state * kept[h:h + 1, :] + written
        z = 0.5 * z_ref[now, here].astype(F32)
        gate = z + z * jnp.tanh(z)
        part_ref[now, here] = out * gate
        gate_ref[now, here] = gate.astype(BF16)


def local_scan(head_size, doc_lengths, a_log, d_skip, dt_raw, b_sel, b_turned, c_rows, x_in, z_gate):
    heads, tokens = dt_raw.shape
    features = x_in.shape[1]
    chunks = tokens // LANES
    held = [pltpu.with_memory_space_constraint(v, pltpu.VMEM) for v in (dt_raw, c_rows, z_gate)]
    return pl.pallas_call(
        functools.partial(scan_kernel, head_size),
        grid_spec=pltpu.PrefetchScalarGridSpec(
            num_scalar_prefetch=3,
            grid=(chunks,),
            in_specs=[in_vmem()] * 6,
            out_specs=[in_vmem()] * 4,
            scratch_shapes=[
                pltpu.VMEM((LANES, features), F32),
                pltpu.VMEM((heads, tokens), F32),
                pltpu.VMEM((heads, tokens), F32),
                pltpu.VMEM((chunks, heads, LANES), F32),
                pltpu.VMEM((chunks, LANES, LANES), F32),
                pltpu.VMEM((chunks, LANES, LANES), F32),
            ],
        ),
        out_shape=[
            pltpu.VMEM((tokens, features), F32),
            pltpu.VMEM((tokens, features), BF16),
            pltpu.VMEM((tokens, LANES), BF16),
            pltpu.VMEM((tokens, LANES), F32),
        ],
        compiler_params=params(),
        cost_estimate=pl.CostEstimate(flops=16 * LANES * tokens * features, bytes_accessed=8 * tokens * features, transcendentals=0),
        name="local_scan",
    )(doc_lengths, a_log, d_skip, held[0], b_sel, b_turned, held[1], x_in, held[2])


def one_language(first, size, starts, lang_ref):
    lang = lang_at(first, starts, lang_ref)
    same = jnp.bool_(True)
    for d, s in enumerate(starts):
        inside = (s > first) & (s < first + size)
        same = same & jnp.logical_not(inside & (lang_ref[d] != lang))
    return lang, same


def other_language(lang, first, size, starts, langs):
    other = lang
    few = jnp.bool_(True)
    for d, s in enumerate(starts):
        inside = (s > first) & (s < first + size) & (langs[d] != lang)
        few = few & jnp.logical_not(inside & (other != lang) & (langs[d] != other))
        other = jnp.where(inside & (other == lang), langs[d], other)
    return other, few


def has_language(which, first, size, starts, lang_ref):
    found = lang_at(first, starts, lang_ref) == which
    for d, s in enumerate(starts):
        found = found | ((s > first) & (s < first + size) & (lang_ref[d] == which))
    return found


def sum_rows(tile):
    return -(-8 * (tile // LANES) // 16) * 16


def combine_kernel(n_states, slot, tile_tokens, offset, len_ref, lang_ref, c_ref, reach_ref, part_ref, gate_ref, gain_ref, down_ref, *rest):
    states, (all_gated_ref, other_ref, mine_ref, enter_ref, low_ref) = rest[:n_states], rest[n_states:]
    step = pl.program_id(0)
    tokens, features = tile_tokens, part_ref.shape[1]
    heads = features // LANES
    tile = (step + 1 + lax.axis_index("head")) % 2
    at = pl.multiple_of(offset + tile * tokens, LANES)
    now = pl.ds(at, tokens)
    gated_ref = all_gated_ref.at[pl.ds(pl.multiple_of(tile * tokens, LANES), tokens)]
    first = lax.axis_index("seq") * part_ref.shape[0] + at
    starts = starts_of(len_ref)
    langs = [lang_ref[d] for d in range(lang_ref.shape[0])]
    lang, same = one_language(first, tokens, starts, langs)

    if n_states > 1:
        @pl.when(step == 0)
        def _():
            total = states[0][...].astype(F32)
            for more in states[1:]:
                total = total + more[...].astype(F32)
            enter_ref[...] = total.astype(BF16)
        entering = enter_ref
    else:
        entering = states[0]

    squares = jnp.zeros((tokens, LANES), F32)
    low = jnp.zeros((tokens, LANES), F32)
    c_low = c_ref[now, :]
    reach = reach_ref[now, :]
    pair = min(2, heads)
    for p in range(heads // pair):
        wide = slice(p * pair * LANES, (p + 1) * pair * LANES)
        both = dot(c_low, entering[:, wide])
        scaled = []
        for i in range(pair):
            h = p * pair + i
            here = slice(h * LANES, (h + 1) * LANES)
            entered = both[:, i * LANES:(i + 1) * LANES] * reach[:, 2 * slot + h:2 * slot + h + 1]
            gated = part_ref[now, here] + entered * gate_ref[now, here].astype(F32)
            squares = squares + gated * gated
            scaled.append((gated * gain_ref[:, here]).astype(BF16))
            gated_ref[:, here] = scaled[-1]
        low = low + dot(jnp.concatenate(scaled, axis=1), down_ref[lang, wide, :])
    low_ref[...] = low

    @pl.when(jnp.logical_not(same))
    def _():
        token_lang = lang_at(first + lax.broadcasted_iota(I32, (tokens, LANES), 0), starts, langs)
        for k in range(down_ref.shape[0]):
            @pl.when(has_language(k, first, tokens, starts, langs) & (lang != k))
            def _():
                low_ref[...] = jnp.where(token_lang == k, dot(gated_ref[...], down_ref[k]), low_ref[...])

    ones = jnp.ones((8, LANES), F32)
    sums = lax.dot_general(ones, squares, (((1,), (1,)), ((), ())), precision=lax.Precision.HIGHEST, preferred_element_type=F32)
    rows = [sums[:, c * LANES:(c + 1) * LANES] for c in range(tokens // LANES)]
    rows = jnp.concatenate(rows + rows[:1] * (sum_rows(tokens) // 8 - len(rows)), axis=0)

    def message(ref):
        ref[0:tokens, :] = low_ref[...].astype(BF16)
        ref[tokens:tokens + sum_rows(tokens), :] = rows.astype(BF16)

    @pl.when(step == 0)
    def _():
        message(other_ref)

    @pl.when(step == 1)
    def _():
        message(mine_ref)


def combine(docs, c_sel, reach, part, gate, gain, down, states, offset, tile, slot):
    features = part.shape[1]
    held = [pltpu.with_memory_space_constraint(v, pltpu.VMEM) for v in [gain, down] + states]
    return pl.pallas_call(
        functools.partial(combine_kernel, len(states), slot, tile, offset),
        grid_spec=pltpu.PrefetchScalarGridSpec(
            num_scalar_prefetch=2,
            grid=(2,),
            in_specs=[in_vmem()] * (6 + len(states)),
            out_specs=[in_vmem()] * 3,
            scratch_shapes=[
                pltpu.VMEM(states[0].shape, BF16),
                pltpu.VMEM((tile, LANES), F32),
            ],
        ),
        out_shape=[
            pltpu.VMEM((2 * tile, features), BF16),
            pltpu.VMEM((tile + sum_rows(tile), LANES), BF16),
            pltpu.VMEM((tile + sum_rows(tile), LANES), BF16),
        ],
        compiler_params=params(),
        name="combine",
    )(*docs, c_sel, reach, part, gate, *held)


def finish_kernel(tile, offset, all_tokens, all_features, len_ref, lang_ref, mine_ref, other_ref, all_gated_ref, up_ref, *rest):
    out_ref = rest[-1]
    step = pl.program_id(0)
    tokens, features = out_ref.shape
    per = tile // tokens
    inside = pl.multiple_of((step % per) * tokens, LANES)
    gated_ref = all_gated_ref.at[pl.ds(pl.multiple_of(step * tokens, LANES), tokens)]
    ranks = up_ref.shape[1]
    first = lax.axis_index("seq") * all_tokens + offset + step * tokens
    starts = starts_of(len_ref)
    langs = [lang_ref[d] for d in range(lang_ref.shape[0])]
    is_mine = (step // per) == lax.axis_index("head") % 2
    low = jnp.where(is_mine, mine_ref[pl.ds(inside, tokens), :].astype(F32), other_ref[pl.ds(inside, tokens), :].astype(F32))
    sums = pl.ds(tile, sum_rows(tile))
    sums = jnp.where(is_mine, mine_ref[sums, :].astype(F32), other_ref[sums, :].astype(F32))
    scale = lax.rsqrt(sums / all_features + EPS)
    scale = jnp.concatenate([scale] * (LANES // sum_rows(tile)), axis=0).T
    columns = []
    for c in range(tokens // LANES):
        column = scale[:, 8 * c:8 * c + 1]
        for q in range(1, per):
            k = 8 * (c + q * (tokens // LANES))
            column = jnp.where(step % per == q, scale[:, k:k + 1], column)
        columns.append(column)
    scale = jnp.concatenate(columns, axis=0)
    low = (low * scale).astype(BF16)
    lang, _ = one_language(first, tokens, starts, langs)
    other, few = other_language(lang, first, tokens, starts, langs)
    token_lang = lang_at(first + lax.broadcasted_iota(I32, (tokens, LANES), 0), starts, langs)
    zero = jnp.zeros((), BF16)
    piece = min(4 * LANES, features)

    @pl.when(few)
    def _():
        spread = jnp.concatenate([
            jnp.where(token_lang == lang, low, zero),
            jnp.where(token_lang != lang, low, zero),
        ], axis=1)
        for at in range(0, features, piece):
            here = slice(at, at + piece)
            lifted = dot(spread, jnp.concatenate([up_ref[lang, :, here], up_ref[other, :, here]], axis=0))
            out_ref[:, here] = (gated_ref[:, here].astype(F32) * scale + lifted).astype(BF16)

    @pl.when(jnp.logical_not(few))
    def _():
        spread = jnp.concatenate([jnp.where(token_lang == k, low, zero) for k in range(up_ref.shape[0])], axis=1)
        for at in range(0, features, piece):
            here = slice(at, at + piece)
            lifted = dot(spread, up_ref[:, :, here].reshape(up_ref.shape[0] * ranks, piece))
            out_ref[:, here] = (gated_ref[:, here].astype(F32) * scale + lifted).astype(BF16)


def finish(docs, mine, other, gated, up, offset, all_tokens, all_features, into=None):
    features = gated.shape[1]
    tile = gated.shape[0] // 2
    rows = next(r for r in (2 * LANES, LANES) if tile % r == 0 and offset % r == 0)
    held = [pltpu.with_memory_space_constraint(v, pltpu.VMEM) for v in (mine, other, gated, up)]
    more = [] if into is None else [into]
    return pl.pallas_call(
        functools.partial(finish_kernel, tile, offset, all_tokens, all_features),
        grid_spec=pltpu.PrefetchScalarGridSpec(
            num_scalar_prefetch=2,
            grid=(2 * tile // rows,),
            in_specs=[in_vmem()] * 4 + [pl.BlockSpec(memory_space=pl.ANY) for _ in more],
            out_specs=pl.BlockSpec((rows, features), lambda s, *_: (offset // rows + s, 0)),
        ),
        out_shape=jax.ShapeDtypeStruct((all_tokens, features), BF16),
        input_output_aliases={6: 0} if more else {},
        compiler_params=params(),
        name="finish",
    )(*docs, *held, *more)


def sum_over_head(other, mine, devices, beside=None):
    def across(v, mask):
        return lax.ppermute(v, "head", [(i, i ^ mask) for i in range(devices)])

    more = () if beside is None else (beside,)
    if devices == 1:
        return (mine, other) + more
    total = (mine.astype(F32) + across(other, 1).astype(F32)).astype(BF16)
    bit = 2
    while bit < devices:
        masks = [bit] if 2 * bit >= devices else [bit, 2 * bit, 3 * bit]
        arrived = [across(total, m) for m in masks]
        if bit == 2 and more:
            arrived, more = lax.optimization_barrier((arrived, more))
        added = total.astype(F32)
        for a in arrived:
            added = added + a.astype(F32)
        total = added.astype(BF16)
        bit *= 2 ** (1 if len(masks) == 1 else 2)
    return (total, across(total, 1)) + more


def run(seq_size, head_size, relayed, x_in, z_gate, b_input, c_input, dt_raw, a_log, d_skip, norm_gain,
        doc_lengths, doc_lang, adapt_down, adapt_up):
    tokens, features = x_in.shape
    heads = dt_raw.shape[0]
    groups = b_input.shape[1]
    b_rows = b_input.reshape(tokens * groups, b_input.shape[2])
    c_rows = c_input.reshape(tokens * groups, c_input.shape[2])
    docs = (doc_lengths, doc_lang)
    gain = norm_gain.reshape(1, features)
    all_features = features * head_size
    slot = max(8, heads)
    onward = [(i, i + 1) for i in range(seq_size - 1)]

    state, through, b_sel, b_turned, x_held = block_states(head_size, doc_lengths, a_log, dt_raw, b_rows, x_in)
    state, z_gate, c_rows = lax.optimization_barrier((state, z_gate, c_rows))
    arrived = lax.ppermute(state, "seq", onward)
    part, gate, c_sel, reach = local_scan(head_size, doc_lengths, a_log, d_skip, dt_raw, b_sel, b_turned, c_rows, x_held, z_gate)
    arrived, part = lax.optimization_barrier((arrived, part))
    states = [arrived]
    for _ in range(1, hops_of(tokens, seq_size) if relayed else 1):
        arrived = lax.ppermute((arrived.astype(F32) * through[0:1]).astype(BF16), "seq", onward)
        states.append(arrived)

    head = tokens
    if relayed:
        reached = longest_of(tokens, seq_size) - 1 - (len(states) - 1) * tokens
        head = next((h for h in (tokens // 4, tokens // 2) if reached <= h), tokens)

    def joined(states, offset, tile):
        return combine(docs, c_sel, reach, part, gate, gain, adapt_down, states, offset, tile, slot)

    if head == tokens:
        gated, other, mine = joined(states, 0, tokens // 2)
        sums = sum_over_head(other, mine, head_size)
        return finish(docs, *sums, gated, adapt_up, 0, tokens, all_features)
    late, other, mine = joined(states[:-1], head, (tokens - head) // 2)
    late_sums = sum_over_head(other, mine, head_size)
    states[-1], late_sums = lax.optimization_barrier((states[-1], late_sums))
    early, other, mine = joined(states, 0, head // 2)
    out = finish(docs, *late_sums, late, adapt_up, head, tokens, all_features)
    *early_sums, out = sum_over_head(other, mine, head_size, out)
    return finish(docs, *early_sums, early, adapt_up, 0, tokens, all_features, out)


def longest_of(tokens, seq_size):
    return tokens * seq_size // LONGEST_SHARE


def hops_of(tokens, seq_size):
    return min(-(-(longest_of(tokens, seq_size) - 1) // tokens), seq_size - 1)


def covered_kernel(tokens, seq_size, len_ref, out_ref):
    found, at = jnp.int32(0), jnp.int32(0)
    for d in range(len_ref.shape[0]):
        end = at + len_ref[d]
        for block in range(1, seq_size - 1):
            found = jnp.where((at < block * tokens) & (end > (block + 1) * tokens), 1, found)
        at = end
    out_ref[0] = found


def per_device(seq_size, head_size, *args):
    tokens = args[0].shape[0]
    doc_lengths = args[8]
    if hops_of(tokens, seq_size) < 2:
        return run(seq_size, head_size, False, *args)
    covered = pl.pallas_call(
        functools.partial(covered_kernel, tokens, seq_size),
        in_specs=[pl.BlockSpec(memory_space=pltpu.SMEM)],
        out_specs=pl.BlockSpec(memory_space=pltpu.SMEM),
        out_shape=jax.ShapeDtypeStruct((1,), I32),
        name="covered",
    )(doc_lengths)[0] > 0
    return lax.cond(
        covered,
        functools.partial(run, seq_size, head_size, True),
        functools.partial(run, seq_size, head_size, False),
        *args,
    )


def solution(mesh):
    placed = (
        P("seq", "head"),
        P("seq", "head"),
        P("seq", None, None),
        P("seq", None, None),
        P("head", "seq"),
        P("head"),
        P("head"),
        P("head"),
        P(),
        P(),
        P(None, "head", None),
        P(None, None, "head"),
    )
    return jax.shard_map(
        functools.partial(per_device, mesh.shape["seq"], mesh.shape["head"]),
        mesh=mesh, in_specs=placed, out_specs=P("seq", "head"), check_vma=False,
    )
```

```python
import functools

import jax
import jax.numpy as jnp
from jax import lax
from jax.experimental import pallas as pl
from jax.experimental.pallas import tpu as pltpu
from jax.sharding import PartitionSpec as P

F32 = jnp.float32
BF16 = jnp.bfloat16
I32 = jnp.int32
LOG2E = 1.4426950408889634
EPS = 1e-05
LANES = 128
LONGEST_SHARE = 3
VMEM_LIMIT = 16 * 1024 * 1024


def params():
    return pltpu.CompilerParams(vmem_limit_bytes=VMEM_LIMIT)


def starts_of(len_ref):
    starts, at = [], jnp.int32(0)
    for d in range(len_ref.shape[0]):
        starts.append(at)
        at = at + len_ref[d]
    return starts


def doc_at(pos, starts):
    found = jnp.where(pos >= starts[0], 0, -1)
    for s in starts[1:]:
        found = found + jnp.where(pos >= s, 1, 0)
    return found


def lang_at(pos, starts, lang_ref):
    found = jnp.where(pos >= 0, lang_ref[0], 0)
    for d in range(1, len(starts)):
        found = jnp.where(pos >= starts[d], lang_ref[d], found)
    return found


def rates(alog_ref, rows):
    which = lax.broadcasted_iota(I32, (rows, LANES), 0)
    column = jnp.zeros((rows, LANES), F32)
    for h in range(rows):
        column = jnp.where(which == h, alog_ref[h], column)
    return -LOG2E * jnp.exp(column)


def softplus(v):
    return jnp.maximum(v, 0.0) + jnp.log(1.0 + jnp.exp(-jnp.abs(v)))


def running(v, back):
    width = v.shape[1]
    lane = lax.broadcasted_iota(I32, v.shape, 1)
    step = 1
    while step < width:
        if back:
            v = v + jnp.where(lane + step < width, pltpu.roll(v, width - step, 1), 0.0)
        else:
            v = v + jnp.where(lane >= step, pltpu.roll(v, step, 1), 0.0)
        step *= 2
    return v


def pick_matrix(group, groups):
    shape = (LANES, LANES * groups)
    row = lax.broadcasted_iota(I32, shape, 0)
    col = lax.broadcasted_iota(I32, shape, 1)
    return jnp.where(col == row * groups + group, 1.0, 0.0).astype(BF16)


def dot(a, b):
    return jnp.dot(a, b, preferred_element_type=F32)


def group_of(head_rank, heads, head_size, groups):
    return head_rank * heads // (heads * head_size // groups)


def state_kernel(head_size, len_hbm, alog_hbm, dt_hbm, b_hbm, x_hbm, state_ref, thr_ref, bsel_ref, bt_ref, x_ref,
                 reach_ref, before_ref, fresh_ref, kept_ref, len_ref, alog_ref, dt_ref, b_ref, w_ref, all_ref, stack_ref, sems):
    heads, tokens = dt_ref.shape
    groups = b_ref.shape[0] // tokens
    copies = [
        pltpu.make_async_copy(source, target, sems.at[i])
        for i, (source, target) in enumerate([
            (dt_hbm, dt_ref), (len_hbm, len_ref), (alog_hbm, alog_ref), (b_hbm, b_ref), (x_hbm, x_ref),
        ])
    ]
    for copy in copies:
        copy.start()
    for copy in copies[:3]:
        copy.wait()

    starts = starts_of(len_ref)
    base = lax.axis_index("seq") * tokens
    rate = rates(alog_ref, heads)
    parts, totals = [], []
    for c in range(tokens // LANES):
        step_dt = softplus(dt_ref[:, c * LANES:(c + 1) * LANES])
        decay = step_dt * rate
        after = running(decay, True)
        parts.append((step_dt, after - decay))
        totals.append(after[:, 0:1])
    last_doc = doc_at(base + tokens - 1, starts)
    first_doc = doc_at(base - 1, starts)
    later = jnp.zeros((heads, 1), F32)
    for c in reversed(range(tokens // LANES)):
        step_dt, inside = parts[c]
        pos = base + c * LANES + lax.broadcasted_iota(I32, (heads, LANES), 1)
        alive = doc_at(pos, starts) == last_doc
        w_ref[:, c * LANES:(c + 1) * LANES] = jnp.where(alive, jnp.exp2(inside + later) * step_dt, 0.0)
        later = later + totals[c]
    kept = jnp.where(last_doc == first_doc, 1.0, 0.0)
    all_ref[...] = jnp.broadcast_to(jnp.exp2(later) * kept, all_ref.shape)
    for h in range(heads):
        thr_ref[:, h * LANES:(h + 1) * LANES] = jnp.broadcast_to(all_ref[h:h + 1, :], (8, LANES))

    slot = max(8, heads)
    stack_ref[...] = jnp.zeros_like(stack_ref)
    past = jnp.zeros((heads, LANES), F32)
    for c in range(tokens // LANES):
        here = slice(c * LANES, (c + 1) * LANES)
        first = base + c * LANES
        step_dt = parts[c][0]
        total_to = running(step_dt * rate, False)
        chunk_total = jnp.broadcast_to(total_to[:, LANES - 1:LANES], (heads, LANES))
        before_ref[:, here] = total_to - jnp.log(step_dt) * LOG2E
        doc = doc_at(first + lax.broadcasted_iota(I32, (heads, LANES), 1), starts)
        doc_in = doc_at(first - 1, starts)
        doc_out = doc_at(first + LANES - 1, starts)
        fresh_ref[:, here] = jnp.where(doc == doc_out, jnp.exp2(chunk_total - total_to) * step_dt, 0.0)
        kept_ref[c] = jnp.exp2(chunk_total) * jnp.where(doc_in == doc_out, 1.0, 0.0)
        stack_ref[c, 0:heads, :] = total_to
        stack_ref[c, slot:slot + heads, :] = jnp.where(doc == doc_in, jnp.exp2(total_to), 0.0)
        stack_ref[c, 2 * slot:2 * slot + heads, :] = jnp.where(doc == first_doc, jnp.exp2(past + total_to), 0.0)
        past = past + chunk_total
        reach_ref[here, :] = stack_ref[c].T

    pick = pick_matrix(group_of(lax.axis_index("head"), heads, head_size, groups), groups)
    copies[3].wait()
    for c in range(tokens // LANES):
        here = slice(c * LANES, (c + 1) * LANES)
        chosen = dot(pick, b_ref[c * LANES * groups:(c + 1) * LANES * groups, :])
        bsel_ref[here, :] = chosen.astype(BF16)
        bt_ref[:, here] = chosen.T.astype(BF16)

    copies[4].wait()
    for h in range(heads):
        here = slice(h * LANES, (h + 1) * LANES)
        weighted = bt_ref[...] * w_ref[h:h + 1, :].astype(BF16)
        state_ref[:, here] = dot(weighted, x_ref[:, here]).astype(BF16)


def in_vmem():
    return pl.BlockSpec(memory_space=pltpu.VMEM)


def block_states(head_size, doc_lengths, a_log, dt_raw, b_rows, x_in):
    heads, tokens = dt_raw.shape
    features = x_in.shape[1]
    return pl.pallas_call(
        functools.partial(state_kernel, head_size),
        grid_spec=pltpu.PrefetchScalarGridSpec(
            num_scalar_prefetch=0,
            grid=(1,),
            in_specs=[pl.BlockSpec(memory_space=pl.ANY)] * 5,
            out_specs=[in_vmem()] * 9,
            scratch_shapes=[
                pltpu.SMEM(doc_lengths.shape, I32),
                pltpu.SMEM(a_log.shape, F32),
                pltpu.VMEM((heads, tokens), F32),
                pltpu.VMEM(b_rows.shape, BF16),
                pltpu.VMEM((heads, tokens), F32),
                pltpu.VMEM((heads, LANES), F32),
                pltpu.VMEM((tokens // LANES, LANES, LANES), F32),
                pltpu.SemaphoreType.DMA((5,)),
            ],
        ),
        out_shape=[
            pltpu.VMEM((LANES, features), BF16),
            pltpu.VMEM((8, features), F32),
            pltpu.VMEM((tokens, LANES), BF16),
            pltpu.VMEM((LANES, tokens), BF16),
            pltpu.VMEM((tokens, features), BF16),
            pltpu.VMEM((tokens, LANES), F32),
            pltpu.VMEM((heads, tokens), F32),
            pltpu.VMEM((heads, tokens), F32),
            pltpu.VMEM((tokens // LANES, heads, LANES), F32),
        ],
        compiler_params=params(),
        cost_estimate=pl.CostEstimate(flops=2 * LANES * tokens * features, bytes_accessed=8 * tokens * features, transcendentals=0),
        name="block_states",
    )(*[pltpu.with_memory_space_constraint(v, pltpu.HBM) for v in (doc_lengths, a_log, dt_raw, b_rows, x_in)])


def scan_kernel(head_size, len_ref, skip_ref, b_ref, bt_ref, reach_ref, before_ref, fresh_ref, kept_ref, c_ref, x_ref, z_ref,
                part_ref, gate_ref, csel_ref, state_ref, scores_ref):
    step = pl.program_id(0)
    heads, tokens = before_ref.shape
    groups = c_ref.shape[0] // tokens
    slot = max(8, heads)

    @pl.when(step == 0)
    def _():
        state_ref[...] = jnp.zeros_like(state_ref)
        starts = starts_of(len_ref)
        block = lax.axis_index("seq") * tokens
        pick = pick_matrix(group_of(lax.axis_index("head"), heads, head_size, groups), groups)
        for c in range(tokens // LANES):
            here = slice(c * LANES, (c + 1) * LANES)
            base = block + c * LANES
            row_pos = base + lax.broadcasted_iota(I32, (LANES, LANES), 0)
            col_pos = base + lax.broadcasted_iota(I32, (LANES, LANES), 1)
            keep = (row_pos >= col_pos) & (doc_at(row_pos, starts) == doc_at(col_pos, starts))
            c_low = dot(pick, c_ref[c * LANES * groups:(c + 1) * LANES * groups, :]).astype(BF16)
            csel_ref[here, :] = c_low
            scores = lax.dot_general(c_low, b_ref[here, :], (((1,), (1,)), ((), ())), preferred_element_type=F32)
            scores_ref[c] = jnp.where(keep, scores, 0.0)

    now = pl.ds(pl.multiple_of(step * LANES, LANES), LANES)
    columns = reach_ref[now, :]
    chosen = csel_ref[now, :]
    before = before_ref[:, now]
    fresh = fresh_ref[:, now].astype(BF16)
    kept = kept_ref[step]
    scores = scores_ref[step]
    b_turned = bt_ref[:, now]

    for h in range(heads):
        here = slice(h * LANES, (h + 1) * LANES)
        gaps = jnp.minimum(columns[:, h:h + 1] - before[h:h + 1, :], 80.0)
        weights = (jnp.exp2(gaps) * scores).astype(BF16)
        carried = chosen * columns[:, slot + h:slot + h + 1].astype(BF16)
        x_head = x_ref[now, here]
        state = state_ref[:, here]
        out = dot(jnp.concatenate([weights, carried], axis=1), jnp.concatenate([x_head, state.astype(BF16)], axis=0))
        out = out + skip_ref[h] * x_head.astype(F32)
        written = dot(b_turned * fresh[h:h + 1, :], x_head)
        state_ref[:, here] = state * kept[h:h + 1, :] + written
        z = 0.5 * z_ref[now, here].astype(F32)
        gate = z + z * jnp.tanh(z)
        part_ref[now, here] = out * gate
        gate_ref[now, here] = gate.astype(BF16)


def local_scan(head_size, doc_lengths, d_skip, b_sel, b_turned, decays, c_rows, x_in, z_gate):
    tokens, features = x_in.shape
    chunks = tokens // LANES
    held = [pltpu.with_memory_space_constraint(v, pltpu.VMEM) for v in (c_rows, z_gate)]
    return pl.pallas_call(
        functools.partial(scan_kernel, head_size),
        grid_spec=pltpu.PrefetchScalarGridSpec(
            num_scalar_prefetch=2,
            grid=(chunks,),
            in_specs=[in_vmem()] * 9,
            out_specs=[in_vmem()] * 3,
            scratch_shapes=[
                pltpu.VMEM((LANES, features), F32),
                pltpu.VMEM((chunks, LANES, LANES), F32),
            ],
        ),
        out_shape=[
            pltpu.VMEM((tokens, features), F32),
            pltpu.VMEM((tokens, features), BF16),
            pltpu.VMEM((tokens, LANES), BF16),
        ],
        compiler_params=params(),
        cost_estimate=pl.CostEstimate(flops=16 * LANES * tokens * features, bytes_accessed=8 * tokens * features, transcendentals=0),
        name="local_scan",
    )(doc_lengths, d_skip, b_sel, b_turned, *decays, held[0], x_in, held[1])


def other_language(lang, first, size, starts, langs):
    other = lang
    few = jnp.bool_(True)
    for d, s in enumerate(starts):
        inside = (s > first) & (s < first + size) & (langs[d] != lang)
        few = few & jnp.logical_not(inside & (other != lang) & (langs[d] != other))
        other = jnp.where(inside & (other == lang), langs[d], other)
    return other, few


def has_language(which, first, size, starts, lang_ref):
    found = lang_at(first, starts, lang_ref) == which
    for d, s in enumerate(starts):
        found = found | ((s > first) & (s < first + size) & (lang_ref[d] == which))
    return found


def sum_rows(tile):
    return -(-8 * (tile // LANES) // 16) * 16


def combine_kernel(n_states, slot, tile_tokens, offset, len_ref, lang_ref, c_ref, reach_ref, part_ref, gate_ref, gain_ref, down_ref, *rest):
    states, (all_gated_ref, other_ref, mine_ref, enter_ref, low_ref) = rest[:n_states], rest[n_states:]
    step = pl.program_id(0)
    tokens, features = tile_tokens, part_ref.shape[1]
    heads = features // LANES
    tile = (step + 1 + lax.axis_index("head")) % 2
    at = pl.multiple_of(offset + tile * tokens, LANES)
    now = pl.ds(at, tokens)
    gated_ref = all_gated_ref.at[pl.ds(pl.multiple_of(tile * tokens, LANES), tokens)]
    first = lax.axis_index("seq") * part_ref.shape[0] + at
    starts = starts_of(len_ref)
    langs = [lang_ref[d] for d in range(lang_ref.shape[0])]
    lang = lang_at(first, starts, langs)
    other, few = other_language(lang, first, tokens, starts, langs)

    if n_states > 1:
        @pl.when(step == 0)
        def _():
            total = states[0][...].astype(F32)
            for more in states[1:]:
                total = total + more[...].astype(F32)
            enter_ref[...] = total.astype(BF16)
        entering = enter_ref
    else:
        entering = states[0]

    squares = jnp.zeros((tokens, LANES), F32)
    c_low = c_ref[now, :]
    reach = reach_ref[now, :]
    pair = min(2, heads)
    for p in range(heads // pair):
        wide = slice(p * pair * LANES, (p + 1) * pair * LANES)
        both = dot(c_low, entering[:, wide])
        for i in range(pair):
            h = p * pair + i
            here = slice(h * LANES, (h + 1) * LANES)
            entered = both[:, i * LANES:(i + 1) * LANES] * reach[:, 2 * slot + h:2 * slot + h + 1]
            gated = part_ref[now, here] + entered * gate_ref[now, here].astype(F32)
            squares = squares + gated * gated
            gated_ref[:, here] = (gated * gain_ref[:, here]).astype(BF16)
    token_lang = lang_at(first + lax.broadcasted_iota(I32, (tokens, LANES), 0), starts, langs)
    both = dot(gated_ref[...], jnp.concatenate([down_ref[lang], down_ref[other]], axis=1))
    low_ref[...] = jnp.where(token_lang == lang, both[:, :LANES], both[:, LANES:])

    @pl.when(jnp.logical_not(few))
    def _():
        for k in range(down_ref.shape[0]):
            @pl.when(has_language(k, first, tokens, starts, langs) & (lang != k) & (other != k))
            def _():
                low_ref[...] = jnp.where(token_lang == k, dot(gated_ref[...], down_ref[k]), low_ref[...])

    ones = jnp.ones((8, LANES), BF16)
    whole = squares.astype(BF16)
    rest_of = (squares - whole.astype(F32)).astype(BF16)
    turned = (((1,), (1,)), ((), ()))
    sums = lax.dot_general(ones, whole, turned, preferred_element_type=F32) + lax.dot_general(ones, rest_of, turned, preferred_element_type=F32)
    rows = [sums[:, c * LANES:(c + 1) * LANES] for c in range(tokens // LANES)]
    rows = jnp.concatenate(rows + rows[:1] * (sum_rows(tokens) // 8 - len(rows)), axis=0)

    def message(ref):
        ref[0:tokens, :] = low_ref[...].astype(BF16)
        ref[tokens:tokens + sum_rows(tokens), :] = rows.astype(BF16)

    @pl.when(step == 0)
    def _():
        message(other_ref)

    @pl.when(step == 1)
    def _():
        message(mine_ref)


def combine(docs, c_sel, reach, part, gate, gain, down, states, offset, tile, slot):
    features = part.shape[1]
    held = [pltpu.with_memory_space_constraint(v, pltpu.VMEM) for v in [gain, down] + states]
    return pl.pallas_call(
        functools.partial(combine_kernel, len(states), slot, tile, offset),
        grid_spec=pltpu.PrefetchScalarGridSpec(
            num_scalar_prefetch=2,
            grid=(2,),
            in_specs=[in_vmem()] * (6 + len(states)),
            out_specs=[in_vmem()] * 3,
            scratch_shapes=[
                pltpu.VMEM(states[0].shape, BF16),
                pltpu.VMEM((tile, LANES), F32),
            ],
        ),
        out_shape=[
            pltpu.VMEM((2 * tile, features), BF16),
            pltpu.VMEM((tile + sum_rows(tile), LANES), BF16),
            pltpu.VMEM((tile + sum_rows(tile), LANES), BF16),
        ],
        compiler_params=params(),
        name="combine",
    )(*docs, c_sel, reach, part, gate, *held)


def finish_kernel(tile, offset, all_tokens, all_features, len_ref, lang_ref, mine_ref, other_ref, all_gated_ref, up_ref, *rest):
    out_ref = rest[-1]
    step = pl.program_id(0)
    tokens, features = out_ref.shape
    per = tile // tokens
    inside = pl.multiple_of((step % per) * tokens, LANES)
    gated_ref = all_gated_ref.at[pl.ds(pl.multiple_of(step * tokens, LANES), tokens)]
    ranks = up_ref.shape[1]
    first = lax.axis_index("seq") * all_tokens + offset + step * tokens
    starts = starts_of(len_ref)
    langs = [lang_ref[d] for d in range(lang_ref.shape[0])]
    is_mine = (step // per) == lax.axis_index("head") % 2
    low = jnp.where(is_mine, mine_ref[pl.ds(inside, tokens), :].astype(F32), other_ref[pl.ds(inside, tokens), :].astype(F32))
    sums = pl.ds(tile, sum_rows(tile))
    sums = jnp.where(is_mine, mine_ref[sums, :].astype(F32), other_ref[sums, :].astype(F32))
    scale = lax.rsqrt(sums / all_features + EPS)
    scale = jnp.concatenate([scale] * (LANES // sum_rows(tile)), axis=0).T
    columns = []
    for c in range(tokens // LANES):
        column = scale[:, 8 * c:8 * c + 1]
        for q in range(1, per):
            k = 8 * (c + q * (tokens // LANES))
            column = jnp.where(step % per == q, scale[:, k:k + 1], column)
        columns.append(column)
    scale = jnp.concatenate(columns, axis=0)
    low = (low * scale).astype(BF16)
    lang = lang_at(first, starts, langs)
    other, few = other_language(lang, first, tokens, starts, langs)
    token_lang = lang_at(first + lax.broadcasted_iota(I32, (tokens, LANES), 0), starts, langs)
    zero = jnp.zeros((), BF16)
    piece = min(4 * LANES, features)

    @pl.when(few)
    def _():
        spread = jnp.concatenate([
            jnp.where(token_lang == lang, low, zero),
            jnp.where(token_lang != lang, low, zero),
        ], axis=1)
        for at in range(0, features, piece):
            here = slice(at, at + piece)
            lifted = dot(spread, jnp.concatenate([up_ref[lang, :, here], up_ref[other, :, here]], axis=0))
            out_ref[:, here] = (gated_ref[:, here].astype(F32) * scale + lifted).astype(BF16)

    @pl.when(jnp.logical_not(few))
    def _():
        spread = jnp.concatenate([jnp.where(token_lang == k, low, zero) for k in range(up_ref.shape[0])], axis=1)
        for at in range(0, features, piece):
            here = slice(at, at + piece)
            lifted = dot(spread, up_ref[:, :, here].reshape(up_ref.shape[0] * ranks, piece))
            out_ref[:, here] = (gated_ref[:, here].astype(F32) * scale + lifted).astype(BF16)


def finish(docs, mine, other, gated, up, offset, all_tokens, all_features, into=None):
    features = gated.shape[1]
    tile = gated.shape[0] // 2
    rows = next(r for r in (4 * LANES, 2 * LANES, LANES) if tile % r == 0 and offset % r == 0)
    held = [pltpu.with_memory_space_constraint(v, pltpu.VMEM) for v in (mine, other, gated, up)]
    more = [] if into is None else [into]
    return pl.pallas_call(
        functools.partial(finish_kernel, tile, offset, all_tokens, all_features),
        grid_spec=pltpu.PrefetchScalarGridSpec(
            num_scalar_prefetch=2,
            grid=(2 * tile // rows,),
            in_specs=[in_vmem()] * 4 + [pl.BlockSpec(memory_space=pl.ANY) for _ in more],
            out_specs=pl.BlockSpec((rows, features), lambda s, *_: (offset // rows + s, 0)),
        ),
        out_shape=jax.ShapeDtypeStruct((all_tokens, features), BF16),
        input_output_aliases={6: 0} if more else {},
        compiler_params=params(),
        name="finish",
    )(*docs, *held, *more)


def sum_over_head(other, mine, devices, beside=None):
    def across(v, mask):
        return lax.ppermute(v, "head", [(i, i ^ mask) for i in range(devices)])

    more = () if beside is None else (beside,)
    if devices == 1:
        return (mine, other) + more
    total = (mine.astype(F32) + across(other, 1).astype(F32)).astype(BF16)
    bit = 2
    while bit < devices:
        masks = [bit] if 2 * bit >= devices else [3 * bit, bit, 2 * bit]
        arrived = [across(total, m) for m in masks]
        if bit == 2 and more:
            arrived, more = lax.optimization_barrier((arrived, more))
        added = total.astype(F32)
        for a in arrived:
            added = added + a.astype(F32)
        total = added.astype(BF16)
        bit *= 2 ** (1 if len(masks) == 1 else 2)
    return (total, across(total, 1)) + more


def run(seq_size, head_size, relayed, x_in, z_gate, b_input, c_input, dt_raw, a_log, d_skip, norm_gain,
        doc_lengths, doc_lang, adapt_down, adapt_up):
    tokens, features = x_in.shape
    heads = dt_raw.shape[0]
    groups = b_input.shape[1]
    b_rows = b_input.reshape(tokens * groups, b_input.shape[2])
    c_rows = c_input.reshape(tokens * groups, c_input.shape[2])
    docs = (doc_lengths, doc_lang)
    gain = norm_gain.reshape(1, features)
    all_features = features * head_size
    slot = max(8, heads)
    onward = [(i, i + 1) for i in range(seq_size - 1)]

    state, through, b_sel, b_turned, x_held, *decays = block_states(head_size, doc_lengths, a_log, dt_raw, b_rows, x_in)
    state, z_gate, c_rows = lax.optimization_barrier((state, z_gate, c_rows))
    arrived = lax.ppermute(state, "seq", onward)
    part, gate, c_sel = local_scan(head_size, doc_lengths, d_skip, b_sel, b_turned, decays, c_rows, x_held, z_gate)
    reach = decays[0]
    arrived, part = lax.optimization_barrier((arrived, part))
    states = [arrived]
    for _ in range(1, hops_of(tokens, seq_size) if relayed else 1):
        arrived = lax.ppermute((arrived.astype(F32) * through[0:1]).astype(BF16), "seq", onward)
        states.append(arrived)

    head = tokens
    if relayed:
        reached = longest_of(tokens, seq_size) - 1 - (len(states) - 1) * tokens
        head = next((h for h in (tokens // 4, tokens // 2) if reached <= h), tokens)

    def joined(states, offset, tile):
        return combine(docs, c_sel, reach, part, gate, gain, adapt_down, states, offset, tile, slot)

    if head == tokens:
        gated, other, mine = joined(states, 0, tokens // 2)
        sums = sum_over_head(other, mine, head_size)
        return finish(docs, *sums, gated, adapt_up, 0, tokens, all_features)
    late, other, mine = joined(states[:-1], head, (tokens - head) // 2)
    late_sums = sum_over_head(other, mine, head_size)
    states[-1], late_sums = lax.optimization_barrier((states[-1], late_sums))
    early, other, mine = joined(states, 0, head // 2)
    out = finish(docs, *late_sums, late, adapt_up, head, tokens, all_features)
    *early_sums, out = sum_over_head(other, mine, head_size, out)
    return finish(docs, *early_sums, early, adapt_up, 0, tokens, all_features, out)


def longest_of(tokens, seq_size):
    return tokens * seq_size // LONGEST_SHARE


def hops_of(tokens, seq_size):
    return min(-(-(longest_of(tokens, seq_size) - 1) // tokens), seq_size - 1)


def covered_kernel(tokens, seq_size, len_ref, out_ref):
    found, at = jnp.int32(0), jnp.int32(0)
    for d in range(len_ref.shape[0]):
        end = at + len_ref[d]
        for block in range(1, seq_size - 1):
            found = jnp.where((at < block * tokens) & (end > (block + 1) * tokens), 1, found)
        at = end
    out_ref[0] = found


def per_device(seq_size, head_size, *args):
    tokens = args[0].shape[0]
    doc_lengths = args[8]
    if hops_of(tokens, seq_size) < 2:
        return run(seq_size, head_size, False, *args)
    covered = pl.pallas_call(
        functools.partial(covered_kernel, tokens, seq_size),
        in_specs=[pl.BlockSpec(memory_space=pltpu.SMEM)],
        out_specs=pl.BlockSpec(memory_space=pltpu.SMEM),
        out_shape=jax.ShapeDtypeStruct((1,), I32),
        name="covered",
    )(doc_lengths)[0] > 0
    return lax.cond(
        covered,
        functools.partial(run, seq_size, head_size, True),
        functools.partial(run, seq_size, head_size, False),
        *args,
    )


def solution(mesh):
    placed = (
        P("seq", "head"),
        P("seq", "head"),
        P("seq", None, None),
        P("seq", None, None),
        P("head", "seq"),
        P("head"),
        P("head"),
        P("head"),
        P(),
        P(),
        P(None, "head", None),
        P(None, None, "head"),
    )
    return jax.shard_map(
        functools.partial(per_device, mesh.shape["seq"], mesh.shape["head"]),
        mesh=mesh, in_specs=placed, out_specs=P("seq", "head"), check_vma=False,
    )
```

```python
import functools

import jax
import jax.numpy as jnp
from jax import lax
from jax.experimental import pallas as pl
from jax.experimental.pallas import tpu as pltpu
from jax.sharding import PartitionSpec as P

F32 = jnp.float32
BF16 = jnp.bfloat16
I32 = jnp.int32
LOG2E = 1.4426950408889634
EPS = 1e-05
LANES = 128
LONGEST_SHARE = 3
VMEM_LIMIT = 16 * 1024 * 1024


def params():
    return pltpu.CompilerParams(vmem_limit_bytes=VMEM_LIMIT)


def starts_of(len_ref):
    starts, at = [], jnp.int32(0)
    for d in range(len_ref.shape[0]):
        starts.append(at)
        at = at + len_ref[d]
    return starts


def doc_at(pos, starts):
    found = jnp.where(pos >= starts[0], 0, -1)
    for s in starts[1:]:
        found = found + jnp.where(pos >= s, 1, 0)
    return found


def lang_at(pos, starts, lang_ref):
    found = jnp.where(pos >= 0, lang_ref[0], 0)
    for d in range(1, len(starts)):
        found = jnp.where(pos >= starts[d], lang_ref[d], found)
    return found


def rates(alog_ref, rows):
    which = lax.broadcasted_iota(I32, (rows, LANES), 0)
    column = jnp.zeros((rows, LANES), F32)
    for h in range(rows):
        column = jnp.where(which == h, alog_ref[h], column)
    return -LOG2E * jnp.exp(column)


def softplus(v):
    return jnp.maximum(v, 0.0) + jnp.log(1.0 + jnp.exp(-jnp.abs(v)))


def running(v, back):
    width = v.shape[1]
    lane = lax.broadcasted_iota(I32, v.shape, 1)
    step = 1
    while step < width:
        if back:
            v = v + jnp.where(lane + step < width, pltpu.roll(v, width - step, 1), 0.0)
        else:
            v = v + jnp.where(lane >= step, pltpu.roll(v, step, 1), 0.0)
        step *= 2
    return v


def pick_matrix(group, groups):
    shape = (LANES, LANES * groups)
    row = lax.broadcasted_iota(I32, shape, 0)
    col = lax.broadcasted_iota(I32, shape, 1)
    return jnp.where(col == row * groups + group, 1.0, 0.0).astype(BF16)


def dot(a, b):
    return jnp.dot(a, b, preferred_element_type=F32)


def group_of(head_rank, heads, head_size, groups):
    return head_rank * heads // (heads * head_size // groups)


def state_kernel(head_size, len_hbm, alog_hbm, dt_hbm, b_hbm, x_hbm, state_ref, thr_ref, bsel_ref, bt_ref, x_ref,
                 reach_ref, before_ref, fresh_ref, kept_ref, len_ref, alog_ref, dt_ref, b_ref, w_ref, all_ref, stack_ref, sems):
    heads, tokens = dt_ref.shape
    groups = b_ref.shape[0] // tokens
    copies = [
        pltpu.make_async_copy(source, target, sems.at[i])
        for i, (source, target) in enumerate([
            (dt_hbm, dt_ref), (len_hbm, len_ref), (alog_hbm, alog_ref), (b_hbm, b_ref), (x_hbm, x_ref),
        ])
    ]
    for copy in copies:
        copy.start()
    for copy in copies[:3]:
        copy.wait()

    starts = starts_of(len_ref)
    base = lax.axis_index("seq") * tokens
    rate = rates(alog_ref, heads)
    parts, totals = [], []
    for c in range(tokens // LANES):
        step_dt = softplus(dt_ref[:, c * LANES:(c + 1) * LANES])
        decay = step_dt * rate
        after = running(decay, True)
        parts.append((step_dt, after - decay))
        totals.append(after[:, 0:1])
    last_doc = doc_at(base + tokens - 1, starts)
    first_doc = doc_at(base - 1, starts)
    later = jnp.zeros((heads, 1), F32)
    for c in reversed(range(tokens // LANES)):
        step_dt, inside = parts[c]
        pos = base + c * LANES + lax.broadcasted_iota(I32, (heads, LANES), 1)
        alive = doc_at(pos, starts) == last_doc
        w_ref[:, c * LANES:(c + 1) * LANES] = jnp.where(alive, jnp.exp2(inside + later) * step_dt, 0.0)
        later = later + totals[c]
    kept = jnp.where(last_doc == first_doc, 1.0, 0.0)
    all_ref[...] = jnp.broadcast_to(jnp.exp2(later) * kept, all_ref.shape)
    for h in range(heads):
        thr_ref[:, h * LANES:(h + 1) * LANES] = jnp.broadcast_to(all_ref[h:h + 1, :], (8, LANES))

    slot = max(8, heads)
    stack_ref[...] = jnp.zeros_like(stack_ref)
    past = jnp.zeros((heads, LANES), F32)
    for c in range(tokens // LANES):
        here = slice(c * LANES, (c + 1) * LANES)
        first = base + c * LANES
        step_dt = parts[c][0]
        total_to = running(step_dt * rate, False)
        chunk_total = jnp.broadcast_to(total_to[:, LANES - 1:LANES], (heads, LANES))
        before_ref[:, here] = total_to - jnp.log(step_dt) * LOG2E
        doc = doc_at(first + lax.broadcasted_iota(I32, (heads, LANES), 1), starts)
        doc_in = doc_at(first - 1, starts)
        doc_out = doc_at(first + LANES - 1, starts)
        fresh_ref[:, here] = jnp.where(doc == doc_out, jnp.exp2(chunk_total - total_to) * step_dt, 0.0)
        kept_ref[c] = jnp.exp2(chunk_total) * jnp.where(doc_in == doc_out, 1.0, 0.0)
        stack_ref[c, 0:heads, :] = total_to
        stack_ref[c, slot:slot + heads, :] = jnp.where(doc == doc_in, jnp.exp2(total_to), 0.0)
        stack_ref[c, 2 * slot:2 * slot + heads, :] = jnp.where(doc == first_doc, jnp.exp2(past + total_to), 0.0)
        past = past + chunk_total
        reach_ref[here, :] = stack_ref[c].T

    pick = pick_matrix(group_of(lax.axis_index("head"), heads, head_size, groups), groups)
    copies[3].wait()
    for c in range(tokens // LANES):
        here = slice(c * LANES, (c + 1) * LANES)
        chosen = dot(pick, b_ref[c * LANES * groups:(c + 1) * LANES * groups, :])
        bsel_ref[here, :] = chosen.astype(BF16)
        bt_ref[:, here] = chosen.T.astype(BF16)

    copies[4].wait()
    for h in range(heads):
        here = slice(h * LANES, (h + 1) * LANES)
        weighted = bt_ref[...] * w_ref[h:h + 1, :].astype(BF16)
        state_ref[:, here] = dot(weighted, x_ref[:, here]).astype(BF16)


def in_vmem():
    return pl.BlockSpec(memory_space=pltpu.VMEM)


def block_states(head_size, doc_lengths, a_log, dt_raw, b_rows, x_in):
    heads, tokens = dt_raw.shape
    features = x_in.shape[1]
    return pl.pallas_call(
        functools.partial(state_kernel, head_size),
        grid_spec=pltpu.PrefetchScalarGridSpec(
            num_scalar_prefetch=0,
            grid=(1,),
            in_specs=[pl.BlockSpec(memory_space=pl.ANY)] * 5,
            out_specs=[in_vmem()] * 9,
            scratch_shapes=[
                pltpu.SMEM(doc_lengths.shape, I32),
                pltpu.SMEM(a_log.shape, F32),
                pltpu.VMEM((heads, tokens), F32),
                pltpu.VMEM(b_rows.shape, BF16),
                pltpu.VMEM((heads, tokens), F32),
                pltpu.VMEM((heads, LANES), F32),
                pltpu.VMEM((tokens // LANES, LANES, LANES), F32),
                pltpu.SemaphoreType.DMA((5,)),
            ],
        ),
        out_shape=[
            pltpu.VMEM((LANES, features), BF16),
            pltpu.VMEM((8, features), F32),
            pltpu.VMEM((tokens, LANES), BF16),
            pltpu.VMEM((LANES, tokens), BF16),
            pltpu.VMEM((tokens, features), BF16),
            pltpu.VMEM((tokens, LANES), F32),
            pltpu.VMEM((heads, tokens), F32),
            pltpu.VMEM((heads, tokens), F32),
            pltpu.VMEM((tokens // LANES, heads, LANES), F32),
        ],
        compiler_params=params(),
        cost_estimate=pl.CostEstimate(flops=2 * LANES * tokens * features, bytes_accessed=8 * tokens * features, transcendentals=0),
        name="block_states",
    )(*[pltpu.with_memory_space_constraint(v, pltpu.HBM) for v in (doc_lengths, a_log, dt_raw, b_rows, x_in)])


def scan_kernel(head_size, len_ref, skip_ref, b_ref, bt_ref, reach_ref, before_ref, fresh_ref, kept_ref, c_ref, x_ref, z_ref,
                part_ref, gate_ref, csel_ref, state_ref, scores_ref):
    step = pl.program_id(0)
    heads, tokens = before_ref.shape
    groups = c_ref.shape[0] // tokens
    slot = max(8, heads)

    @pl.when(step == 0)
    def _():
        state_ref[...] = jnp.zeros_like(state_ref)
        starts = starts_of(len_ref)
        block = lax.axis_index("seq") * tokens
        pick = pick_matrix(group_of(lax.axis_index("head"), heads, head_size, groups), groups)
        for c in range(tokens // LANES):
            here = slice(c * LANES, (c + 1) * LANES)
            base = block + c * LANES
            row_pos = base + lax.broadcasted_iota(I32, (LANES, LANES), 0)
            col_pos = base + lax.broadcasted_iota(I32, (LANES, LANES), 1)
            keep = (row_pos >= col_pos) & (doc_at(row_pos, starts) == doc_at(col_pos, starts))
            c_low = dot(pick, c_ref[c * LANES * groups:(c + 1) * LANES * groups, :]).astype(BF16)
            csel_ref[here, :] = c_low
            scores = lax.dot_general(c_low, b_ref[here, :], (((1,), (1,)), ((), ())), preferred_element_type=F32)
            scores_ref[c] = jnp.where(keep, scores, 0.0)

    now = pl.ds(pl.multiple_of(step * LANES, LANES), LANES)
    columns = reach_ref[now, :]
    chosen = csel_ref[now, :]
    before = before_ref[:, now]
    fresh = fresh_ref[:, now].astype(BF16)
    kept = kept_ref[step]
    scores = scores_ref[step]
    b_turned = bt_ref[:, now]

    for h in range(heads):
        here = slice(h * LANES, (h + 1) * LANES)
        gaps = jnp.minimum(columns[:, h:h + 1] - before[h:h + 1, :], 80.0)
        weights = (jnp.exp2(gaps) * scores).astype(BF16)
        carried = chosen * columns[:, slot + h:slot + h + 1].astype(BF16)
        x_head = x_ref[now, here]
        state = state_ref[:, here]
        out = dot(jnp.concatenate([weights, carried], axis=1), jnp.concatenate([x_head, state.astype(BF16)], axis=0))
        out = out + skip_ref[h] * x_head.astype(F32)
        written = dot(b_turned * fresh[h:h + 1, :], x_head)
        state_ref[:, here] = state * kept[h:h + 1, :] + written
        z = 0.5 * z_ref[now, here].astype(F32)
        gate = z + z * jnp.tanh(z)
        part_ref[now, here] = out * gate
        gate_ref[now, here] = gate.astype(BF16)


def local_scan(head_size, doc_lengths, d_skip, b_sel, b_turned, decays, c_rows, x_in, z_gate):
    tokens, features = x_in.shape
    chunks = tokens // LANES
    held = [pltpu.with_memory_space_constraint(v, pltpu.VMEM) for v in (c_rows, z_gate)]
    return pl.pallas_call(
        functools.partial(scan_kernel, head_size),
        grid_spec=pltpu.PrefetchScalarGridSpec(
            num_scalar_prefetch=2,
            grid=(chunks,),
            in_specs=[in_vmem()] * 9,
            out_specs=[in_vmem()] * 3,
            scratch_shapes=[
                pltpu.VMEM((LANES, features), F32),
                pltpu.VMEM((chunks, LANES, LANES), F32),
            ],
        ),
        out_shape=[
            pltpu.VMEM((tokens, features), F32),
            pltpu.VMEM((tokens, features), BF16),
            pltpu.VMEM((tokens, LANES), BF16),
        ],
        compiler_params=params(),
        cost_estimate=pl.CostEstimate(flops=16 * LANES * tokens * features, bytes_accessed=8 * tokens * features, transcendentals=0),
        name="local_scan",
    )(doc_lengths, d_skip, b_sel, b_turned, *decays, held[0], x_in, held[1])


def other_language(lang, first, size, starts, langs):
    other = lang
    few = jnp.bool_(True)
    for d, s in enumerate(starts):
        inside = (s > first) & (s < first + size) & (langs[d] != lang)
        few = few & jnp.logical_not(inside & (other != lang) & (langs[d] != other))
        other = jnp.where(inside & (other == lang), langs[d], other)
    return other, few


def has_language(which, first, size, starts, lang_ref):
    found = lang_at(first, starts, lang_ref) == which
    for d, s in enumerate(starts):
        found = found | ((s > first) & (s < first + size) & (lang_ref[d] == which))
    return found


def sum_rows(tile):
    return -(-8 * (tile // LANES) // 16) * 16


def block_of(tile):
    return 2 * LANES if tile % (2 * LANES) == 0 else LANES


def steps_of(tile):
    return 1 if tile <= 2 * LANES else 2


def combine_kernel(n_states, slot, tile, offset, len_ref, lang_ref, c_ref, reach_ref, part_ref, gate_ref, gain_ref, down_ref, *rest):
    states, (gated_ref, other_ref, mine_ref, enter_ref) = rest[:n_states], rest[n_states:]
    features = part_ref.shape[1]
    heads = features // LANES
    starts = starts_of(len_ref)
    langs = [lang_ref[d] for d in range(lang_ref.shape[0])]
    entering = states[0]
    if n_states > 1:
        total = states[0][...].astype(F32)
        for more in states[1:]:
            total = total + more[...].astype(F32)
        enter_ref[...] = total.astype(BF16)
        entering = enter_ref

    odd = lax.axis_index("head") % 2
    pair = min(2, heads)
    rare = []
    halves = [(1 - odd, [(True, other_ref)]), (odd, [(True, mine_ref)])]
    if steps_of(tile) == 2:
        step = pl.program_id(0)
        halves = [((step + 1 + odd) % 2, [(step == 0, other_ref), (step == 1, mine_ref)])]

    def write(refs, rows, value):
        for now, ref in refs:
            if now is True:
                ref[rows, :] = value
                continue

            @pl.when(now)
            def _(ref=ref):
                ref[rows, :] = value

    for half, refs in halves:
        inside = pl.ds(pl.multiple_of(half * tile, LANES), tile)
        at = pl.multiple_of(offset + half * tile, LANES)
        now = pl.ds(at, tile)
        first = lax.axis_index("seq") * part_ref.shape[0] + at
        lang = lang_at(first, starts, langs)
        other, few = other_language(lang, first, tile, starts, langs)
        squares = jnp.zeros((tile, LANES), F32)
        c_low = c_ref[now, :]
        reach = reach_ref[now, :]
        for p in range(heads // pair):
            both = dot(c_low, entering[:, p * pair * LANES:(p + 1) * pair * LANES])
            for i in range(pair):
                h = p * pair + i
                here = slice(h * LANES, (h + 1) * LANES)
                entered = both[:, i * LANES:(i + 1) * LANES] * reach[:, 2 * slot + h:2 * slot + h + 1]
                gated = part_ref[now, here] + entered * gate_ref[now, here].astype(F32)
                squares = squares + gated * gated
                gated_ref[inside, here] = (gated * gain_ref[:, here]).astype(BF16)
        token_lang = lang_at(first + lax.broadcasted_iota(I32, (tile, LANES), 0), starts, langs)
        both = dot(gated_ref[inside, :], jnp.concatenate([down_ref[lang], down_ref[other]], axis=1))
        write(refs, slice(0, tile), jnp.where(token_lang == lang, both[:, :LANES], both[:, LANES:]).astype(BF16))

        ones = jnp.ones((8, LANES), BF16)
        whole = squares.astype(BF16)
        rest_of = (squares - whole.astype(F32)).astype(BF16)
        turned = (((1,), (1,)), ((), ()))
        sums = lax.dot_general(ones, whole, turned, preferred_element_type=F32) + lax.dot_general(ones, rest_of, turned, preferred_element_type=F32)
        rows = [sums[:, c * LANES:(c + 1) * LANES] for c in range(tile // LANES)]
        rows = jnp.concatenate(rows + rows[:1] * (sum_rows(tile) // 8 - len(rows)), axis=0)
        write(refs, slice(tile, tile + sum_rows(tile)), rows.astype(BF16))
        rare += [(jnp.logical_not(few) & now, ref, inside, first, lang, other) for now, ref in refs]

    for many, ref, inside, first, lang, other in rare:
        @pl.when(many)
        def _():
            token_lang = lang_at(first + lax.broadcasted_iota(I32, (tile, LANES), 0), starts, langs)
            for k in range(down_ref.shape[0]):
                @pl.when(has_language(k, first, tile, starts, langs) & (lang != k) & (other != k))
                def _():
                    low = dot(gated_ref[inside, :], down_ref[k])
                    ref[0:tile, :] = jnp.where(token_lang == k, low, ref[0:tile, :].astype(F32)).astype(BF16)


def combine(docs, c_sel, reach, part, gate, gain, down, states, offset, tile, slot):
    features = part.shape[1]
    held = [pltpu.with_memory_space_constraint(v, pltpu.VMEM) for v in [gain, down] + states]
    return pl.pallas_call(
        functools.partial(combine_kernel, len(states), slot, tile, offset),
        grid_spec=pltpu.PrefetchScalarGridSpec(
            num_scalar_prefetch=2,
            grid=(steps_of(tile),),
            in_specs=[in_vmem()] * (6 + len(states)),
            out_specs=[in_vmem()] * 3,
            scratch_shapes=[pltpu.VMEM(states[0].shape, BF16)],
        ),
        out_shape=[
            pltpu.VMEM((2 * tile, features), BF16),
            pltpu.VMEM((tile + sum_rows(tile), LANES), BF16),
            pltpu.VMEM((tile + sum_rows(tile), LANES), BF16),
        ],
        compiler_params=params(),
        cost_estimate=pl.CostEstimate(flops=0, bytes_accessed=0, transcendentals=0),
        name="combine",
    )(*docs, c_sel, reach, part, gate, *held)


def finish_kernel(tile, offset, all_tokens, all_features, len_ref, lang_ref, mine_ref, other_ref, gated_ref, up_ref, *rest):
    out_hbm, out_ref, sems = rest[-3:]
    features = gated_ref.shape[1]
    ranks = up_ref.shape[1]
    starts = starts_of(len_ref)
    langs = [lang_ref[d] for d in range(lang_ref.shape[0])]
    odd = lax.axis_index("head") % 2
    piece = min(4 * LANES, features)
    tokens = tile
    per = 1

    def copy_of(step, begin):
        at = step * tokens
        here = pl.ds(begin, piece)
        return pltpu.make_async_copy(
            out_ref.at[pl.ds(at, tokens), here],
            out_hbm.at[pl.ds(offset + at, tokens), here],
            sems.at[step * (features // piece) + begin // piece],
        )

    def block(step):
        is_mine = odd == step // per
        inside = (step % per) * tokens
        now = pl.ds(step * tokens, tokens)
        scale = jnp.where(is_mine, mine_ref[tile:, :].astype(F32), other_ref[tile:, :].astype(F32))
        scale = lax.rsqrt(scale / all_features + EPS)
        turned = jnp.concatenate([scale] * (LANES // sum_rows(tile)), axis=0).T
        skip = step % per * (tokens // LANES)
        scale = jnp.concatenate([turned[:, 8 * (skip + c):8 * (skip + c) + 1] for c in range(tokens // LANES)], axis=0)
        here = pl.ds(inside, tokens)
        low = jnp.where(is_mine, mine_ref[here, :].astype(F32), other_ref[here, :].astype(F32))
        low = (low * scale).astype(BF16)
        first = lax.axis_index("seq") * all_tokens + offset + step * tokens
        lang = lang_at(first, starts, langs)
        other, few = other_language(lang, first, tokens, starts, langs)
        token_lang = lang_at(first + lax.broadcasted_iota(I32, (tokens, LANES), 0), starts, langs)
        zero = jnp.zeros((), BF16)

        @pl.when(few)
        def _():
            spread = jnp.concatenate([
                jnp.where(token_lang == lang, low, zero),
                jnp.where(token_lang != lang, low, zero),
            ], axis=1)
            for begin in range(0, features, piece):
                here = slice(begin, begin + piece)
                lifted = dot(spread, jnp.concatenate([up_ref[lang, :, here], up_ref[other, :, here]], axis=0))
                out_ref[now, here] = (gated_ref[now, here].astype(F32) * scale + lifted).astype(BF16)
                copy_of(step, begin).start()

        @pl.when(jnp.logical_not(few))
        def _():
            spread = jnp.concatenate([jnp.where(token_lang == k, low, zero) for k in range(up_ref.shape[0])], axis=1)

            def column_piece(i, _):
                here = pl.ds(pl.multiple_of(i * piece, LANES), piece)
                lifted = dot(spread, up_ref[:, :, here].reshape(up_ref.shape[0] * ranks, piece))
                out_ref[now, here] = (gated_ref[now, here].astype(F32) * scale + lifted).astype(BF16)
                return 0

            lax.fori_loop(0, features // piece, column_piece, 0)
            for begin in range(0, features, piece):
                copy_of(step, begin).start()

    for step in range(2 * per):
        block(step)
    for step in range(2 * per):
        for begin in range(0, features, piece):
            copy_of(step, begin).wait()


def finish(docs, mine, other, gated, up, offset, all_tokens, all_features, into=None):
    features = gated.shape[1]
    tile = gated.shape[0] // 2
    held = [pltpu.with_memory_space_constraint(v, pltpu.VMEM) for v in (mine, other, gated, up)]
    more = [] if into is None else [into]
    return pl.pallas_call(
        functools.partial(finish_kernel, tile, offset, all_tokens, all_features),
        grid_spec=pltpu.PrefetchScalarGridSpec(
            num_scalar_prefetch=2,
            grid=(1,),
            in_specs=[in_vmem()] * 4 + [pl.BlockSpec(memory_space=pl.ANY) for _ in more],
            out_specs=pl.BlockSpec(memory_space=pl.ANY),
            scratch_shapes=[
                pltpu.VMEM(gated.shape, BF16),
                pltpu.SemaphoreType.DMA((2 * (features // min(4 * LANES, features)),)),
            ],
        ),
        out_shape=jax.ShapeDtypeStruct((all_tokens, features), BF16),
        input_output_aliases={6: 0} if more else {},
        compiler_params=params(),
        name="finish",
    )(*docs, *held, *more)


def sum_over_head(other, mine, devices, beside=None):
    def across(v, mask):
        return lax.ppermute(v, "head", [(i, i ^ mask) for i in range(devices)])

    more = () if beside is None else (beside,)
    if devices == 1:
        return (mine, other) + more
    total = (mine.astype(F32) + across(other, 1).astype(F32)).astype(BF16)
    bit = 2
    while bit < devices:
        masks = [bit] if 2 * bit >= devices else [3 * bit, bit, 2 * bit]
        arrived = [across(total, m) for m in masks]
        if bit == 2 and more:
            arrived, more = lax.optimization_barrier((arrived, more))
        added = total.astype(F32)
        for a in arrived:
            added = added + a.astype(F32)
        total = added.astype(BF16)
        bit *= 2 ** (1 if len(masks) == 1 else 2)
    return (total, across(total, 1)) + more


def run(seq_size, head_size, relayed, x_in, z_gate, b_input, c_input, dt_raw, a_log, d_skip, norm_gain,
        doc_lengths, doc_lang, adapt_down, adapt_up):
    tokens, features = x_in.shape
    heads = dt_raw.shape[0]
    groups = b_input.shape[1]
    b_rows = b_input.reshape(tokens * groups, b_input.shape[2])
    c_rows = c_input.reshape(tokens * groups, c_input.shape[2])
    docs = (doc_lengths, doc_lang)
    gain = norm_gain.reshape(1, features)
    all_features = features * head_size
    slot = max(8, heads)
    onward = [(i, i + 1) for i in range(seq_size - 1)]

    state, through, b_sel, b_turned, x_held, *decays = block_states(head_size, doc_lengths, a_log, dt_raw, b_rows, x_in)
    state, z_gate, c_rows = lax.optimization_barrier((state, z_gate, c_rows))
    arrived = lax.ppermute(state, "seq", onward)
    part, gate, c_sel = local_scan(head_size, doc_lengths, d_skip, b_sel, b_turned, decays, c_rows, x_held, z_gate)
    reach = decays[0]
    arrived, part = lax.optimization_barrier((arrived, part))
    states = [arrived]
    for _ in range(1, hops_of(tokens, seq_size) if relayed else 1):
        arrived = lax.ppermute((arrived.astype(F32) * through[0:1]).astype(BF16), "seq", onward)
        states.append(arrived)

    head = tokens
    if relayed:
        reached = longest_of(tokens, seq_size) - 1 - (len(states) - 1) * tokens
        head = next((h for h in (tokens // 4, tokens // 2) if reached <= h), tokens)

    def joined(states, offset, tile):
        return combine(docs, c_sel, reach, part, gate, gain, adapt_down, states, offset, tile, slot)

    if head == tokens:
        gated, other, mine = joined(states, 0, tokens // 2)
        sums = sum_over_head(other, mine, head_size)
        return finish(docs, *sums, gated, adapt_up, 0, tokens, all_features)
    late, other, mine = joined(states[:-1], head, (tokens - head) // 2)
    late_sums = sum_over_head(other, mine, head_size)
    states[-1], late_sums = lax.optimization_barrier((states[-1], late_sums))
    early, other, mine = joined(states, 0, head // 2)
    out = finish(docs, *late_sums, late, adapt_up, head, tokens, all_features)
    *early_sums, out = sum_over_head(other, mine, head_size, out)
    return finish(docs, *early_sums, early, adapt_up, 0, tokens, all_features, out)


def longest_of(tokens, seq_size):
    return tokens * seq_size // LONGEST_SHARE


def hops_of(tokens, seq_size):
    return min(-(-(longest_of(tokens, seq_size) - 1) // tokens), seq_size - 1)


def covered_kernel(tokens, seq_size, len_ref, out_ref):
    found, at = jnp.int32(0), jnp.int32(0)
    for d in range(len_ref.shape[0]):
        end = at + len_ref[d]
        for block in range(1, seq_size - 1):
            found = jnp.where((at < block * tokens) & (end > (block + 1) * tokens), 1, found)
        at = end
    out_ref[0] = found


def per_device(seq_size, head_size, *args):
    tokens = args[0].shape[0]
    doc_lengths = args[8]
    if hops_of(tokens, seq_size) < 2:
        return run(seq_size, head_size, False, *args)
    covered = pl.pallas_call(
        functools.partial(covered_kernel, tokens, seq_size),
        in_specs=[pl.BlockSpec(memory_space=pltpu.SMEM)],
        out_specs=pl.BlockSpec(memory_space=pltpu.SMEM),
        out_shape=pltpu.SMEM((1,), I32),
        name="covered",
    )(doc_lengths)[0] > 0
    return lax.cond(
        covered,
        functools.partial(run, seq_size, head_size, True),
        functools.partial(run, seq_size, head_size, False),
        *args,
    )


def solution(mesh):
    placed = (
        P("seq", "head"),
        P("seq", "head"),
        P("seq", None, None),
        P("seq", None, None),
        P("head", "seq"),
        P("head"),
        P("head"),
        P("head"),
        P(),
        P(),
        P(None, "head", None),
        P(None, None, "head"),
    )
    return jax.shard_map(
        functools.partial(per_device, mesh.shape["seq"], mesh.shape["head"]),
        mesh=mesh, in_specs=placed, out_specs=P("seq", "head"), check_vma=False,
    )
```

```python
import functools

import jax
import jax.numpy as jnp
from jax import lax
from jax.experimental import pallas as pl
from jax.experimental.pallas import tpu as pltpu
from jax.sharding import PartitionSpec as P

F32 = jnp.float32
BF16 = jnp.bfloat16
I32 = jnp.int32
LOG2E = 1.4426950408889634
EPS = 1e-05
LANES = 128
LONGEST_SHARE = 3
VMEM_LIMIT = 16 * 1024 * 1024


def params():
    return pltpu.CompilerParams(vmem_limit_bytes=VMEM_LIMIT)


def starts_of(len_ref):
    starts, at = [], jnp.int32(0)
    for d in range(len_ref.shape[0]):
        starts.append(at)
        at = at + len_ref[d]
    return starts


def doc_at(pos, starts):
    found = jnp.where(pos >= starts[0], 0, -1)
    for s in starts[1:]:
        found = found + jnp.where(pos >= s, 1, 0)
    return found


def lang_at(pos, starts, lang_ref):
    found = jnp.where(pos >= 0, lang_ref[0], 0)
    for d in range(1, len(starts)):
        found = jnp.where(pos >= starts[d], lang_ref[d], found)
    return found


def rates(alog_ref, rows):
    which = lax.broadcasted_iota(I32, (rows, LANES), 0)
    column = jnp.zeros((rows, LANES), F32)
    for h in range(rows):
        column = jnp.where(which == h, alog_ref[h], column)
    return -LOG2E * jnp.exp(column)


def softplus(v):
    return jnp.maximum(v, 0.0) + jnp.log(1.0 + jnp.exp(-jnp.abs(v)))


def running(v, back):
    width = v.shape[1]
    lane = lax.broadcasted_iota(I32, v.shape, 1)
    step = 1
    while step < width:
        if back:
            v = v + jnp.where(lane + step < width, pltpu.roll(v, width - step, 1), 0.0)
        else:
            v = v + jnp.where(lane >= step, pltpu.roll(v, step, 1), 0.0)
        step *= 2
    return v


def pick_matrix(group, groups):
    shape = (LANES, LANES * groups)
    row = lax.broadcasted_iota(I32, shape, 0)
    col = lax.broadcasted_iota(I32, shape, 1)
    return jnp.where(col == row * groups + group, 1.0, 0.0).astype(BF16)


def dot(a, b):
    return jnp.dot(a, b, preferred_element_type=F32)


def group_of(head_rank, heads, head_size, groups):
    return head_rank * heads // (heads * head_size // groups)


def state_kernel(head_size, len_hbm, alog_hbm, dt_hbm, b_hbm, x_hbm, state_ref, thr_ref, bsel_ref, bt_ref, x_ref,
                 reach_ref, before_ref, fresh_ref, kept_ref, len_ref, alog_ref, dt_ref, b_ref, w_ref, all_ref, stack_ref, sems):
    heads, tokens = dt_ref.shape
    groups = b_ref.shape[0] // tokens
    copies = [
        pltpu.make_async_copy(source, target, sems.at[i])
        for i, (source, target) in enumerate([
            (dt_hbm, dt_ref), (len_hbm, len_ref), (alog_hbm, alog_ref), (b_hbm, b_ref), (x_hbm, x_ref),
        ])
    ]
    for copy in copies:
        copy.start()
    for copy in copies[:3]:
        copy.wait()

    starts = starts_of(len_ref)
    base = lax.axis_index("seq") * tokens
    rate = rates(alog_ref, heads)
    parts, totals = [], []
    for c in range(tokens // LANES):
        step_dt = softplus(dt_ref[:, c * LANES:(c + 1) * LANES])
        decay = step_dt * rate
        after = running(decay, True)
        parts.append((step_dt, after - decay))
        totals.append(after[:, 0:1])
    last_doc = doc_at(base + tokens - 1, starts)
    first_doc = doc_at(base - 1, starts)
    later = jnp.zeros((heads, 1), F32)
    for c in reversed(range(tokens // LANES)):
        step_dt, inside = parts[c]
        pos = base + c * LANES + lax.broadcasted_iota(I32, (heads, LANES), 1)
        alive = doc_at(pos, starts) == last_doc
        w_ref[:, c * LANES:(c + 1) * LANES] = jnp.where(alive, jnp.exp2(inside + later) * step_dt, 0.0)
        later = later + totals[c]
    kept = jnp.where(last_doc == first_doc, 1.0, 0.0)
    all_ref[...] = jnp.broadcast_to(jnp.exp2(later) * kept, all_ref.shape)
    for h in range(heads):
        thr_ref[:, h * LANES:(h + 1) * LANES] = jnp.broadcast_to(all_ref[h:h + 1, :], (8, LANES))

    slot = max(8, heads)
    stack_ref[...] = jnp.zeros_like(stack_ref)
    past = jnp.zeros((heads, LANES), F32)
    for c in range(tokens // LANES):
        here = slice(c * LANES, (c + 1) * LANES)
        first = base + c * LANES
        step_dt = parts[c][0]
        total_to = running(step_dt * rate, False)
        chunk_total = jnp.broadcast_to(total_to[:, LANES - 1:LANES], (heads, LANES))
        before_ref[:, here] = total_to - jnp.log(step_dt) * LOG2E
        doc = doc_at(first + lax.broadcasted_iota(I32, (heads, LANES), 1), starts)
        doc_in = doc_at(first - 1, starts)
        doc_out = doc_at(first + LANES - 1, starts)
        fresh_ref[:, here] = jnp.where(doc == doc_out, jnp.exp2(chunk_total - total_to) * step_dt, 0.0)
        kept_ref[c] = jnp.exp2(chunk_total) * jnp.where(doc_in == doc_out, 1.0, 0.0)
        stack_ref[c, 0:heads, :] = total_to
        stack_ref[c, slot:slot + heads, :] = jnp.where(doc == doc_in, jnp.exp2(total_to), 0.0)
        stack_ref[c, 2 * slot:2 * slot + heads, :] = jnp.where(doc == first_doc, jnp.exp2(past + total_to), 0.0)
        past = past + chunk_total
        reach_ref[here, :] = stack_ref[c].T

    pick = pick_matrix(group_of(lax.axis_index("head"), heads, head_size, groups), groups)
    copies[3].wait()
    for c in range(tokens // LANES):
        here = slice(c * LANES, (c + 1) * LANES)
        chosen = dot(pick, b_ref[c * LANES * groups:(c + 1) * LANES * groups, :])
        bsel_ref[here, :] = chosen.astype(BF16)
        bt_ref[:, here] = chosen.T.astype(BF16)

    copies[4].wait()
    for h in range(heads):
        here = slice(h * LANES, (h + 1) * LANES)
        weighted = bt_ref[...] * w_ref[h:h + 1, :].astype(BF16)
        state_ref[:, here] = dot(weighted, x_ref[:, here]).astype(BF16)


def in_vmem():
    return pl.BlockSpec(memory_space=pltpu.VMEM)


def block_states(head_size, doc_lengths, a_log, dt_raw, b_rows, x_in):
    heads, tokens = dt_raw.shape
    features = x_in.shape[1]
    return pl.pallas_call(
        functools.partial(state_kernel, head_size),
        grid_spec=pltpu.PrefetchScalarGridSpec(
            num_scalar_prefetch=0,
            grid=(1,),
            in_specs=[pl.BlockSpec(memory_space=pl.ANY)] * 5,
            out_specs=[in_vmem()] * 9,
            scratch_shapes=[
                pltpu.SMEM(doc_lengths.shape, I32),
                pltpu.SMEM(a_log.shape, F32),
                pltpu.VMEM((heads, tokens), F32),
                pltpu.VMEM(b_rows.shape, BF16),
                pltpu.VMEM((heads, tokens), F32),
                pltpu.VMEM((heads, LANES), F32),
                pltpu.VMEM((tokens // LANES, LANES, LANES), F32),
                pltpu.SemaphoreType.DMA((5,)),
            ],
        ),
        out_shape=[
            pltpu.VMEM((LANES, features), BF16),
            pltpu.VMEM((8, features), F32),
            pltpu.VMEM((tokens, LANES), BF16),
            pltpu.VMEM((LANES, tokens), BF16),
            pltpu.VMEM((tokens, features), BF16),
            pltpu.VMEM((tokens, LANES), F32),
            pltpu.VMEM((heads, tokens), F32),
            pltpu.VMEM((heads, tokens), F32),
            pltpu.VMEM((tokens // LANES, heads, LANES), F32),
        ],
        compiler_params=params(),
        cost_estimate=pl.CostEstimate(flops=2 * LANES * tokens * features, bytes_accessed=8 * tokens * features, transcendentals=0),
        name="block_states",
    )(*[pltpu.with_memory_space_constraint(v, pltpu.HBM) for v in (doc_lengths, a_log, dt_raw, b_rows, x_in)])


def scan_kernel(head_size, len_ref, skip_ref, b_ref, bt_ref, reach_ref, before_ref, fresh_ref, kept_ref, c_ref, x_ref, z_ref,
                part_ref, gate_ref, csel_ref, state_ref, scores_ref):
    step = pl.program_id(0)
    heads, tokens = before_ref.shape
    groups = c_ref.shape[0] // tokens
    slot = max(8, heads)

    @pl.when(step == 0)
    def _():
        state_ref[...] = jnp.zeros_like(state_ref)
        starts = starts_of(len_ref)
        block = lax.axis_index("seq") * tokens
        pick = pick_matrix(group_of(lax.axis_index("head"), heads, head_size, groups), groups)
        for c in range(tokens // LANES):
            here = slice(c * LANES, (c + 1) * LANES)
            base = block + c * LANES
            row_pos = base + lax.broadcasted_iota(I32, (LANES, LANES), 0)
            col_pos = base + lax.broadcasted_iota(I32, (LANES, LANES), 1)
            keep = (row_pos >= col_pos) & (doc_at(row_pos, starts) == doc_at(col_pos, starts))
            c_low = dot(pick, c_ref[c * LANES * groups:(c + 1) * LANES * groups, :]).astype(BF16)
            csel_ref[here, :] = c_low
            scores = lax.dot_general(c_low, b_ref[here, :], (((1,), (1,)), ((), ())), preferred_element_type=F32)
            scores_ref[c] = jnp.where(keep, scores, 0.0)

    now = pl.ds(pl.multiple_of(step * LANES, LANES), LANES)
    columns = reach_ref[now, :]
    chosen = csel_ref[now, :]
    before = before_ref[:, now]
    fresh = fresh_ref[:, now].astype(BF16)
    kept = kept_ref[step]
    scores = scores_ref[step]
    b_turned = bt_ref[:, now]

    for h in range(heads):
        here = slice(h * LANES, (h + 1) * LANES)
        gaps = jnp.minimum(columns[:, h:h + 1] - before[h:h + 1, :], 80.0)
        weights = (jnp.exp2(gaps) * scores).astype(BF16)
        carried = chosen * columns[:, slot + h:slot + h + 1].astype(BF16)
        x_head = x_ref[now, here]
        state = state_ref[:, here]
        out = dot(jnp.concatenate([weights, carried], axis=1), jnp.concatenate([x_head, state.astype(BF16)], axis=0))
        out = out + skip_ref[h] * x_head.astype(F32)
        written = dot(b_turned * fresh[h:h + 1, :], x_head)
        state_ref[:, here] = state * kept[h:h + 1, :] + written
        z = 0.5 * z_ref[now, here].astype(F32)
        gate = z + z * jnp.tanh(z)
        part_ref[now, here] = out * gate
        gate_ref[now, here] = gate.astype(BF16)


def local_scan(head_size, doc_lengths, d_skip, b_sel, b_turned, decays, c_rows, x_in, z_gate):
    tokens, features = x_in.shape
    chunks = tokens // LANES
    held = [pltpu.with_memory_space_constraint(v, pltpu.VMEM) for v in (c_rows, z_gate)]
    return pl.pallas_call(
        functools.partial(scan_kernel, head_size),
        grid_spec=pltpu.PrefetchScalarGridSpec(
            num_scalar_prefetch=2,
            grid=(chunks,),
            in_specs=[in_vmem()] * 9,
            out_specs=[in_vmem()] * 3,
            scratch_shapes=[
                pltpu.VMEM((LANES, features), F32),
                pltpu.VMEM((chunks, LANES, LANES), F32),
            ],
        ),
        out_shape=[
            pltpu.VMEM((tokens, features), F32),
            pltpu.VMEM((tokens, features), BF16),
            pltpu.VMEM((tokens, LANES), BF16),
        ],
        compiler_params=params(),
        cost_estimate=pl.CostEstimate(flops=16 * LANES * tokens * features, bytes_accessed=8 * tokens * features, transcendentals=0),
        name="local_scan",
    )(doc_lengths, d_skip, b_sel, b_turned, *decays, held[0], x_in, held[1])


def other_language(lang, first, size, starts, langs):
    other = lang
    few = jnp.bool_(True)
    for d, s in enumerate(starts):
        inside = (s > first) & (s < first + size) & (langs[d] != lang)
        few = few & jnp.logical_not(inside & (other != lang) & (langs[d] != other))
        other = jnp.where(inside & (other == lang), langs[d], other)
    return other, few


def has_language(which, first, size, starts, lang_ref):
    found = lang_at(first, starts, lang_ref) == which
    for d, s in enumerate(starts):
        found = found | ((s > first) & (s < first + size) & (lang_ref[d] == which))
    return found


def sum_rows(tile):
    return -(-8 * (tile // LANES) // 16) * 16


def combine_kernel(n_states, slot, tile, mine, len_ref, lang_ref, c_ref, reach_ref, part_ref, gate_ref, gain_ref, down_ref, *rest):
    states, (gated_ref, ref, enter_ref) = rest[:n_states], rest[-3:]
    features = part_ref.shape[1]
    heads = features // LANES
    starts = starts_of(len_ref)
    langs = [lang_ref[d] for d in range(lang_ref.shape[0])]
    entering = states[0]
    if n_states > 1:
        total = states[0][...].astype(F32)
        for more in states[1:]:
            total = total + more[...].astype(F32)
        enter_ref[...] = total.astype(BF16)
        entering = enter_ref

    odd = lax.axis_index("head") % 2
    half = odd if mine else 1 - odd
    pair = min(2, heads)
    at = pl.multiple_of(half * tile, LANES)
    now = pl.ds(at, tile)
    first = lax.axis_index("seq") * part_ref.shape[0] + at
    lang = lang_at(first, starts, langs)
    other, few = other_language(lang, first, tile, starts, langs)
    squares = jnp.zeros((tile, LANES), F32)
    c_low = c_ref[now, :]
    reach = reach_ref[now, :]
    for p in range(heads // pair):
        both = dot(c_low, entering[:, p * pair * LANES:(p + 1) * pair * LANES])
        for i in range(pair):
            h = p * pair + i
            here = slice(h * LANES, (h + 1) * LANES)
            entered = both[:, i * LANES:(i + 1) * LANES] * reach[:, 2 * slot + h:2 * slot + h + 1]
            gated = part_ref[now, here] + entered * gate_ref[now, here].astype(F32)
            squares = squares + gated * gated
            gated_ref[now, here] = (gated * gain_ref[:, here]).astype(BF16)
    token_lang = lang_at(first + lax.broadcasted_iota(I32, (tile, LANES), 0), starts, langs)
    both = dot(gated_ref[now, :], jnp.concatenate([down_ref[lang], down_ref[other]], axis=1))
    ref[0:tile, :] = jnp.where(token_lang == lang, both[:, :LANES], both[:, LANES:]).astype(BF16)

    ones = jnp.ones((8, LANES), BF16)
    whole = squares.astype(BF16)
    rest_of = (squares - whole.astype(F32)).astype(BF16)
    turned = (((1,), (1,)), ((), ()))
    sums = lax.dot_general(ones, whole, turned, preferred_element_type=F32) + lax.dot_general(ones, rest_of, turned, preferred_element_type=F32)
    rows = [sums[:, c * LANES:(c + 1) * LANES] for c in range(tile // LANES)]
    rows = jnp.concatenate(rows + rows[:1] * (sum_rows(tile) // 8 - len(rows)), axis=0)
    ref[tile:tile + sum_rows(tile), :] = rows.astype(BF16)

    @pl.when(jnp.logical_not(few))
    def _():
        token_lang = lang_at(first + lax.broadcasted_iota(I32, (tile, LANES), 0), starts, langs)
        for k in range(down_ref.shape[0]):
            @pl.when(has_language(k, first, tile, starts, langs) & (lang != k) & (other != k))
            def _():
                low = dot(gated_ref[now, :], down_ref[k])
                ref[0:tile, :] = jnp.where(token_lang == k, low, ref[0:tile, :].astype(F32)).astype(BF16)


def combine(docs, c_sel, reach, part, gate, gain, down, states, slot, mine, into=None):
    tokens, features = part.shape
    tile = tokens // 2
    held = [pltpu.with_memory_space_constraint(v, pltpu.VMEM) for v in [gain, down] + states]
    more = [] if into is None else [into]
    return pl.pallas_call(
        functools.partial(combine_kernel, len(states), slot, tile, mine),
        grid_spec=pltpu.PrefetchScalarGridSpec(
            num_scalar_prefetch=2,
            grid=(1,),
            in_specs=[in_vmem()] * (6 + len(states)) + [pl.BlockSpec(memory_space=pl.ANY) for _ in more],
            out_specs=[in_vmem()] * 2,
            scratch_shapes=[pltpu.VMEM(states[0].shape, BF16)],
        ),
        out_shape=[
            pltpu.VMEM((tokens, features), BF16),
            pltpu.VMEM((tile + sum_rows(tile), LANES), BF16),
        ],
        input_output_aliases={8 + len(states): 0} if more else {},
        compiler_params=params(),
        cost_estimate=pl.CostEstimate(flops=0, bytes_accessed=0, transcendentals=0),
        name="combine",
    )(*docs, c_sel, reach, part, gate, *held, *more)


def finish_kernel(tile, all_features, len_ref, lang_ref, mine_ref, other_ref, gated_ref, up_ref, out_hbm, out_ref, sems):
    features = gated_ref.shape[1]
    ranks = up_ref.shape[1]
    starts = starts_of(len_ref)
    langs = [lang_ref[d] for d in range(lang_ref.shape[0])]
    odd = lax.axis_index("head") % 2
    piece = min(4 * LANES, features)
    tokens = tile

    def copy_of(step, i):
        at = step * tokens
        here = pl.ds(pl.multiple_of(i * piece, LANES), piece)
        return pltpu.make_async_copy(
            out_ref.at[pl.ds(at, tokens), here],
            out_hbm.at[pl.ds(at, tokens), here],
            sems.at[step * (features // piece) + i],
        )

    def block(step):
        is_mine = odd == step
        now = pl.ds(step * tokens, tokens)
        scale = jnp.where(is_mine, mine_ref[tile:, :].astype(F32), other_ref[tile:, :].astype(F32))
        scale = lax.rsqrt(scale / all_features + EPS)
        turned = jnp.concatenate([scale] * (LANES // sum_rows(tile)), axis=0).T
        scale = jnp.concatenate([turned[:, 8 * c:8 * c + 1] for c in range(tokens // LANES)], axis=0)
        low = jnp.where(is_mine, mine_ref[0:tokens, :].astype(F32), other_ref[0:tokens, :].astype(F32))
        low = (low * scale).astype(BF16)
        first = (lax.axis_index("seq") * 2 + step) * tokens
        lang = lang_at(first, starts, langs)
        other, few = other_language(lang, first, tokens, starts, langs)
        token_lang = lang_at(first + lax.broadcasted_iota(I32, (tokens, LANES), 0), starts, langs)
        zero = jnp.zeros((), BF16)

        @pl.when(few)
        def _():
            spread = jnp.concatenate([
                jnp.where(token_lang == lang, low, zero),
                jnp.where(token_lang != lang, low, zero),
            ], axis=1)
            for begin in range(0, features, piece):
                here = slice(begin, begin + piece)
                lifted = dot(spread, jnp.concatenate([up_ref[lang, :, here], up_ref[other, :, here]], axis=0))
                out_ref[now, here] = (gated_ref[now, here].astype(F32) * scale + lifted).astype(BF16)
                copy_of(step, begin // piece).start()

        @pl.when(jnp.logical_not(few))
        def _():
            spread = jnp.concatenate([jnp.where(token_lang == k, low, zero) for k in range(up_ref.shape[0])], axis=1)

            def column_piece(i, _):
                here = pl.ds(pl.multiple_of(i * piece, LANES), piece)
                lifted = dot(spread, up_ref[:, :, here].reshape(up_ref.shape[0] * ranks, piece))
                out_ref[now, here] = (gated_ref[now, here].astype(F32) * scale + lifted).astype(BF16)
                copy_of(step, i).start()
                return 0

            lax.fori_loop(0, features // piece, column_piece, 0)

    for step in range(2):
        block(step)
    for step in range(2):
        for i in range(features // piece):
            copy_of(step, i).wait()


def finish(docs, mine, other, gated, up, all_features):
    tokens, features = gated.shape
    tile = tokens // 2
    held = [pltpu.with_memory_space_constraint(v, pltpu.VMEM) for v in (mine, other, gated, up)]
    return pl.pallas_call(
        functools.partial(finish_kernel, tile, all_features),
        grid_spec=pltpu.PrefetchScalarGridSpec(
            num_scalar_prefetch=2,
            grid=(1,),
            in_specs=[in_vmem()] * 4,
            out_specs=pl.BlockSpec(memory_space=pl.ANY),
            scratch_shapes=[
                pltpu.VMEM(gated.shape, BF16),
                pltpu.SemaphoreType.DMA((2 * (features // min(4 * LANES, features)),)),
            ],
        ),
        out_shape=pltpu.HBM(gated.shape, BF16),
        compiler_params=params(),
        name="finish",
    )(*docs, *held)


def sum_over_head(mine, sent, across, devices):
    total = (mine.astype(F32) + sent.astype(F32)).astype(BF16)
    bit = 2
    while bit < devices:
        masks = [bit] if 2 * bit >= devices else [3 * bit, bit, 2 * bit]
        added = total.astype(F32)
        for arrived in [across(total, m) for m in masks]:
            added = added + arrived.astype(F32)
        total = added.astype(BF16)
        bit *= 2 ** (1 if len(masks) == 1 else 2)
    return total, across(total, 1)


def run(seq_size, head_size, relayed, x_in, z_gate, b_input, c_input, dt_raw, a_log, d_skip, norm_gain,
        doc_lengths, doc_lang, adapt_down, adapt_up):
    tokens, features = x_in.shape
    heads = dt_raw.shape[0]
    groups = b_input.shape[1]
    b_rows = b_input.reshape(tokens * groups, b_input.shape[2])
    c_rows = c_input.reshape(tokens * groups, c_input.shape[2])
    docs = (doc_lengths, doc_lang)
    gain = norm_gain.reshape(1, features)
    all_features = features * head_size
    slot = max(8, heads)
    onward = [(i, i + 1) for i in range(seq_size - 1)]

    state, through, b_sel, b_turned, x_held, *decays = block_states(head_size, doc_lengths, a_log, dt_raw, b_rows, x_in)
    state, z_gate, c_rows = lax.optimization_barrier((state, z_gate, c_rows))
    arrived = lax.ppermute(state, "seq", onward)
    part, gate, c_sel = local_scan(head_size, doc_lengths, d_skip, b_sel, b_turned, decays, c_rows, x_held, z_gate)
    reach = decays[0]
    arrived, part = lax.optimization_barrier((arrived, part))
    states = [arrived]
    for _ in range(1, hops_of(tokens, seq_size) if relayed else 1):
        arrived = lax.ppermute((arrived.astype(F32) * through[0:1]).astype(BF16), "seq", onward)
        states.append(arrived)

    def across(v, mask):
        return lax.ppermute(v, "head", [(i, i ^ mask) for i in range(head_size)])

    shared = (docs, c_sel, reach, part, gate, gain, adapt_down, states, slot)
    gated, theirs = combine(*shared, False)
    sent = across(theirs, 1)
    gated, mine = combine(*shared, True, gated)
    mine, other = sum_over_head(mine, sent, across, head_size)
    return finish(docs, mine, other, gated, adapt_up, all_features)


def longest_of(tokens, seq_size):
    return tokens * seq_size // LONGEST_SHARE


def hops_of(tokens, seq_size):
    return min(-(-(longest_of(tokens, seq_size) - 1) // tokens), seq_size - 1)


def covered_kernel(tokens, seq_size, len_ref, out_ref):
    found, at = jnp.int32(0), jnp.int32(0)
    for d in range(len_ref.shape[0]):
        end = at + len_ref[d]
        for block in range(1, seq_size - 1):
            found = jnp.where((at < block * tokens) & (end > (block + 1) * tokens), 1, found)
        at = end
    out_ref[0] = found


def per_device(seq_size, head_size, *args):
    tokens = args[0].shape[0]
    doc_lengths = args[8]
    if hops_of(tokens, seq_size) < 2:
        return run(seq_size, head_size, False, *args)
    covered = pl.pallas_call(
        functools.partial(covered_kernel, tokens, seq_size),
        in_specs=[pl.BlockSpec(memory_space=pltpu.SMEM)],
        out_specs=pl.BlockSpec(memory_space=pltpu.SMEM),
        out_shape=pltpu.SMEM((1,), I32),
        name="covered",
    )(doc_lengths)[0] > 0
    return lax.cond(
        covered,
        functools.partial(run, seq_size, head_size, True),
        functools.partial(run, seq_size, head_size, False),
        *args,
    )


def solution(mesh):
    placed = (
        P("seq", "head"),
        P("seq", "head"),
        P("seq", None, None),
        P("seq", None, None),
        P("head", "seq"),
        P("head"),
        P("head"),
        P("head"),
        P(),
        P(),
        P(None, "head", None),
        P(None, None, "head"),
    )
    return jax.shard_map(
        functools.partial(per_device, mesh.shape["seq"], mesh.shape["head"]),
        mesh=mesh, in_specs=placed, out_specs=P("seq", "head"), check_vma=False,
    )
```

```python
import functools

import jax
import jax.numpy as jnp
from jax import lax
from jax.experimental import pallas as pl
from jax.experimental.pallas import tpu as pltpu
from jax.sharding import PartitionSpec as P

F32 = jnp.float32
BF16 = jnp.bfloat16
I32 = jnp.int32
LOG2E = 1.4426950408889634
EPS = 1e-05
LANES = 128
LONGEST_SHARE = 3
VMEM_LIMIT = 16 * 1024 * 1024


def params():
    return pltpu.CompilerParams(vmem_limit_bytes=VMEM_LIMIT)


def starts_of(len_ref):
    starts, at = [], jnp.int32(0)
    for d in range(len_ref.shape[0]):
        starts.append(at)
        at = at + len_ref[d]
    return starts


def doc_at(pos, starts):
    found = jnp.where(pos >= starts[0], 0, -1)
    for s in starts[1:]:
        found = found + jnp.where(pos >= s, 1, 0)
    return found


def lang_at(pos, starts, lang_ref):
    found = jnp.where(pos >= 0, lang_ref[0], 0)
    for d in range(1, len(starts)):
        found = jnp.where(pos >= starts[d], lang_ref[d], found)
    return found


def rates(alog_ref, rows):
    which = lax.broadcasted_iota(I32, (rows, LANES), 0)
    column = jnp.zeros((rows, LANES), F32)
    for h in range(rows):
        column = jnp.where(which == h, alog_ref[h], column)
    return -LOG2E * jnp.exp(column)


def softplus(v):
    return jnp.maximum(v, 0.0) + jnp.log(1.0 + jnp.exp(-jnp.abs(v)))


def running(v, back):
    width = v.shape[1]
    lane = lax.broadcasted_iota(I32, v.shape, 1)
    step = 1
    while step < width:
        if back:
            v = v + jnp.where(lane + step < width, pltpu.roll(v, width - step, 1), 0.0)
        else:
            v = v + jnp.where(lane >= step, pltpu.roll(v, step, 1), 0.0)
        step *= 2
    return v


def pick_matrix(group, groups):
    shape = (LANES, LANES * groups)
    row = lax.broadcasted_iota(I32, shape, 0)
    col = lax.broadcasted_iota(I32, shape, 1)
    return jnp.where(col == row * groups + group, 1.0, 0.0).astype(BF16)


def dot(a, b):
    return jnp.dot(a, b, preferred_element_type=F32)


def group_of(head_rank, heads, head_size, groups):
    return head_rank * heads // (heads * head_size // groups)


def state_kernel(head_size, len_hbm, alog_hbm, dt_hbm, b_hbm, x_hbm, state_ref, thr_ref, bsel_ref, bt_ref, x_ref,
                 reach_ref, before_ref, fresh_ref, kept_ref, len_ref, alog_ref, dt_ref, b_ref, w_ref, all_ref, stack_ref, sems):
    heads, tokens = dt_ref.shape
    groups = b_ref.shape[0] // tokens
    copies = [
        pltpu.make_async_copy(source, target, sems.at[i])
        for i, (source, target) in enumerate([
            (dt_hbm, dt_ref), (len_hbm, len_ref), (alog_hbm, alog_ref), (b_hbm, b_ref), (x_hbm, x_ref),
        ])
    ]
    for copy in copies:
        copy.start()
    for copy in copies[:3]:
        copy.wait()

    starts = starts_of(len_ref)
    base = lax.axis_index("seq") * tokens
    rate = rates(alog_ref, heads)
    parts, totals = [], []
    for c in range(tokens // LANES):
        step_dt = softplus(dt_ref[:, c * LANES:(c + 1) * LANES])
        decay = step_dt * rate
        after = running(decay, True)
        parts.append((step_dt, after - decay))
        totals.append(after[:, 0:1])
    last_doc = doc_at(base + tokens - 1, starts)
    first_doc = doc_at(base - 1, starts)
    later = jnp.zeros((heads, 1), F32)
    for c in reversed(range(tokens // LANES)):
        step_dt, inside = parts[c]
        pos = base + c * LANES + lax.broadcasted_iota(I32, (heads, LANES), 1)
        alive = doc_at(pos, starts) == last_doc
        w_ref[:, c * LANES:(c + 1) * LANES] = jnp.where(alive, jnp.exp2(inside + later) * step_dt, 0.0)
        later = later + totals[c]
    kept = jnp.where(last_doc == first_doc, 1.0, 0.0)
    all_ref[...] = jnp.broadcast_to(jnp.exp2(later) * kept, all_ref.shape)
    for h in range(heads):
        thr_ref[:, h * LANES:(h + 1) * LANES] = jnp.broadcast_to(all_ref[h:h + 1, :], (8, LANES))

    slot = max(8, heads)
    stack_ref[...] = jnp.zeros_like(stack_ref)
    past = jnp.zeros((heads, LANES), F32)
    for c in range(tokens // LANES):
        here = slice(c * LANES, (c + 1) * LANES)
        first = base + c * LANES
        step_dt = parts[c][0]
        total_to = running(step_dt * rate, False)
        chunk_total = jnp.broadcast_to(total_to[:, LANES - 1:LANES], (heads, LANES))
        before_ref[:, here] = total_to - jnp.log(step_dt) * LOG2E
        doc = doc_at(first + lax.broadcasted_iota(I32, (heads, LANES), 1), starts)
        doc_in = doc_at(first - 1, starts)
        doc_out = doc_at(first + LANES - 1, starts)
        fresh_ref[:, here] = jnp.where(doc == doc_out, jnp.exp2(chunk_total - total_to) * step_dt, 0.0)
        kept_ref[c] = jnp.exp2(chunk_total) * jnp.where(doc_in == doc_out, 1.0, 0.0)
        stack_ref[c, 0:heads, :] = total_to
        stack_ref[c, slot:slot + heads, :] = jnp.where(doc == doc_in, jnp.exp2(total_to), 0.0)
        stack_ref[c, 2 * slot:2 * slot + heads, :] = jnp.where(doc == first_doc, jnp.exp2(past + total_to), 0.0)
        past = past + chunk_total
        reach_ref[here, :] = stack_ref[c].T

    pick = pick_matrix(group_of(lax.axis_index("head"), heads, head_size, groups), groups)
    copies[3].wait()
    for c in range(tokens // LANES):
        here = slice(c * LANES, (c + 1) * LANES)
        chosen = dot(pick, b_ref[c * LANES * groups:(c + 1) * LANES * groups, :])
        bsel_ref[here, :] = chosen.astype(BF16)
        bt_ref[:, here] = chosen.T.astype(BF16)

    copies[4].wait()
    for h in range(heads):
        here = slice(h * LANES, (h + 1) * LANES)
        weighted = bt_ref[...] * w_ref[h:h + 1, :].astype(BF16)
        state_ref[:, here] = dot(weighted, x_ref[:, here]).astype(BF16)


def in_vmem():
    return pl.BlockSpec(memory_space=pltpu.VMEM)


def block_states(head_size, doc_lengths, a_log, dt_raw, b_rows, x_in):
    heads, tokens = dt_raw.shape
    features = x_in.shape[1]
    return pl.pallas_call(
        functools.partial(state_kernel, head_size),
        grid_spec=pltpu.PrefetchScalarGridSpec(
            num_scalar_prefetch=0,
            grid=(1,),
            in_specs=[pl.BlockSpec(memory_space=pl.ANY)] * 5,
            out_specs=[in_vmem()] * 9,
            scratch_shapes=[
                pltpu.SMEM(doc_lengths.shape, I32),
                pltpu.SMEM(a_log.shape, F32),
                pltpu.VMEM((heads, tokens), F32),
                pltpu.VMEM(b_rows.shape, BF16),
                pltpu.VMEM((heads, tokens), F32),
                pltpu.VMEM((heads, LANES), F32),
                pltpu.VMEM((tokens // LANES, LANES, LANES), F32),
                pltpu.SemaphoreType.DMA((5,)),
            ],
        ),
        out_shape=[
            pltpu.VMEM((LANES, features), BF16),
            pltpu.VMEM((8, features), F32),
            pltpu.VMEM((tokens, LANES), BF16),
            pltpu.VMEM((LANES, tokens), BF16),
            pltpu.VMEM((tokens, features), BF16),
            pltpu.VMEM((tokens, LANES), F32),
            pltpu.VMEM((heads, tokens), F32),
            pltpu.VMEM((heads, tokens), F32),
            pltpu.VMEM((tokens // LANES, heads, LANES), F32),
        ],
        compiler_params=params(),
        cost_estimate=pl.CostEstimate(flops=2 * LANES * tokens * features, bytes_accessed=8 * tokens * features, transcendentals=0),
        name="block_states",
    )(*[pltpu.with_memory_space_constraint(v, pltpu.HBM) for v in (doc_lengths, a_log, dt_raw, b_rows, x_in)])


def scan_kernel(head_size, len_ref, skip_ref, b_ref, bt_ref, reach_ref, before_ref, fresh_ref, kept_ref, c_ref, x_ref, z_ref,
                part_ref, gate_ref, csel_ref, state_ref, scores_ref):
    step = pl.program_id(0)
    heads, tokens = before_ref.shape
    groups = c_ref.shape[0] // tokens
    slot = max(8, heads)

    @pl.when(step == 0)
    def _():
        state_ref[...] = jnp.zeros_like(state_ref)
        starts = starts_of(len_ref)
        block = lax.axis_index("seq") * tokens
        pick = pick_matrix(group_of(lax.axis_index("head"), heads, head_size, groups), groups)
        for c in range(tokens // LANES):
            here = slice(c * LANES, (c + 1) * LANES)
            base = block + c * LANES
            row_pos = base + lax.broadcasted_iota(I32, (LANES, LANES), 0)
            col_pos = base + lax.broadcasted_iota(I32, (LANES, LANES), 1)
            keep = (row_pos >= col_pos) & (doc_at(row_pos, starts) == doc_at(col_pos, starts))
            c_low = dot(pick, c_ref[c * LANES * groups:(c + 1) * LANES * groups, :]).astype(BF16)
            csel_ref[here, :] = c_low
            scores = lax.dot_general(c_low, b_ref[here, :], (((1,), (1,)), ((), ())), preferred_element_type=F32)
            scores_ref[c] = jnp.where(keep, scores, 0.0)

    now = pl.ds(pl.multiple_of(step * LANES, LANES), LANES)
    columns = reach_ref[now, :]
    chosen = csel_ref[now, :]
    before = before_ref[:, now]
    fresh = fresh_ref[:, now].astype(BF16)
    kept = kept_ref[step]
    scores = scores_ref[step]
    b_turned = bt_ref[:, now]

    for h in range(heads):
        here = slice(h * LANES, (h + 1) * LANES)
        gaps = jnp.minimum(columns[:, h:h + 1] - before[h:h + 1, :], 80.0)
        weights = (jnp.exp2(gaps) * scores).astype(BF16)
        carried = chosen * columns[:, slot + h:slot + h + 1].astype(BF16)
        x_head = x_ref[now, here]
        state = state_ref[:, here]
        out = dot(jnp.concatenate([weights, carried], axis=1), jnp.concatenate([x_head, state.astype(BF16)], axis=0))
        out = out + skip_ref[h] * x_head.astype(F32)
        written = dot(b_turned * fresh[h:h + 1, :], x_head)
        state_ref[:, here] = state * kept[h:h + 1, :] + written
        z = 0.5 * z_ref[now, here].astype(F32)
        gate = z + z * jnp.tanh(z)
        part_ref[now, here] = out * gate
        gate_ref[now, here] = gate.astype(BF16)


def local_scan(head_size, doc_lengths, d_skip, b_sel, b_turned, decays, c_rows, x_in, z_gate):
    tokens, features = x_in.shape
    chunks = tokens // LANES
    held = [pltpu.with_memory_space_constraint(v, pltpu.VMEM) for v in (c_rows, z_gate)]
    return pl.pallas_call(
        functools.partial(scan_kernel, head_size),
        grid_spec=pltpu.PrefetchScalarGridSpec(
            num_scalar_prefetch=2,
            grid=(chunks,),
            in_specs=[in_vmem()] * 9,
            out_specs=[in_vmem()] * 3,
            scratch_shapes=[
                pltpu.VMEM((LANES, features), F32),
                pltpu.VMEM((chunks, LANES, LANES), F32),
            ],
        ),
        out_shape=[
            pltpu.VMEM((tokens, features), F32),
            pltpu.VMEM((tokens, features), BF16),
            pltpu.VMEM((tokens, LANES), BF16),
        ],
        compiler_params=params(),
        cost_estimate=pl.CostEstimate(flops=16 * LANES * tokens * features, bytes_accessed=8 * tokens * features, transcendentals=0),
        name="local_scan",
    )(doc_lengths, d_skip, b_sel, b_turned, *decays, held[0], x_in, held[1])


def other_language(lang, first, size, starts, langs):
    other = lang
    few = jnp.bool_(True)
    for d, s in enumerate(starts):
        inside = (s > first) & (s < first + size) & (langs[d] != lang)
        few = few & jnp.logical_not(inside & (other != lang) & (langs[d] != other))
        other = jnp.where(inside & (other == lang), langs[d], other)
    return other, few


def has_language(which, first, size, starts, lang_ref):
    found = lang_at(first, starts, lang_ref) == which
    for d, s in enumerate(starts):
        found = found | ((s > first) & (s < first + size) & (lang_ref[d] == which))
    return found


def sum_rows(tile):
    return -(-4 * (tile // LANES) // 16) * 16


def combine_kernel(n_states, slot, tile, mine, len_ref, lang_ref, c_ref, reach_ref, part_ref, gate_ref, gain_ref, down_ref, *rest):
    states, (gated_ref, ref, enter_ref) = rest[:n_states], rest[-3:]
    features = part_ref.shape[1]
    heads = features // LANES
    starts = starts_of(len_ref)
    langs = [lang_ref[d] for d in range(lang_ref.shape[0])]
    entering = states[0]
    if n_states > 1:
        total = states[0][...].astype(F32)
        for more in states[1:]:
            total = total + more[...].astype(F32)
        enter_ref[...] = total.astype(BF16)
        entering = enter_ref

    odd = lax.axis_index("head") % 2
    half = odd if mine else 1 - odd
    pair = min(2, heads)
    at = pl.multiple_of(half * tile, LANES)
    now = pl.ds(at, tile)
    first = lax.axis_index("seq") * part_ref.shape[0] + at
    lang = lang_at(first, starts, langs)
    other, few = other_language(lang, first, tile, starts, langs)
    squares = jnp.zeros((tile, LANES), F32)
    c_low = c_ref[now, :]
    reach = reach_ref[now, :]
    for p in range(heads // pair):
        both = dot(c_low, entering[:, p * pair * LANES:(p + 1) * pair * LANES])
        for i in range(pair):
            h = p * pair + i
            here = slice(h * LANES, (h + 1) * LANES)
            entered = both[:, i * LANES:(i + 1) * LANES] * reach[:, 2 * slot + h:2 * slot + h + 1]
            gated = part_ref[now, here] + entered * gate_ref[now, here].astype(F32)
            squares = squares + gated * gated
            gated_ref[now, here] = (gated * gain_ref[:, here]).astype(BF16)
    token_lang = lang_at(first + lax.broadcasted_iota(I32, (tile, LANES), 0), starts, langs)
    both = dot(gated_ref[now, :], jnp.concatenate([down_ref[lang], down_ref[other]], axis=1))
    ref[0:tile, :] = jnp.where(token_lang == lang, both[:, :LANES], both[:, LANES:]).astype(BF16)

    ones = jnp.ones((8, LANES), BF16)
    whole = squares.astype(BF16)
    rest_of = (squares - whole.astype(F32)).astype(BF16)
    turned = (((1,), (1,)), ((), ()))
    sums = lax.dot_general(ones, whole, turned, preferred_element_type=F32) + lax.dot_general(ones, rest_of, turned, preferred_element_type=F32)
    rows = [sums[:, c * LANES:(c + 1) * LANES] for c in range(tile // LANES)]
    rows += rows[:1] * (sum_rows(tile) // 4 - len(rows))
    upper = lax.broadcasted_iota(I32, (8, LANES), 0) < 4
    rows = jnp.concatenate([jnp.where(upper, a, b) for a, b in zip(rows[0::2], rows[1::2])], axis=0)
    ref[tile:tile + sum_rows(tile), :] = rows.astype(BF16)

    @pl.when(jnp.logical_not(few))
    def _():
        token_lang = lang_at(first + lax.broadcasted_iota(I32, (tile, LANES), 0), starts, langs)
        for k in range(down_ref.shape[0]):
            @pl.when(has_language(k, first, tile, starts, langs) & (lang != k) & (other != k))
            def _():
                low = dot(gated_ref[now, :], down_ref[k])
                ref[0:tile, :] = jnp.where(token_lang == k, low, ref[0:tile, :].astype(F32)).astype(BF16)


def combine(docs, c_sel, reach, part, gate, gain, down, states, slot, mine, into=None):
    tokens, features = part.shape
    tile = tokens // 2
    held = [pltpu.with_memory_space_constraint(v, pltpu.VMEM) for v in [gain, down] + states]
    more = [] if into is None else [into]
    return pl.pallas_call(
        functools.partial(combine_kernel, len(states), slot, tile, mine),
        grid_spec=pltpu.PrefetchScalarGridSpec(
            num_scalar_prefetch=2,
            grid=(1,),
            in_specs=[in_vmem()] * (6 + len(states)) + [pl.BlockSpec(memory_space=pl.ANY) for _ in more],
            out_specs=[in_vmem()] * 2,
            scratch_shapes=[pltpu.VMEM(states[0].shape, BF16)],
        ),
        out_shape=[
            pltpu.VMEM((tokens, features), BF16),
            pltpu.VMEM((tile + sum_rows(tile), LANES), BF16),
        ],
        input_output_aliases={8 + len(states): 0} if more else {},
        compiler_params=params(),
        cost_estimate=pl.CostEstimate(flops=0, bytes_accessed=0, transcendentals=0),
        name="combine",
    )(*docs, c_sel, reach, part, gate, *held, *more)


def finish_kernel(tile, all_features, len_ref, lang_ref, mine_ref, other_ref, gated_ref, up_ref, out_hbm, out_ref, sems):
    features = gated_ref.shape[1]
    ranks = up_ref.shape[1]
    starts = starts_of(len_ref)
    langs = [lang_ref[d] for d in range(lang_ref.shape[0])]
    odd = lax.axis_index("head") % 2
    piece = min(4 * LANES, features)
    tokens = tile

    def copy_of(step, i):
        at = step * tokens
        here = pl.ds(pl.multiple_of(i * piece, LANES), piece)
        return pltpu.make_async_copy(
            out_ref.at[pl.ds(at, tokens), here],
            out_hbm.at[pl.ds(at, tokens), here],
            sems.at[step * (features // piece) + i],
        )

    def block(step):
        is_mine = odd == step
        now = pl.ds(step * tokens, tokens)
        scale = jnp.where(is_mine, mine_ref[tile:, :].astype(F32), other_ref[tile:, :].astype(F32))
        scale = lax.rsqrt(scale / all_features + EPS)
        turned = jnp.concatenate([scale] * (LANES // sum_rows(tile)), axis=0).T
        scale = jnp.concatenate([turned[:, 4 * c:4 * c + 1] for c in range(tokens // LANES)], axis=0)
        low = jnp.where(is_mine, mine_ref[0:tokens, :].astype(F32), other_ref[0:tokens, :].astype(F32))
        low = (low * scale).astype(BF16)
        first = (lax.axis_index("seq") * 2 + step) * tokens
        lang = lang_at(first, starts, langs)
        other, few = other_language(lang, first, tokens, starts, langs)
        token_lang = lang_at(first + lax.broadcasted_iota(I32, (tokens, LANES), 0), starts, langs)
        zero = jnp.zeros((), BF16)

        @pl.when(few)
        def _():
            spread = jnp.concatenate([
                jnp.where(token_lang == lang, low, zero),
                jnp.where(token_lang != lang, low, zero),
            ], axis=1)
            for begin in range(0, features, piece):
                here = slice(begin, begin + piece)
                lifted = dot(spread, jnp.concatenate([up_ref[lang, :, here], up_ref[other, :, here]], axis=0))
                out_ref[now, here] = (gated_ref[now, here].astype(F32) * scale + lifted).astype(BF16)
                copy_of(step, begin // piece).start()

        @pl.when(jnp.logical_not(few))
        def _():
            spread = jnp.concatenate([jnp.where(token_lang == k, low, zero) for k in range(up_ref.shape[0])], axis=1)

            def column_piece(i, _):
                here = pl.ds(pl.multiple_of(i * piece, LANES), piece)
                lifted = dot(spread, up_ref[:, :, here].reshape(up_ref.shape[0] * ranks, piece))
                out_ref[now, here] = (gated_ref[now, here].astype(F32) * scale + lifted).astype(BF16)
                copy_of(step, i).start()
                return 0

            lax.fori_loop(0, features // piece, column_piece, 0)

    for step in range(2):
        block(step)
    for step in range(2):
        for i in range(features // piece):
            copy_of(step, i).wait()


def finish(docs, mine, other, gated, up, all_features):
    tokens, features = gated.shape
    tile = tokens // 2
    held = [pltpu.with_memory_space_constraint(v, pltpu.VMEM) for v in (mine, other, gated, up)]
    return pl.pallas_call(
        functools.partial(finish_kernel, tile, all_features),
        grid_spec=pltpu.PrefetchScalarGridSpec(
            num_scalar_prefetch=2,
            grid=(1,),
            in_specs=[in_vmem()] * 4,
            out_specs=pl.BlockSpec(memory_space=pl.ANY),
            scratch_shapes=[
                pltpu.VMEM(gated.shape, BF16),
                pltpu.SemaphoreType.DMA((2 * (features // min(4 * LANES, features)),)),
            ],
        ),
        out_shape=pltpu.HBM(gated.shape, BF16),
        compiler_params=params(),
        name="finish",
    )(*docs, *held)


def sum_over_head(mine, sent, across, devices):
    total = (mine.astype(F32) + sent.astype(F32)).astype(BF16)
    bit = 2
    while bit < devices:
        masks = [bit] if 2 * bit >= devices else [2 * bit, bit, 3 * bit]
        added = total.astype(F32)
        for arrived in [across(total, m) for m in masks]:
            added = added + arrived.astype(F32)
        total = added.astype(BF16)
        bit *= 2 ** (1 if len(masks) == 1 else 2)
    return total, across(total, 1)


def run(seq_size, head_size, relayed, x_in, z_gate, b_input, c_input, dt_raw, a_log, d_skip, norm_gain,
        doc_lengths, doc_lang, adapt_down, adapt_up):
    tokens, features = x_in.shape
    heads = dt_raw.shape[0]
    groups = b_input.shape[1]
    b_rows = b_input.reshape(tokens * groups, b_input.shape[2])
    c_rows = c_input.reshape(tokens * groups, c_input.shape[2])
    docs = (doc_lengths, doc_lang)
    gain = norm_gain.reshape(1, features)
    all_features = features * head_size
    slot = max(8, heads)
    onward = [(i, i + 1) for i in range(seq_size - 1)]

    state, through, b_sel, b_turned, x_held, *decays = block_states(head_size, doc_lengths, a_log, dt_raw, b_rows, x_in)
    state, z_gate, c_rows = lax.optimization_barrier((state, z_gate, c_rows))
    arrived = lax.ppermute(state, "seq", onward)
    part, gate, c_sel = local_scan(head_size, doc_lengths, d_skip, b_sel, b_turned, decays, c_rows, x_held, z_gate)
    reach = decays[0]
    arrived, part = lax.optimization_barrier((arrived, part))
    states = [arrived]
    for _ in range(1, hops_of(tokens, seq_size) if relayed else 1):
        arrived = lax.ppermute((arrived.astype(F32) * through[0:1]).astype(BF16), "seq", onward)
        states.append(arrived)

    def across(v, mask):
        return lax.ppermute(v, "head", [(i, i ^ mask) for i in range(head_size)])

    shared = (docs, c_sel, reach, part, gate, gain, adapt_down, states, slot)
    gated, theirs = combine(*shared, False)
    sent = across(theirs, 1)
    gated, mine = combine(*shared, True, gated)
    mine, other = sum_over_head(mine, sent, across, head_size)
    return finish(docs, mine, other, gated, adapt_up, all_features)


def longest_of(tokens, seq_size):
    return tokens * seq_size // LONGEST_SHARE


def hops_of(tokens, seq_size):
    return min(-(-(longest_of(tokens, seq_size) - 1) // tokens), seq_size - 1)


def covered_kernel(tokens, seq_size, len_ref, out_ref):
    found, at = jnp.int32(0), jnp.int32(0)
    for d in range(len_ref.shape[0]):
        end = at + len_ref[d]
        for block in range(1, seq_size - 1):
            found = jnp.where((at < block * tokens) & (end > (block + 1) * tokens), 1, found)
        at = end
    out_ref[0] = found


def per_device(seq_size, head_size, *args):
    tokens = args[0].shape[0]
    doc_lengths = args[8]
    if hops_of(tokens, seq_size) < 2:
        return run(seq_size, head_size, False, *args)
    covered = pl.pallas_call(
        functools.partial(covered_kernel, tokens, seq_size),
        in_specs=[pl.BlockSpec(memory_space=pltpu.SMEM)],
        out_specs=pl.BlockSpec(memory_space=pltpu.SMEM),
        out_shape=pltpu.SMEM((1,), I32),
        name="covered",
    )(doc_lengths)[0] > 0
    return lax.cond(
        covered,
        functools.partial(run, seq_size, head_size, True),
        functools.partial(run, seq_size, head_size, False),
        *args,
    )


def solution(mesh):
    placed = (
        P("seq", "head"),
        P("seq", "head"),
        P("seq", None, None),
        P("seq", None, None),
        P("head", "seq"),
        P("head"),
        P("head"),
        P("head"),
        P(),
        P(),
        P(None, "head", None),
        P(None, None, "head"),
    )
    return jax.shard_map(
        functools.partial(per_device, mesh.shape["seq"], mesh.shape["head"]),
        mesh=mesh, in_specs=placed, out_specs=P("seq", "head"), check_vma=False,
    )
```

```python
import functools

import jax
import jax.numpy as jnp
from jax import lax
from jax.experimental import pallas as pl
from jax.experimental.pallas import tpu as pltpu
from jax.sharding import PartitionSpec as P

F32 = jnp.float32
BF16 = jnp.bfloat16
I32 = jnp.int32
LOG2E = 1.4426950408889634
EPS = 1e-05
LANES = 128
LONGEST_SHARE = 3
VMEM_LIMIT = 16 * 1024 * 1024


def params():
    return pltpu.CompilerParams(vmem_limit_bytes=VMEM_LIMIT)


def starts_of(docs):
    starts, at = [], jnp.int32(0)
    for d in range(docs.shape[0] // 2):
        starts.append(at)
        at = at + docs[d]
    return starts


def doc_at(pos, starts):
    found = jnp.where(pos >= starts[0], 0, -1)
    for s in starts[1:]:
        found = found + jnp.where(pos >= s, 1, 0)
    return found


def lang_at(pos, starts, lang_ref):
    found = jnp.where(pos >= 0, lang_ref[0], 0)
    for d in range(1, len(starts)):
        found = jnp.where(pos >= starts[d], lang_ref[d], found)
    return found


def rates(alog_ref, rows):
    which = lax.broadcasted_iota(I32, (rows, LANES), 0)
    column = jnp.zeros((rows, LANES), F32)
    for h in range(rows):
        column = jnp.where(which == h, alog_ref[h], column)
    return -LOG2E * jnp.exp(column)


def softplus(v):
    return jnp.maximum(v, 0.0) + jnp.log(1.0 + jnp.exp(-jnp.abs(v)))


def running(v, back):
    width = v.shape[1]
    lane = lax.broadcasted_iota(I32, v.shape, 1)
    step = 1
    while step < width:
        if back:
            v = v + jnp.where(lane + step < width, pltpu.roll(v, width - step, 1), 0.0)
        else:
            v = v + jnp.where(lane >= step, pltpu.roll(v, step, 1), 0.0)
        step *= 2
    return v


def pick_matrix(group, groups):
    shape = (LANES, LANES * groups)
    row = lax.broadcasted_iota(I32, shape, 0)
    col = lax.broadcasted_iota(I32, shape, 1)
    return jnp.where(col == row * groups + group, 1.0, 0.0).astype(BF16)


def dot(a, b):
    return jnp.dot(a, b, preferred_element_type=F32)


def group_of(head_rank, heads, head_size, groups):
    return head_rank * heads // (heads * head_size // groups)


def state_kernel(head_size, len_hbm, lang_hbm, alog_hbm, dt_hbm, b_hbm, x_hbm, state_ref, thr_ref, bsel_ref, bt_ref, x_ref,
                 reach_ref, before_ref, fresh_ref, kept_ref, docs_ref, len_ref, lang_ref, alog_ref, dt_ref, b_ref, w_ref, all_ref, stack_ref, sems):
    heads, tokens = dt_ref.shape
    groups = b_ref.shape[0] // tokens
    copies = [
        pltpu.make_async_copy(source, target, sems.at[i])
        for i, (source, target) in enumerate([
            (dt_hbm, dt_ref), (len_hbm, len_ref), (lang_hbm, lang_ref), (alog_hbm, alog_ref), (b_hbm, b_ref), (x_hbm, x_ref),
        ])
    ]
    for copy in copies:
        copy.start()
    for copy in copies[:4]:
        copy.wait()
    count = len_ref.shape[0]
    for d in range(count):
        docs_ref[d] = len_ref[d]
        docs_ref[count + d] = lang_ref[d]

    starts = starts_of(docs_ref)
    base = lax.axis_index("seq") * tokens
    rate = rates(alog_ref, heads)
    parts, totals = [], []
    for c in range(tokens // LANES):
        step_dt = softplus(dt_ref[:, c * LANES:(c + 1) * LANES])
        decay = step_dt * rate
        after = running(decay, True)
        parts.append((step_dt, after - decay))
        totals.append(after[:, 0:1])
    last_doc = doc_at(base + tokens - 1, starts)
    first_doc = doc_at(base - 1, starts)
    later = jnp.zeros((heads, 1), F32)
    for c in reversed(range(tokens // LANES)):
        step_dt, inside = parts[c]
        pos = base + c * LANES + lax.broadcasted_iota(I32, (heads, LANES), 1)
        alive = doc_at(pos, starts) == last_doc
        w_ref[:, c * LANES:(c + 1) * LANES] = jnp.where(alive, jnp.exp2(inside + later) * step_dt, 0.0)
        later = later + totals[c]
    kept = jnp.where(last_doc == first_doc, 1.0, 0.0)
    all_ref[...] = jnp.broadcast_to(jnp.exp2(later) * kept, all_ref.shape)
    for h in range(heads):
        thr_ref[:, h * LANES:(h + 1) * LANES] = jnp.broadcast_to(all_ref[h:h + 1, :], (8, LANES))

    slot = max(8, heads)
    stack_ref[...] = jnp.zeros_like(stack_ref)
    past = jnp.zeros((heads, LANES), F32)
    for c in range(tokens // LANES):
        here = slice(c * LANES, (c + 1) * LANES)
        first = base + c * LANES
        step_dt = parts[c][0]
        total_to = running(step_dt * rate, False)
        chunk_total = jnp.broadcast_to(total_to[:, LANES - 1:LANES], (heads, LANES))
        before_ref[:, here] = total_to - jnp.log(step_dt) * LOG2E
        doc = doc_at(first + lax.broadcasted_iota(I32, (heads, LANES), 1), starts)
        doc_in = doc_at(first - 1, starts)
        doc_out = doc_at(first + LANES - 1, starts)
        fresh_ref[:, here] = jnp.where(doc == doc_out, jnp.exp2(chunk_total - total_to) * step_dt, 0.0)
        kept_ref[c] = jnp.exp2(chunk_total) * jnp.where(doc_in == doc_out, 1.0, 0.0)
        stack_ref[c, 0:heads, :] = total_to
        stack_ref[c, slot:slot + heads, :] = jnp.where(doc == doc_in, jnp.exp2(total_to), 0.0)
        stack_ref[c, 2 * slot:2 * slot + heads, :] = jnp.where(doc == first_doc, jnp.exp2(past + total_to), 0.0)
        past = past + chunk_total
        reach_ref[here, :] = stack_ref[c].T

    pick = pick_matrix(group_of(lax.axis_index("head"), heads, head_size, groups), groups)
    copies[4].wait()
    for c in range(tokens // LANES):
        here = slice(c * LANES, (c + 1) * LANES)
        chosen = dot(pick, b_ref[c * LANES * groups:(c + 1) * LANES * groups, :])
        bsel_ref[here, :] = chosen.astype(BF16)
        bt_ref[:, here] = chosen.T.astype(BF16)

    copies[5].wait()
    for h in range(heads):
        here = slice(h * LANES, (h + 1) * LANES)
        weighted = bt_ref[...] * w_ref[h:h + 1, :].astype(BF16)
        state_ref[:, here] = dot(weighted, x_ref[:, here]).astype(BF16)


def in_smem():
    return pl.BlockSpec(memory_space=pltpu.SMEM)


def in_vmem():
    return pl.BlockSpec(memory_space=pltpu.VMEM)


def block_states(head_size, doc_lengths, doc_lang, a_log, dt_raw, b_rows, x_in):
    heads, tokens = dt_raw.shape
    features = x_in.shape[1]
    return pl.pallas_call(
        functools.partial(state_kernel, head_size),
        grid_spec=pltpu.PrefetchScalarGridSpec(
            num_scalar_prefetch=0,
            grid=(1,),
            in_specs=[pl.BlockSpec(memory_space=pl.ANY)] * 6,
            out_specs=[in_vmem()] * 9 + [in_smem()],
            scratch_shapes=[
                pltpu.SMEM(doc_lengths.shape, I32),
                pltpu.SMEM(doc_lang.shape, I32),
                pltpu.SMEM(a_log.shape, F32),
                pltpu.VMEM((heads, tokens), F32),
                pltpu.VMEM(b_rows.shape, BF16),
                pltpu.VMEM((heads, tokens), F32),
                pltpu.VMEM((heads, LANES), F32),
                pltpu.VMEM((tokens // LANES, LANES, LANES), F32),
                pltpu.SemaphoreType.DMA((6,)),
            ],
        ),
        out_shape=[
            pltpu.VMEM((LANES, features), BF16),
            pltpu.VMEM((8, features), F32),
            pltpu.VMEM((tokens, LANES), BF16),
            pltpu.VMEM((LANES, tokens), BF16),
            pltpu.VMEM((tokens, features), BF16),
            pltpu.VMEM((tokens, LANES), F32),
            pltpu.VMEM((heads, tokens), F32),
            pltpu.VMEM((heads, tokens), F32),
            pltpu.VMEM((tokens // LANES, heads, LANES), F32),
            pltpu.SMEM((2 * doc_lengths.shape[0],), I32),
        ],
        compiler_params=params(),
        cost_estimate=pl.CostEstimate(flops=2 * LANES * tokens * features, bytes_accessed=8 * tokens * features, transcendentals=0),
        name="block_states",
    )(*[pltpu.with_memory_space_constraint(v, pltpu.HBM) for v in (doc_lengths, doc_lang, a_log, dt_raw, b_rows, x_in)])


def scan_kernel(head_size, skip_ref, docs, b_ref, bt_ref, reach_ref, before_ref, fresh_ref, kept_ref, c_ref, x_ref, z_ref,
                part_ref, gate_ref, csel_ref, state_ref, scores_ref):
    step = pl.program_id(0)
    heads, tokens = before_ref.shape
    groups = c_ref.shape[0] // tokens
    slot = max(8, heads)

    @pl.when(step == 0)
    def _():
        state_ref[...] = jnp.zeros_like(state_ref)
        starts = starts_of(docs)
        block = lax.axis_index("seq") * tokens
        pick = pick_matrix(group_of(lax.axis_index("head"), heads, head_size, groups), groups)
        for c in range(tokens // LANES):
            here = slice(c * LANES, (c + 1) * LANES)
            base = block + c * LANES
            row_pos = base + lax.broadcasted_iota(I32, (LANES, LANES), 0)
            col_pos = base + lax.broadcasted_iota(I32, (LANES, LANES), 1)
            keep = (row_pos >= col_pos) & (doc_at(row_pos, starts) == doc_at(col_pos, starts))
            c_low = dot(pick, c_ref[c * LANES * groups:(c + 1) * LANES * groups, :]).astype(BF16)
            csel_ref[here, :] = c_low
            scores = lax.dot_general(c_low, b_ref[here, :], (((1,), (1,)), ((), ())), preferred_element_type=F32)
            scores_ref[c] = jnp.where(keep, scores, 0.0)

    now = pl.ds(pl.multiple_of(step * LANES, LANES), LANES)
    columns = reach_ref[now, :]
    chosen = csel_ref[now, :]
    before = before_ref[:, now]
    fresh = fresh_ref[:, now].astype(BF16)
    kept = kept_ref[step]
    scores = scores_ref[step]
    b_turned = bt_ref[:, now]

    for h in range(heads):
        here = slice(h * LANES, (h + 1) * LANES)
        gaps = jnp.minimum(columns[:, h:h + 1] - before[h:h + 1, :], 80.0)
        weights = (jnp.exp2(gaps) * scores).astype(BF16)
        carried = chosen * columns[:, slot + h:slot + h + 1].astype(BF16)
        x_head = x_ref[now, here]
        state = state_ref[:, here]
        out = dot(jnp.concatenate([weights, carried], axis=1), jnp.concatenate([x_head, state.astype(BF16)], axis=0))
        out = out + skip_ref[h] * x_head.astype(F32)
        written = dot(b_turned * fresh[h:h + 1, :], x_head)
        state_ref[:, here] = state * kept[h:h + 1, :] + written
        z = 0.5 * z_ref[now, here].astype(F32)
        gate = z + z * jnp.tanh(z)
        part_ref[now, here] = out * gate
        gate_ref[now, here] = gate.astype(BF16)


def local_scan(head_size, docs, d_skip, b_sel, b_turned, decays, c_rows, x_in, z_gate):
    tokens, features = x_in.shape
    chunks = tokens // LANES
    held = [pltpu.with_memory_space_constraint(v, pltpu.VMEM) for v in (c_rows, z_gate)]
    return pl.pallas_call(
        functools.partial(scan_kernel, head_size),
        grid_spec=pltpu.PrefetchScalarGridSpec(
            num_scalar_prefetch=1,
            grid=(chunks,),
            in_specs=[in_smem()] + [in_vmem()] * 9,
            out_specs=[in_vmem()] * 3,
            scratch_shapes=[
                pltpu.VMEM((LANES, features), F32),
                pltpu.VMEM((chunks, LANES, LANES), F32),
            ],
        ),
        out_shape=[
            pltpu.VMEM((tokens, features), F32),
            pltpu.VMEM((tokens, features), BF16),
            pltpu.VMEM((tokens, LANES), BF16),
        ],
        compiler_params=params(),
        cost_estimate=pl.CostEstimate(flops=16 * LANES * tokens * features, bytes_accessed=8 * tokens * features, transcendentals=0),
        name="local_scan",
    )(d_skip, docs, b_sel, b_turned, *decays, held[0], x_in, held[1])


def other_language(lang, first, size, starts, langs):
    other = lang
    few = jnp.bool_(True)
    for d, s in enumerate(starts):
        inside = (s > first) & (s < first + size) & (langs[d] != lang)
        few = few & jnp.logical_not(inside & (other != lang) & (langs[d] != other))
        other = jnp.where(inside & (other == lang), langs[d], other)
    return other, few


def has_language(which, first, size, starts, lang_ref):
    found = lang_at(first, starts, lang_ref) == which
    for d, s in enumerate(starts):
        found = found | ((s > first) & (s < first + size) & (lang_ref[d] == which))
    return found


def sum_rows(tile):
    return -(-4 * (tile // LANES) // 16) * 16


def combine_kernel(n_states, slot, tile, mine, docs, c_ref, reach_ref, part_ref, gate_ref, gain_ref, down_ref, *rest):
    states, (gated_ref, ref, enter_ref) = rest[:n_states], rest[-3:]
    features = part_ref.shape[1]
    heads = features // LANES
    starts = starts_of(docs)
    langs = [docs[len(starts) + d] for d in range(len(starts))]
    entering = states[0]
    if n_states > 1:
        total = states[0][...].astype(F32)
        for more in states[1:]:
            total = total + more[...].astype(F32)
        enter_ref[...] = total.astype(BF16)
        entering = enter_ref

    odd = lax.axis_index("head") % 2
    half = odd if mine else 1 - odd
    pair = min(2, heads)
    at = pl.multiple_of(half * tile, LANES)
    now = pl.ds(at, tile)
    first = lax.axis_index("seq") * part_ref.shape[0] + at
    lang = lang_at(first, starts, langs)
    other, few = other_language(lang, first, tile, starts, langs)
    squares = jnp.zeros((tile, LANES), F32)
    c_low = c_ref[now, :]
    reach = reach_ref[now, :]
    for p in range(heads // pair):
        both = dot(c_low, entering[:, p * pair * LANES:(p + 1) * pair * LANES])
        for i in range(pair):
            h = p * pair + i
            here = slice(h * LANES, (h + 1) * LANES)
            entered = both[:, i * LANES:(i + 1) * LANES] * reach[:, 2 * slot + h:2 * slot + h + 1]
            gated = part_ref[now, here] + entered * gate_ref[now, here].astype(F32)
            squares = squares + gated * gated
            gated_ref[now, here] = (gated * gain_ref[:, here]).astype(BF16)
    token_lang = lang_at(first + lax.broadcasted_iota(I32, (tile, LANES), 0), starts, langs)
    both = dot(gated_ref[now, :], jnp.concatenate([down_ref[lang], down_ref[other]], axis=1))
    ref[0:tile, :] = jnp.where(token_lang == lang, both[:, :LANES], both[:, LANES:]).astype(BF16)

    ones = jnp.ones((8, LANES), BF16)
    whole = squares.astype(BF16)
    rest_of = (squares - whole.astype(F32)).astype(BF16)
    turned = (((1,), (1,)), ((), ()))
    sums = lax.dot_general(ones, whole, turned, preferred_element_type=F32) + lax.dot_general(ones, rest_of, turned, preferred_element_type=F32)
    rows = [sums[:, c * LANES:(c + 1) * LANES] for c in range(tile // LANES)]
    rows += rows[:1] * (sum_rows(tile) // 4 - len(rows))
    upper = lax.broadcasted_iota(I32, (8, LANES), 0) < 4
    rows = jnp.concatenate([jnp.where(upper, a, b) for a, b in zip(rows[0::2], rows[1::2])], axis=0)
    ref[tile:tile + sum_rows(tile), :] = rows.astype(BF16)

    @pl.when(jnp.logical_not(few))
    def _():
        token_lang = lang_at(first + lax.broadcasted_iota(I32, (tile, LANES), 0), starts, langs)
        for k in range(down_ref.shape[0]):
            @pl.when(has_language(k, first, tile, starts, langs) & (lang != k) & (other != k))
            def _():
                low = dot(gated_ref[now, :], down_ref[k])
                ref[0:tile, :] = jnp.where(token_lang == k, low, ref[0:tile, :].astype(F32)).astype(BF16)


def combine(docs, c_sel, reach, part, gate, gain, down, states, slot, mine, into=None):
    tokens, features = part.shape
    tile = tokens // 2
    held = [pltpu.with_memory_space_constraint(v, pltpu.VMEM) for v in [gain, down] + states]
    more = [] if into is None else [into]
    return pl.pallas_call(
        functools.partial(combine_kernel, len(states), slot, tile, mine),
        grid_spec=pltpu.PrefetchScalarGridSpec(
            num_scalar_prefetch=0,
            grid=(1,),
            in_specs=[in_smem()] + [in_vmem()] * (6 + len(states)) + [pl.BlockSpec(memory_space=pl.ANY) for _ in more],
            out_specs=[in_vmem()] * 2,
            scratch_shapes=[pltpu.VMEM(states[0].shape, BF16)],
        ),
        out_shape=[
            pltpu.VMEM((tokens, features), BF16),
            pltpu.VMEM((tile + sum_rows(tile), LANES), BF16),
        ],
        input_output_aliases={7 + len(states): 0} if more else {},
        compiler_params=params(),
        cost_estimate=pl.CostEstimate(flops=0, bytes_accessed=0, transcendentals=0),
        name="combine",
    )(docs, c_sel, reach, part, gate, *held, *more)


def finish_kernel(tile, all_features, docs, mine_ref, other_ref, gated_ref, up_ref, out_hbm, out_ref, sems):
    features = gated_ref.shape[1]
    ranks = up_ref.shape[1]
    starts = starts_of(docs)
    langs = [docs[len(starts) + d] for d in range(len(starts))]
    odd = lax.axis_index("head") % 2
    piece = min(4 * LANES, features)
    tokens = tile

    def copy_of(step, i):
        at = step * tokens
        here = pl.ds(pl.multiple_of(i * piece, LANES), piece)
        return pltpu.make_async_copy(
            out_ref.at[pl.ds(at, tokens), here],
            out_hbm.at[pl.ds(at, tokens), here],
            sems.at[step * (features // piece) + i],
        )

    def block(step):
        is_mine = odd == step
        now = pl.ds(step * tokens, tokens)
        scale = jnp.where(is_mine, mine_ref[tile:, :].astype(F32), other_ref[tile:, :].astype(F32))
        scale = lax.rsqrt(scale / all_features + EPS)
        turned = jnp.concatenate([scale] * (LANES // sum_rows(tile)), axis=0).T
        scale = jnp.concatenate([turned[:, 4 * c:4 * c + 1] for c in range(tokens // LANES)], axis=0)
        low = jnp.where(is_mine, mine_ref[0:tokens, :].astype(F32), other_ref[0:tokens, :].astype(F32))
        low = (low * scale).astype(BF16)
        first = (lax.axis_index("seq") * 2 + step) * tokens
        lang = lang_at(first, starts, langs)
        other, few = other_language(lang, first, tokens, starts, langs)
        token_lang = lang_at(first + lax.broadcasted_iota(I32, (tokens, LANES), 0), starts, langs)
        zero = jnp.zeros((), BF16)

        @pl.when(few)
        def _():
            spread = jnp.concatenate([
                jnp.where(token_lang == lang, low, zero),
                jnp.where(token_lang != lang, low, zero),
            ], axis=1)
            for begin in range(0, features, piece):
                here = slice(begin, begin + piece)
                lifted = dot(spread, jnp.concatenate([up_ref[lang, :, here], up_ref[other, :, here]], axis=0))
                out_ref[now, here] = (gated_ref[now, here].astype(F32) * scale + lifted).astype(BF16)
                copy_of(step, begin // piece).start()

        @pl.when(jnp.logical_not(few))
        def _():
            spread = jnp.concatenate([jnp.where(token_lang == k, low, zero) for k in range(up_ref.shape[0])], axis=1)

            def column_piece(i, _):
                here = pl.ds(pl.multiple_of(i * piece, LANES), piece)
                lifted = dot(spread, up_ref[:, :, here].reshape(up_ref.shape[0] * ranks, piece))
                out_ref[now, here] = (gated_ref[now, here].astype(F32) * scale + lifted).astype(BF16)
                copy_of(step, i).start()
                return 0

            lax.fori_loop(0, features // piece, column_piece, 0)

    for step in range(2):
        block(step)
    for step in range(2):
        for i in range(features // piece):
            copy_of(step, i).wait()


def finish(docs, mine, other, gated, up, all_features):
    tokens, features = gated.shape
    tile = tokens // 2
    held = [pltpu.with_memory_space_constraint(v, pltpu.VMEM) for v in (mine, other, gated, up)]
    return pl.pallas_call(
        functools.partial(finish_kernel, tile, all_features),
        grid_spec=pltpu.PrefetchScalarGridSpec(
            num_scalar_prefetch=0,
            grid=(1,),
            in_specs=[in_smem()] + [in_vmem()] * 4,
            out_specs=pl.BlockSpec(memory_space=pl.ANY),
            scratch_shapes=[
                pltpu.VMEM(gated.shape, BF16),
                pltpu.SemaphoreType.DMA((2 * (features // min(4 * LANES, features)),)),
            ],
        ),
        out_shape=pltpu.HBM(gated.shape, BF16),
        compiler_params=params(),
        name="finish",
    )(docs, *held)


def sum_over_head(mine, sent, across, devices):
    total = (mine.astype(F32) + sent.astype(F32)).astype(BF16)
    bit = 2
    while bit < devices:
        masks = [bit] if 2 * bit >= devices else [2 * bit, bit, 3 * bit]
        added = total.astype(F32)
        for arrived in [across(total, m) for m in masks]:
            added = added + arrived.astype(F32)
        total = added.astype(BF16)
        bit *= 2 ** (1 if len(masks) == 1 else 2)
    return total, across(total, 1)


def run(seq_size, head_size, relayed, x_in, z_gate, b_input, c_input, dt_raw, a_log, d_skip, norm_gain,
        doc_lengths, doc_lang, adapt_down, adapt_up):
    tokens, features = x_in.shape
    heads = dt_raw.shape[0]
    groups = b_input.shape[1]
    b_rows = b_input.reshape(tokens * groups, b_input.shape[2])
    c_rows = c_input.reshape(tokens * groups, c_input.shape[2])
    gain = norm_gain.reshape(1, features)
    all_features = features * head_size
    slot = max(8, heads)
    onward = [(i, i + 1) for i in range(seq_size - 1)]

    state, through, b_sel, b_turned, x_held, *decays, docs = block_states(head_size, doc_lengths, doc_lang, a_log, dt_raw, b_rows, x_in)
    state, z_gate, c_rows = lax.optimization_barrier((state, z_gate, c_rows))
    arrived = lax.ppermute(state, "seq", onward)
    part, gate, c_sel = local_scan(head_size, docs, d_skip, b_sel, b_turned, decays, c_rows, x_held, z_gate)
    reach = decays[0]
    arrived, part = lax.optimization_barrier((arrived, part))
    states = [arrived]
    for _ in range(1, hops_of(tokens, seq_size) if relayed else 1):
        arrived = lax.ppermute((arrived.astype(F32) * through[0:1]).astype(BF16), "seq", onward)
        states.append(arrived)

    def across(v, mask):
        return lax.ppermute(v, "head", [(i, i ^ mask) for i in range(head_size)])

    shared = (docs, c_sel, reach, part, gate, gain, adapt_down, states, slot)
    gated, theirs = combine(*shared, False)
    sent = across(theirs, 1)
    gated, mine = combine(*shared, True, gated)
    mine, other = sum_over_head(mine, sent, across, head_size)
    return finish(docs, mine, other, gated, adapt_up, all_features)


def longest_of(tokens, seq_size):
    return tokens * seq_size // LONGEST_SHARE


def hops_of(tokens, seq_size):
    return min(-(-(longest_of(tokens, seq_size) - 1) // tokens), seq_size - 1)


def covered_kernel(tokens, seq_size, len_ref, out_ref):
    found, at = jnp.int32(0), jnp.int32(0)
    for d in range(len_ref.shape[0]):
        end = at + len_ref[d]
        for block in range(1, seq_size - 1):
            found = jnp.where((at < block * tokens) & (end > (block + 1) * tokens), 1, found)
        at = end
    out_ref[0] = found


def per_device(seq_size, head_size, *args):
    tokens = args[0].shape[0]
    doc_lengths = args[8]
    if hops_of(tokens, seq_size) < 2:
        return run(seq_size, head_size, False, *args)
    covered = pl.pallas_call(
        functools.partial(covered_kernel, tokens, seq_size),
        in_specs=[pl.BlockSpec(memory_space=pltpu.SMEM)],
        out_specs=pl.BlockSpec(memory_space=pltpu.SMEM),
        out_shape=pltpu.SMEM((1,), I32),
        name="covered",
    )(doc_lengths)[0] > 0
    return lax.cond(
        covered,
        functools.partial(run, seq_size, head_size, True),
        functools.partial(run, seq_size, head_size, False),
        *args,
    )


def solution(mesh):
    placed = (
        P("seq", "head"),
        P("seq", "head"),
        P("seq", None, None),
        P("seq", None, None),
        P("head", "seq"),
        P("head"),
        P("head"),
        P("head"),
        P(),
        P(),
        P(None, "head", None),
        P(None, None, "head"),
    )
    return jax.shard_map(
        functools.partial(per_device, mesh.shape["seq"], mesh.shape["head"]),
        mesh=mesh, in_specs=placed, out_specs=P("seq", "head"), check_vma=False,
    )
```

```python
import functools

import jax
import jax.numpy as jnp
from jax import lax
from jax.experimental import pallas as pl
from jax.experimental.pallas import tpu as pltpu
from jax.sharding import PartitionSpec as P

F32 = jnp.float32
BF16 = jnp.bfloat16
I32 = jnp.int32
LOG2E = 1.4426950408889634
EPS = 1e-05
LANES = 128
LONGEST_SHARE = 3
VMEM_LIMIT = 16 * 1024 * 1024


def params():
    return pltpu.CompilerParams(vmem_limit_bytes=VMEM_LIMIT)


def starts_of(docs):
    starts, at = [], jnp.int32(0)
    for d in range(docs.shape[0] // 2):
        starts.append(at)
        at = at + docs[d]
    return starts


def doc_at(pos, starts):
    found = jnp.where(pos >= starts[0], 0, -1)
    for s in starts[1:]:
        found = found + jnp.where(pos >= s, 1, 0)
    return found


def lang_at(pos, starts, lang_ref):
    found = jnp.where(pos >= 0, lang_ref[0], 0)
    for d in range(1, len(starts)):
        found = jnp.where(pos >= starts[d], lang_ref[d], found)
    return found


def rates(alog_ref, rows):
    which = lax.broadcasted_iota(I32, (rows, LANES), 0)
    column = jnp.zeros((rows, LANES), F32)
    for h in range(rows):
        column = jnp.where(which == h, alog_ref[h], column)
    return -LOG2E * jnp.exp(column)


def softplus(v):
    return jnp.maximum(v, 0.0) + jnp.log(1.0 + jnp.exp(-jnp.abs(v)))


def running(v, back):
    width = v.shape[1]
    lane = lax.broadcasted_iota(I32, v.shape, 1)
    step = 1
    while step < width:
        if back:
            v = v + jnp.where(lane + step < width, pltpu.roll(v, width - step, 1), 0.0)
        else:
            v = v + jnp.where(lane >= step, pltpu.roll(v, step, 1), 0.0)
        step *= 2
    return v


def pick_matrix(group, groups):
    shape = (LANES, LANES * groups)
    row = lax.broadcasted_iota(I32, shape, 0)
    col = lax.broadcasted_iota(I32, shape, 1)
    return jnp.where(col == row * groups + group, 1.0, 0.0).astype(BF16)


def dot(a, b):
    return jnp.dot(a, b, preferred_element_type=F32)


def group_of(head_rank, heads, head_size, groups):
    return head_rank * heads // (heads * head_size // groups)


def state_kernel(head_size, len_hbm, lang_hbm, alog_hbm, dt_hbm, b_hbm, x_hbm, state_ref, thr_ref, bsel_ref, bt_ref, x_ref,
                 reach_ref, before_ref, fresh_ref, kept_ref, docs_ref, len_ref, lang_ref, alog_ref, dt_ref, b_ref, w_ref, all_ref, stack_ref, sems):
    heads, tokens = dt_ref.shape
    groups = b_ref.shape[0] // tokens
    copies = [
        pltpu.make_async_copy(source, target, sems.at[i])
        for i, (source, target) in enumerate([
            (dt_hbm, dt_ref), (len_hbm, len_ref), (lang_hbm, lang_ref), (alog_hbm, alog_ref), (b_hbm, b_ref), (x_hbm, x_ref),
        ])
    ]
    for copy in copies:
        copy.start()
    for copy in copies[:4]:
        copy.wait()
    count = len_ref.shape[0]
    for d in range(count):
        docs_ref[d] = len_ref[d]
        docs_ref[count + d] = lang_ref[d]

    starts = starts_of(docs_ref)
    base = lax.axis_index("seq") * tokens
    rate = rates(alog_ref, heads)
    parts, totals = [], []
    for c in range(tokens // LANES):
        step_dt = softplus(dt_ref[:, c * LANES:(c + 1) * LANES])
        decay = step_dt * rate
        after = running(decay, True)
        parts.append((step_dt, after - decay))
        totals.append(after[:, 0:1])
    last_doc = doc_at(base + tokens - 1, starts)
    first_doc = doc_at(base - 1, starts)
    later = jnp.zeros((heads, 1), F32)
    for c in reversed(range(tokens // LANES)):
        step_dt, inside = parts[c]
        pos = base + c * LANES + lax.broadcasted_iota(I32, (heads, LANES), 1)
        alive = doc_at(pos, starts) == last_doc
        w_ref[:, c * LANES:(c + 1) * LANES] = jnp.where(alive, jnp.exp2(inside + later) * step_dt, 0.0)
        later = later + totals[c]
    kept = jnp.where(last_doc == first_doc, 1.0, 0.0)
    all_ref[...] = jnp.broadcast_to(jnp.exp2(later) * kept, all_ref.shape)
    for h in range(heads):
        thr_ref[:, h * LANES:(h + 1) * LANES] = jnp.broadcast_to(all_ref[h:h + 1, :], (8, LANES))

    slot = max(8, heads)
    stack_ref[...] = jnp.zeros_like(stack_ref)
    past = jnp.zeros((heads, LANES), F32)
    for c in range(tokens // LANES):
        here = slice(c * LANES, (c + 1) * LANES)
        first = base + c * LANES
        step_dt = parts[c][0]
        total_to = running(step_dt * rate, False)
        chunk_total = jnp.broadcast_to(total_to[:, LANES - 1:LANES], (heads, LANES))
        before_ref[:, here] = total_to - jnp.log(step_dt) * LOG2E
        doc = doc_at(first + lax.broadcasted_iota(I32, (heads, LANES), 1), starts)
        doc_in = doc_at(first - 1, starts)
        doc_out = doc_at(first + LANES - 1, starts)
        fresh_ref[:, here] = jnp.where(doc == doc_out, jnp.exp2(chunk_total - total_to) * step_dt, 0.0)
        kept_ref[c] = jnp.exp2(chunk_total) * jnp.where(doc_in == doc_out, 1.0, 0.0)
        stack_ref[c, 0:heads, :] = total_to
        stack_ref[c, slot:slot + heads, :] = jnp.where(doc == doc_in, jnp.exp2(total_to), 0.0)
        stack_ref[c, 2 * slot:2 * slot + heads, :] = jnp.where(doc == first_doc, jnp.exp2(past + total_to), 0.0)
        past = past + chunk_total
        reach_ref[here, :] = stack_ref[c].T

    pick = pick_matrix(group_of(lax.axis_index("head"), heads, head_size, groups), groups)
    copies[4].wait()
    for c in range(tokens // LANES):
        here = slice(c * LANES, (c + 1) * LANES)
        chosen = dot(pick, b_ref[c * LANES * groups:(c + 1) * LANES * groups, :])
        bsel_ref[here, :] = chosen.astype(BF16)
        bt_ref[:, here] = chosen.T.astype(BF16)

    copies[5].wait()
    for h in range(heads):
        here = slice(h * LANES, (h + 1) * LANES)
        weighted = bt_ref[...] * w_ref[h:h + 1, :].astype(BF16)
        state_ref[:, here] = dot(weighted, x_ref[:, here]).astype(BF16)


def in_smem():
    return pl.BlockSpec(memory_space=pltpu.SMEM)


def in_vmem():
    return pl.BlockSpec(memory_space=pltpu.VMEM)


def block_states(head_size, doc_lengths, doc_lang, a_log, dt_raw, b_rows, x_in):
    heads, tokens = dt_raw.shape
    features = x_in.shape[1]
    return pl.pallas_call(
        functools.partial(state_kernel, head_size),
        grid_spec=pltpu.PrefetchScalarGridSpec(
            num_scalar_prefetch=0,
            grid=(1,),
            in_specs=[pl.BlockSpec(memory_space=pl.ANY)] * 6,
            out_specs=[in_vmem()] * 9 + [in_smem()],
            scratch_shapes=[
                pltpu.SMEM(doc_lengths.shape, I32),
                pltpu.SMEM(doc_lang.shape, I32),
                pltpu.SMEM(a_log.shape, F32),
                pltpu.VMEM((heads, tokens), F32),
                pltpu.VMEM(b_rows.shape, BF16),
                pltpu.VMEM((heads, tokens), F32),
                pltpu.VMEM((heads, LANES), F32),
                pltpu.VMEM((tokens // LANES, LANES, LANES), F32),
                pltpu.SemaphoreType.DMA((6,)),
            ],
        ),
        out_shape=[
            pltpu.VMEM((LANES, features), BF16),
            pltpu.VMEM((8, features), F32),
            pltpu.VMEM((tokens, LANES), BF16),
            pltpu.VMEM((LANES, tokens), BF16),
            pltpu.VMEM((tokens, features), BF16),
            pltpu.VMEM((tokens, LANES), F32),
            pltpu.VMEM((heads, tokens), F32),
            pltpu.VMEM((heads, tokens), F32),
            pltpu.VMEM((tokens // LANES, heads, LANES), F32),
            pltpu.SMEM((2 * doc_lengths.shape[0],), I32),
        ],
        compiler_params=params(),
        cost_estimate=pl.CostEstimate(flops=2 * LANES * tokens * features, bytes_accessed=8 * tokens * features, transcendentals=0),
        name="block_states",
    )(*[pltpu.with_memory_space_constraint(v, pltpu.HBM) for v in (doc_lengths, doc_lang, a_log, dt_raw, b_rows, x_in)])


def scan_kernel(head_size, skip_ref, docs, b_ref, bt_ref, reach_ref, before_ref, fresh_ref, kept_ref, c_ref, x_ref, z_ref,
                part_ref, gate_ref, csel_ref, state_ref, scores_ref):
    step = pl.program_id(0)
    heads, tokens = before_ref.shape
    groups = c_ref.shape[0] // tokens
    slot = max(8, heads)

    @pl.when(step == 0)
    def _():
        state_ref[...] = jnp.zeros_like(state_ref)
        starts = starts_of(docs)
        block = lax.axis_index("seq") * tokens
        pick = pick_matrix(group_of(lax.axis_index("head"), heads, head_size, groups), groups)
        for c in range(tokens // LANES):
            here = slice(c * LANES, (c + 1) * LANES)
            base = block + c * LANES
            row_pos = base + lax.broadcasted_iota(I32, (LANES, LANES), 0)
            col_pos = base + lax.broadcasted_iota(I32, (LANES, LANES), 1)
            keep = (row_pos >= col_pos) & (doc_at(row_pos, starts) == doc_at(col_pos, starts))
            c_low = dot(pick, c_ref[c * LANES * groups:(c + 1) * LANES * groups, :]).astype(BF16)
            csel_ref[here, :] = c_low
            scores = lax.dot_general(c_low, b_ref[here, :], (((1,), (1,)), ((), ())), preferred_element_type=F32)
            scores_ref[c] = jnp.where(keep, scores, 0.0)

    now = pl.ds(pl.multiple_of(step * LANES, LANES), LANES)
    columns = reach_ref[now, :]
    chosen = csel_ref[now, :]
    before = before_ref[:, now]
    fresh = fresh_ref[:, now].astype(BF16)
    kept = kept_ref[step]
    scores = scores_ref[step]
    b_turned = bt_ref[:, now]

    for h in range(heads):
        here = slice(h * LANES, (h + 1) * LANES)
        gaps = jnp.minimum(columns[:, h:h + 1] - before[h:h + 1, :], 80.0)
        weights = (jnp.exp2(gaps) * scores).astype(BF16)
        carried = chosen * columns[:, slot + h:slot + h + 1].astype(BF16)
        x_head = x_ref[now, here]
        state = state_ref[:, here]
        out = dot(jnp.concatenate([weights, carried], axis=1), jnp.concatenate([x_head, state.astype(BF16)], axis=0))
        out = out + skip_ref[h] * x_head.astype(F32)
        written = dot(b_turned * fresh[h:h + 1, :], x_head)
        state_ref[:, here] = state * kept[h:h + 1, :] + written
        z = 0.5 * z_ref[now, here].astype(F32)
        gate = z + z * jnp.tanh(z)
        part_ref[now, here] = out * gate
        gate_ref[now, here] = gate.astype(BF16)


def local_scan(head_size, docs, d_skip, b_sel, b_turned, decays, c_rows, x_in, z_gate):
    tokens, features = x_in.shape
    chunks = tokens // LANES
    held = [pltpu.with_memory_space_constraint(v, pltpu.VMEM) for v in (c_rows, z_gate)]
    return pl.pallas_call(
        functools.partial(scan_kernel, head_size),
        grid_spec=pltpu.PrefetchScalarGridSpec(
            num_scalar_prefetch=1,
            grid=(chunks,),
            in_specs=[in_smem()] + [in_vmem()] * 9,
            out_specs=[in_vmem()] * 3,
            scratch_shapes=[
                pltpu.VMEM((LANES, features), F32),
                pltpu.VMEM((chunks, LANES, LANES), F32),
            ],
        ),
        out_shape=[
            pltpu.VMEM((tokens, features), F32),
            pltpu.VMEM((tokens, features), BF16),
            pltpu.VMEM((tokens, LANES), BF16),
        ],
        compiler_params=params(),
        cost_estimate=pl.CostEstimate(flops=16 * LANES * tokens * features, bytes_accessed=8 * tokens * features, transcendentals=0),
        name="local_scan",
    )(d_skip, docs, b_sel, b_turned, *decays, held[0], x_in, held[1])


def other_language(lang, first, size, starts, langs):
    other = lang
    few = jnp.bool_(True)
    for d, s in enumerate(starts):
        inside = (s > first) & (s < first + size) & (langs[d] != lang)
        few = few & jnp.logical_not(inside & (other != lang) & (langs[d] != other))
        other = jnp.where(inside & (other == lang), langs[d], other)
    return other, few


def has_language(which, first, size, starts, lang_ref):
    found = lang_at(first, starts, lang_ref) == which
    for d, s in enumerate(starts):
        found = found | ((s > first) & (s < first + size) & (lang_ref[d] == which))
    return found


def sum_rows(tile):
    return -(-4 * (tile // LANES) // 16) * 16


def combine_kernel(n_states, slot, tile, mine, docs, c_ref, reach_ref, part_ref, gate_ref, gain_ref, down_ref, *rest):
    states, (gated_ref, ref, enter_ref) = rest[:n_states], rest[-3:]
    features = part_ref.shape[1]
    heads = features // LANES
    starts = starts_of(docs)
    langs = [docs[len(starts) + d] for d in range(len(starts))]
    entering = states[0]
    if n_states > 1:
        total = states[0][...].astype(F32)
        for more in states[1:]:
            total = total + more[...].astype(F32)
        enter_ref[...] = total.astype(BF16)
        entering = enter_ref

    odd = lax.axis_index("head") % 2
    half = odd if mine else 1 - odd
    pair = min(2, heads)
    at = pl.multiple_of(half * tile, LANES)
    now = pl.ds(at, tile)
    first = lax.axis_index("seq") * part_ref.shape[0] + at
    lang = lang_at(first, starts, langs)
    other, few = other_language(lang, first, tile, starts, langs)
    squares = jnp.zeros((tile, LANES), F32)
    c_low = c_ref[now, :]
    reach = reach_ref[now, :]
    for p in range(heads // pair):
        both = dot(c_low, entering[:, p * pair * LANES:(p + 1) * pair * LANES])
        for i in range(pair):
            h = p * pair + i
            here = slice(h * LANES, (h + 1) * LANES)
            entered = both[:, i * LANES:(i + 1) * LANES] * reach[:, 2 * slot + h:2 * slot + h + 1]
            gated = part_ref[now, here] + entered * gate_ref[now, here].astype(F32)
            squares = squares + gated * gated
            gated_ref[now, here] = (gated * gain_ref[:, here]).astype(BF16)
    token_lang = lang_at(first + lax.broadcasted_iota(I32, (tile, LANES), 0), starts, langs)
    both = dot(gated_ref[now, :], jnp.concatenate([down_ref[lang], down_ref[other]], axis=1))
    ref[0:tile, :] = jnp.where(token_lang == lang, both[:, :LANES], both[:, LANES:]).astype(BF16)

    ones = jnp.ones((8, LANES), BF16)
    whole = squares.astype(BF16)
    rest_of = (squares - whole.astype(F32)).astype(BF16)
    turned = (((1,), (1,)), ((), ()))
    sums = lax.dot_general(ones, whole, turned, preferred_element_type=F32) + lax.dot_general(ones, rest_of, turned, preferred_element_type=F32)
    rows = [sums[:, c * LANES:(c + 1) * LANES] for c in range(tile // LANES)]
    rows += rows[:1] * (sum_rows(tile) // 4 - len(rows))
    upper = lax.broadcasted_iota(I32, (8, LANES), 0) < 4
    rows = jnp.concatenate([jnp.where(upper, a, b) for a, b in zip(rows[0::2], rows[1::2])], axis=0)
    ref[tile:tile + sum_rows(tile), :] = rows.astype(BF16)

    @pl.when(jnp.logical_not(few))
    def _():
        token_lang = lang_at(first + lax.broadcasted_iota(I32, (tile, LANES), 0), starts, langs)
        for k in range(down_ref.shape[0]):
            @pl.when(has_language(k, first, tile, starts, langs) & (lang != k) & (other != k))
            def _():
                low = dot(gated_ref[now, :], down_ref[k])
                ref[0:tile, :] = jnp.where(token_lang == k, low, ref[0:tile, :].astype(F32)).astype(BF16)


def combine(docs, c_sel, reach, part, gate, gain, down, states, slot, mine, into=None):
    tokens, features = part.shape
    tile = tokens // 2
    held = [pltpu.with_memory_space_constraint(v, pltpu.VMEM) for v in [gain, down] + states]
    more = [] if into is None else [into]
    return pl.pallas_call(
        functools.partial(combine_kernel, len(states), slot, tile, mine),
        grid_spec=pltpu.PrefetchScalarGridSpec(
            num_scalar_prefetch=0,
            grid=(1,),
            in_specs=[in_smem()] + [in_vmem()] * (6 + len(states)) + [pl.BlockSpec(memory_space=pl.ANY) for _ in more],
            out_specs=[in_vmem()] * 2,
            scratch_shapes=[pltpu.VMEM(states[0].shape, BF16)],
        ),
        out_shape=[
            pltpu.VMEM((tokens, features), BF16),
            pltpu.VMEM((tile + sum_rows(tile), LANES), BF16),
        ],
        input_output_aliases={7 + len(states): 0} if more else {},
        compiler_params=params(),
        cost_estimate=pl.CostEstimate(flops=0, bytes_accessed=0, transcendentals=0),
        name="combine",
    )(docs, c_sel, reach, part, gate, *held, *more)


def finish_kernel(tile, all_features, docs, mine_ref, other_ref, gated_ref, up_ref, out_hbm, out_ref, sems):
    features = gated_ref.shape[1]
    ranks = up_ref.shape[1]
    starts = starts_of(docs)
    langs = [docs[len(starts) + d] for d in range(len(starts))]
    odd = lax.axis_index("head") % 2
    piece = min(4 * LANES, features)
    tokens = tile

    def copy_of(step, i):
        at = step * tokens
        here = pl.ds(pl.multiple_of(i * piece, LANES), piece)
        return pltpu.make_async_copy(
            out_ref.at[pl.ds(at, tokens), here],
            out_hbm.at[pl.ds(at, tokens), here],
            sems.at[step * (features // piece) + i],
        )

    def block(step):
        is_mine = odd == step
        now = pl.ds(step * tokens, tokens)
        scale = jnp.where(is_mine, mine_ref[tile:, :].astype(F32), other_ref[tile:, :].astype(F32))
        scale = lax.rsqrt(scale / all_features + EPS)
        turned = jnp.concatenate([scale] * (LANES // sum_rows(tile)), axis=0).T
        scale = jnp.concatenate([turned[:, 4 * c:4 * c + 1] for c in range(tokens // LANES)], axis=0)
        low = jnp.where(is_mine, mine_ref[0:tokens, :].astype(F32), other_ref[0:tokens, :].astype(F32))
        low = (low * scale).astype(BF16)
        first = (lax.axis_index("seq") * 2 + step) * tokens
        lang = lang_at(first, starts, langs)
        other, few = other_language(lang, first, tokens, starts, langs)
        token_lang = lang_at(first + lax.broadcasted_iota(I32, (tokens, LANES), 0), starts, langs)
        zero = jnp.zeros((), BF16)

        @pl.when(few)
        def _():
            spread = jnp.concatenate([
                jnp.where(token_lang == lang, low, zero),
                jnp.where(token_lang != lang, low, zero),
            ], axis=1)
            for begin in range(0, features, piece):
                here = slice(begin, begin + piece)
                lifted = dot(spread, jnp.concatenate([up_ref[lang, :, here], up_ref[other, :, here]], axis=0))
                out_ref[now, here] = (gated_ref[now, here].astype(F32) * scale + lifted).astype(BF16)
                copy_of(step, begin // piece).start()

        @pl.when(jnp.logical_not(few))
        def _():
            spread = jnp.concatenate([jnp.where(token_lang == k, low, zero) for k in range(up_ref.shape[0])], axis=1)

            def column_piece(i, _):
                here = pl.ds(pl.multiple_of(i * piece, LANES), piece)
                lifted = dot(spread, up_ref[:, :, here].reshape(up_ref.shape[0] * ranks, piece))
                out_ref[now, here] = (gated_ref[now, here].astype(F32) * scale + lifted).astype(BF16)
                copy_of(step, i).start()
                return 0

            lax.fori_loop(0, features // piece, column_piece, 0, unroll=True)

    for step in range(2):
        block(step)
    for step in range(2):
        for i in range(features // piece):
            copy_of(step, i).wait()


def finish(docs, mine, other, gated, up, all_features):
    tokens, features = gated.shape
    tile = tokens // 2
    held = [pltpu.with_memory_space_constraint(v, pltpu.VMEM) for v in (mine, other, gated, up)]
    return pl.pallas_call(
        functools.partial(finish_kernel, tile, all_features),
        grid_spec=pltpu.PrefetchScalarGridSpec(
            num_scalar_prefetch=0,
            grid=(1,),
            in_specs=[in_smem()] + [in_vmem()] * 4,
            out_specs=pl.BlockSpec(memory_space=pl.ANY),
            scratch_shapes=[
                pltpu.VMEM(gated.shape, BF16),
                pltpu.SemaphoreType.DMA((2 * (features // min(4 * LANES, features)),)),
            ],
        ),
        out_shape=pltpu.HBM(gated.shape, BF16),
        compiler_params=params(),
        name="finish",
    )(docs, *held)


def sum_over_head(mine, sent, across, devices):
    total = (mine.astype(F32) + sent.astype(F32)).astype(BF16)
    bit = 2
    while bit < devices:
        masks = [bit] if 2 * bit >= devices else [2 * bit, bit, 3 * bit]
        added = total.astype(F32)
        for arrived in [across(total, m) for m in masks]:
            added = added + arrived.astype(F32)
        total = added.astype(BF16)
        bit *= 2 ** (1 if len(masks) == 1 else 2)
    return total, across(total, 1)


def run(seq_size, head_size, relayed, x_in, z_gate, b_input, c_input, dt_raw, a_log, d_skip, norm_gain,
        doc_lengths, doc_lang, adapt_down, adapt_up):
    tokens, features = x_in.shape
    heads = dt_raw.shape[0]
    groups = b_input.shape[1]
    b_rows = b_input.reshape(tokens * groups, b_input.shape[2])
    c_rows = c_input.reshape(tokens * groups, c_input.shape[2])
    gain = norm_gain.reshape(1, features)
    all_features = features * head_size
    slot = max(8, heads)
    onward = [(i, i + 1) for i in range(seq_size - 1)]

    state, through, b_sel, b_turned, x_held, *decays, docs = block_states(head_size, doc_lengths, doc_lang, a_log, dt_raw, b_rows, x_in)
    state, z_gate, c_rows = lax.optimization_barrier((state, z_gate, c_rows))
    arrived = lax.ppermute(state, "seq", onward)
    part, gate, c_sel = local_scan(head_size, docs, d_skip, b_sel, b_turned, decays, c_rows, x_held, z_gate)
    reach = decays[0]
    arrived, part = lax.optimization_barrier((arrived, part))
    states = [arrived]
    for _ in range(1, hops_of(tokens, seq_size) if relayed else 1):
        arrived = lax.ppermute((arrived.astype(F32) * through[0:1]).astype(BF16), "seq", onward)
        states.append(arrived)

    def across(v, mask):
        return lax.ppermute(v, "head", [(i, i ^ mask) for i in range(head_size)])

    shared = (docs, c_sel, reach, part, gate, gain, adapt_down, states, slot)
    gated, theirs = combine(*shared, False)
    sent = across(theirs, 1)
    gated, mine = combine(*shared, True, gated)
    mine, other = sum_over_head(mine, sent, across, head_size)
    return finish(docs, mine, other, gated, adapt_up, all_features)


def longest_of(tokens, seq_size):
    return tokens * seq_size // LONGEST_SHARE


def hops_of(tokens, seq_size):
    return min(-(-(longest_of(tokens, seq_size) - 1) // tokens), seq_size - 1)


def covered_kernel(tokens, seq_size, len_ref, out_ref):
    found, at = jnp.int32(0), jnp.int32(0)
    for d in range(len_ref.shape[0]):
        end = at + len_ref[d]
        for block in range(1, seq_size - 1):
            found = jnp.where((at < block * tokens) & (end > (block + 1) * tokens), 1, found)
        at = end
    out_ref[0] = found


def per_device(seq_size, head_size, *args):
    tokens = args[0].shape[0]
    doc_lengths = args[8]
    if hops_of(tokens, seq_size) < 2:
        return run(seq_size, head_size, False, *args)
    covered = pl.pallas_call(
        functools.partial(covered_kernel, tokens, seq_size),
        in_specs=[pl.BlockSpec(memory_space=pltpu.SMEM)],
        out_specs=pl.BlockSpec(memory_space=pltpu.SMEM),
        out_shape=pltpu.SMEM((1,), I32),
        name="covered",
    )(doc_lengths)[0] > 0
    return lax.cond(
        covered,
        functools.partial(run, seq_size, head_size, True),
        functools.partial(run, seq_size, head_size, False),
        *args,
    )


def solution(mesh):
    placed = (
        P("seq", "head"),
        P("seq", "head"),
        P("seq", None, None),
        P("seq", None, None),
        P("head", "seq"),
        P("head"),
        P("head"),
        P("head"),
        P(),
        P(),
        P(None, "head", None),
        P(None, None, "head"),
    )
    return jax.shard_map(
        functools.partial(per_device, mesh.shape["seq"], mesh.shape["head"]),
        mesh=mesh, in_specs=placed, out_specs=P("seq", "head"), check_vma=False,
    )
```
